32 devices in a mesh: dp: 8 (over z, y), fsdp: 4 (over x, core).
Axes of the slice: x: 2, y: 2, z: 4, core: 2. Of those that a mesh axis runs over, the one named last changes fastest.
Arguments:
- codes: int32 [64, 256], P(('dp', 'fsdp')), may hold values from 0 to 2024
- mask_pos: int32 [64, 128], P(('dp', 'fsdp')), may hold values from 0 to 255, as said below
- mask_count: int32 [64], P(('dp', 'fsdp')), may hold values from 1 to 128, as said below
- table: float32 [2026, 768], P(None, ('dp', 'fsdp')), may hold values from -0.4330127 to 0.4330127
- w_qkv: float32 [2, 768, 2304], P(None, ('dp', 'fsdp')), may hold values from -0.21875 to 0.21875
- w_out: float32 [2, 768, 768], P(None, ('dp', 'fsdp')), may hold values from -0.875 to 0.875
- w_up: float32 [2, 768, 3072], P(None, ('dp', 'fsdp')), may hold values from -0.21875 to 0.21875
- w_down: float32 [2, 3072, 768], P(None, ('dp', 'fsdp')), may hold values from -0.109375 to 0.109375
- layer_vecs: float32 [2, 9216], P(None, ('dp', 'fsdp')), may hold values from -0.8 to 2.4
- final_norm: float32 [2, 768], P(None, ('dp', 'fsdp')), may hold values from -0.8 to 2.4
- head_bias: float32 [2026], replicated, may hold values from -0.625 to 0.625
- moment_table: float32 [2026, 768], P(None, ('dp', 'fsdp')), may hold values from -1.5258789e-05 to 1.5258789e-05
- moment_qkv: float32 [2, 768, 2304], P(None, ('dp', 'fsdp')), may hold values from -1.5258789e-05 to 1.5258789e-05
- moment_out: float32 [2, 768, 768], P(None, ('dp', 'fsdp')), may hold values from -1.5258789e-05 to 1.5258789e-05
- moment_up: float32 [2, 768, 3072], P(None, ('dp', 'fsdp')), may hold values from -1.5258789e-05 to 1.5258789e-05
- moment_down: float32 [2, 3072, 768], P(None, ('dp', 'fsdp')), may hold values from -1.5258789e-05 to 1.5258789e-05
- moment_vecs: float32 [2, 9216], P(None, ('dp', 'fsdp')), may hold values from -4.5776367e-05 to 4.5776367e-05
- moment_final: float32 [2, 768], P(None, ('dp', 'fsdp')), may hold values from -4.5776367e-05 to 4.5776367e-05
- moment_bias: float32 [2026], replicated, may hold values from -1.5258789e-05 to 1.5258789e-05
- average_table: float32 [2026, 768], P(None, ('dp', 'fsdp')), may hold values from -0.4375 to 0.4375
- average_qkv: float32 [2, 768, 2304], P(None, ('dp', 'fsdp')), may hold values from -0.21875 to 0.21875
- average_out: float32 [2, 768, 768], P(None, ('dp', 'fsdp')), may hold values from -0.875 to 0.875
- average_up: float32 [2, 768, 3072], P(None, ('dp', 'fsdp')), may hold values from -0.21875 to 0.21875
- average_down: float32 [2, 3072, 768], P(None, ('dp', 'fsdp')), may hold values from -0.109375 to 0.109375
- average_vecs: float32 [2, 9216], P(None, ('dp', 'fsdp')), may hold values from 0.5 to 1.5
- average_final: float32 [2, 768], P(None, ('dp', 'fsdp')), may hold values from 0.5 to 1.5
- average_bias: float32 [2026], replicated, may hold values from -0.625 to 0.625
Outputs:
- loss_sum: float32 [], replicated
- mask_total: float32 [], replicated
- grad_norm: float32 [], replicated
- table_new: float32 [2026, 768], P(None, ('dp', 'fsdp'))
- qkv_new: float32 [2, 768, 2304], P(None, ('dp', 'fsdp'))
- out_new: float32 [2, 768, 768], P(None, ('dp', 'fsdp'))
- up_new: float32 [2, 768, 3072], P(None, ('dp', 'fsdp'))
- down_new: float32 [2, 3072, 768], P(None, ('dp', 'fsdp'))
- vecs_new: float32 [2, 9216], P(None, ('dp', 'fsdp'))
- final_new: float32 [2, 768], P(None, ('dp', 'fsdp'))
- bias_new: float32 [2026], replicated
- table_moment: float32 [2026, 768], P(None, ('dp', 'fsdp'))
- qkv_moment: float32 [2, 768, 2304], P(None, ('dp', 'fsdp'))
- out_moment: float32 [2, 768, 768], P(None, ('dp', 'fsdp'))
- up_moment: float32 [2, 768, 3072], P(None, ('dp', 'fsdp'))
- down_moment: float32 [2, 3072, 768], P(None, ('dp', 'fsdp'))
- vecs_moment: float32 [2, 9216], P(None, ('dp', 'fsdp'))
- final_moment: float32 [2, 768], P(None, ('dp', 'fsdp'))
- bias_moment: float32 [2026], replicated
- table_average: float32 [2026, 768], P(None, ('dp', 'fsdp'))
- qkv_average: float32 [2, 768, 2304], P(None, ('dp', 'fsdp'))
- out_average: float32 [2, 768, 768], P(None, ('dp', 'fsdp'))
- up_average: float32 [2, 768, 3072], P(None, ('dp', 'fsdp'))
- down_average: float32 [2, 3072, 768], P(None, ('dp', 'fsdp'))
- vecs_average: float32 [2, 9216], P(None, ('dp', 'fsdp'))
- final_average: float32 [2, 768], P(None, ('dp', 'fsdp'))
- bias_average: float32 [2026], replicated
The draws below stay inside these ranges and needn't reach their ends.
Inputs may be any that keep to these rules, and one draw needn't show every extreme that they name: `mask_pos`: each row holds 128 different positions of its image; the first mask_count entries of the row are the masked ones. `mask_count`: some image has 128 masked positions.
All inputs are finite; a program needn't handle non-finite values.
Results may differ from the reference program's by a relative error of at most 0.012.
The reference program's roundings to bfloat16 on the way count: a program that leaves them out, or rounds other values in their place, can miss the bound.
Values may be sent and summed in bfloat16 or wider, within the bound.
No kernel may reach another device: no remote copies, remote signals or barrier semaphores. Data moves between devices by JAX's collectives and lax.ppermute only.
A program may use at most 320 MiB of HBM per device.

```python
import math
from functools import reduce
import jax
import jax.numpy as jnp
from jax import lax

D = 768
HEADS = 12
HEAD_DIM = 64
FF = 3072
V = 2026
S = 256
M = 128
L = 2
IMG_DEV = 2
IMAGES = 64
DP_SPAN = 8
FS_SPAN = 4
VW = 9216
PARAMS = 15733738


def draw_mask_pos(key, part):
    key = jax.random.fold_in(key, 5)
    noise = jax.random.randint(key, (IMAGES, S), 0, 2 ** 20, dtype=jnp.int32)
    order = jnp.argsort(noise * S + jnp.arange(S, dtype=jnp.int32)[None, :], axis=1)
    return order[:, :M].astype(jnp.int32)


def draw_mask_count(key, part):
    key = jax.random.fold_in(key, 7)
    image = jnp.arange(IMAGES, dtype=jnp.int32)
    device = image // IMG_DEV
    row_dp = device // FS_SPAN
    row_fs = device % FS_SPAN
    base = M * (DP_SPAN - 1 + 2 * row_dp) * (FS_SPAN - 1 + 2 * row_fs) // (9 * (DP_SPAN - 1) * (FS_SPAN - 1))
    cut = jax.random.randint(key, (IMAGES,), 0, 4, dtype=jnp.int32)
    cut = jnp.where(image == IMAGES - 1, 0, cut)
    return jnp.maximum(base - base * cut // 8, 1).astype(jnp.int32)


def gains_and_rest(key, rows, width):
    key_gain, key_rest = jax.random.split(key)
    column = jnp.arange(D, dtype=jnp.float32) / (D - 1)
    rest = 0.2 * jnp.clip(jax.random.normal(key_rest, (rows, width), jnp.float32), -4.0, 4.0)
    wobble = jnp.clip(jax.random.normal(key_gain, (rows, 2, D), jnp.float32), -3.0, 3.0)
    gains = (0.6 + 1.2 * column) * (1.0 + 0.1 * wobble)
    return (gains, rest)


def draw_layer_vecs(key, part):
    key = jax.random.fold_in(key, 11)
    gains, rest = gains_and_rest(key, L, VW)
    rest = rest.at[:, 0:D].set(gains[:, 0])
    rest = rest.at[:, 5 * D:6 * D].set(gains[:, 1])
    return rest


def draw_final_norm(key, part):
    key = jax.random.fold_in(key, 13)
    gains, rest = gains_and_rest(key, 1, D)
    return jnp.concatenate([gains[:, 0], rest], axis=0)


def place_ends(values, rng, low, top_value):
    longest = values.shape.index(max(values.shape))
    spots = []
    for shift in (0, 1):
        where = [jax.random.randint(jax.random.fold_in(rng, axis), (), 0, length) for axis, length in enumerate(values.shape)]
        where[longest] = (where[longest] + shift) % values.shape[longest]
        spots.append(tuple(where))
    return values.at[spots[0]].set(low).at[spots[1]].set(top_value)


def block_scale(own_key, extent, cuts, least, largest):
    level = 1.0
    for position, shards_of in cuts:
        heights = jax.random.uniform(jax.random.fold_in(jax.random.fold_in(own_key, 6), position), (shards_of,), jnp.float32, least / len(cuts), largest / len(cuts))
        level = level * jnp.repeat(jnp.exp(heights), extent[position] // shards_of).reshape((-1,) + (1,) * (len(extent) - 1 - position))
    return level


def gaussian(key, extent, scale, reach, shards=(), held_as=jnp.bfloat16):
    level = block_scale(key, extent, shards, -0.22, 0.18) if shards else 1.0
    array = jax.random.normal(key, extent, jnp.float32) * scale * level
    return jnp.minimum(jnp.maximum(array, -reach), reach).astype(held_as)


def setup_inputs(seed: int = 0) -> dict:
    splits = jax.random.split(jax.random.key(seed), 28)
    return {
        "codes": place_ends(jax.random.randint(splits[0], (IMAGES, S), 0, V - 1), jax.random.fold_in(splits[0], 1), 0, (V - 1) - 1).astype(jnp.int32),
        "mask_pos": draw_mask_pos(jax.random.fold_in(splits[27], 71), 0),
        "mask_count": draw_mask_count(jax.random.fold_in(splits[27], 71), 0),
        "table": gaussian(splits[3], (V, D), (2.0 * D ** -0.5), 0.4330127, ((1, 32),), jnp.float32),
        "w_qkv": gaussian(splits[4], (L, D, 3 * D), D ** -0.5, 0.21875, ((1, 32),), jnp.float32),
        "w_out": gaussian(splits[5], (L, D, D), (D // 16) ** -0.5, 0.875, ((1, 32),), jnp.float32),
        "w_up": gaussian(splits[6], (L, D, FF), D ** -0.5, 0.21875, ((1, 32),), jnp.float32),
        "w_down": gaussian(splits[7], (L, FF, D), FF ** -0.5, 0.109375, ((1, 32),), jnp.float32),
        "layer_vecs": draw_layer_vecs(jax.random.fold_in(splits[27], 71), 0),
        "final_norm": draw_final_norm(jax.random.fold_in(splits[27], 71), 0),
        "head_bias": gaussian(splits[10], (V,), 0.1, 0.625, (), jnp.float32),
        "moment_table": gaussian(splits[11], (V, D), (0.01 * PARAMS ** -0.5), 1.52587890625e-05, ((1, 32),), jnp.float32),
        "moment_qkv": gaussian(splits[12], (L, D, 3 * D), (0.01 * PARAMS ** -0.5), 1.52587890625e-05, ((1, 32),), jnp.float32),
        "moment_out": gaussian(splits[13], (L, D, D), (0.01 * PARAMS ** -0.5), 1.52587890625e-05, ((1, 32),), jnp.float32),
        "moment_up": gaussian(splits[14], (L, D, FF), (0.01 * PARAMS ** -0.5), 1.52587890625e-05, ((1, 32),), jnp.float32),
        "moment_down": gaussian(splits[15], (L, FF, D), (0.01 * PARAMS ** -0.5), 1.52587890625e-05, ((1, 32),), jnp.float32),
        "moment_vecs": gaussian(splits[16], (L, VW), (0.03 * PARAMS ** -0.5), 4.57763671875e-05, ((1, 32),), jnp.float32),
        "moment_final": gaussian(splits[17], (2, D), (0.03 * PARAMS ** -0.5), 4.57763671875e-05, ((1, 32),), jnp.float32),
        "moment_bias": gaussian(splits[18], (V,), (0.01 * PARAMS ** -0.5), 1.52587890625e-05, (), jnp.float32),
        "average_table": gaussian(splits[19], (V, D), (2.0 * D ** -0.5), 0.4375, ((1, 32),), jnp.float32),
        "average_qkv": gaussian(splits[20], (L, D, 3 * D), D ** -0.5, 0.21875, ((1, 32),), jnp.float32),
        "average_out": gaussian(splits[21], (L, D, D), (D // 16) ** -0.5, 0.875, ((1, 32),), jnp.float32),
        "average_up": gaussian(splits[22], (L, D, FF), D ** -0.5, 0.21875, ((1, 32),), jnp.float32),
        "average_down": gaussian(splits[23], (L, FF, D), FF ** -0.5, 0.109375, ((1, 32),), jnp.float32),
        "average_vecs": jnp.clip(1.0 + 0.1 * jax.random.normal(splits[24], (L, VW), jnp.float32), 0.5, 1.5),
        "average_final": jnp.clip(1.0 + 0.1 * jax.random.normal(splits[25], (2, D), jnp.float32), 0.5, 1.5),
        "average_bias": gaussian(splits[26], (V,), 0.1, 0.625, (), jnp.float32),
    }


epsilon = 1e-06
step_rate = 10000.0
inertia = 0.5
average_decay = 0.5
clip_bound = 0.01
highest = lax.Precision.HIGHEST

@jax.custom_vjp
def low(v):
    return lax.optimization_barrier(v.astype(jnp.bfloat16)).astype(jnp.float32)

@jax.custom_vjp
def low_back(v):
    return v

def low_keep(v):
    return (low(v), None)

def low_pass(kept, grad):
    return (grad,)

def back_keep(v):
    return (v, None)

def back_low(kept, grad):
    return (low(grad),)
low.defvjp(low_keep, low_pass)
low_back.defvjp(back_keep, back_low)

def both_ways(value):
    return low(low_back(value))

def normalize(stream, gain, shift):
    centre = stream - lax.optimization_barrier(jnp.mean(stream, -1, keepdims=True))
    scaled = centre * lax.rsqrt(lax.optimization_barrier(jnp.mean(centre * centre, -1, keepdims=True)) + epsilon)
    return scaled * gain + shift

def matmul(left, right):
    return jnp.einsum('bsd,de->bse', left, right, precision=highest)

def block(stream, qkv_weight, out_weight, up_weight, down_weight, vector):
    parts = [vector[segment * D:(segment + 1) * D] for segment in range(8)]
    gain_one, shift_one, query_bias, value_bias, out_bias, gain_two, shift_two, down_bias = parts
    up_bias = vector[8 * D:]
    normed = low(normalize(stream, gain_one, shift_one))
    triple = matmul(normed, qkv_weight)
    queries = both_ways(triple[..., :D] + query_bias)
    key_rows = both_ways(triple[..., D:2 * D])
    values = both_ways(triple[..., 2 * D:] + value_bias)
    head_shape = (stream.shape[0], stream.shape[1], HEADS, HEAD_DIM)
    scores = jnp.einsum('bqhe,bkhe->bhqk', queries.reshape(head_shape), key_rows.reshape(head_shape), precision=highest)
    scores = low_back(scores * HEAD_DIM ** (-0.5))
    peak = lax.optimization_barrier(jnp.max(scores, -1, keepdims=True))
    raised = jnp.exp(scores - peak)
    probs = low(raised / lax.optimization_barrier(jnp.sum(raised, -1, keepdims=True)))
    mixed = jnp.einsum('bhqk,bkhe->bqhe', probs, values.reshape(head_shape), precision=highest)
    mixed = both_ways(mixed.reshape(stream.shape))
    middle = stream + low_back(matmul(mixed, out_weight) + out_bias)
    normed_two = low(normalize(middle, gain_two, shift_two))
    hidden = low_back(matmul(normed_two, up_weight) + up_bias)
    active = low(jax.nn.gelu(hidden))
    return middle + low_back(matmul(active, down_weight) + down_bias)

def forward(params, codes, positions, counts):
    table, qkv_all, out_all, up_all, down_all, vectors, final, head_bias = params
    table_low = low(table)
    slots = jnp.arange(M, dtype=jnp.int32)
    valid = (slots[None, :] < counts[:, None]).astype(jnp.float32)
    hits = positions[:, :, None] == jnp.arange(S, dtype=jnp.int32)[None, None, :]
    masked = jnp.any(hits & (valid[:, :, None] > 0), axis=1)
    inputs = jnp.where(masked, V - 1, codes).astype(jnp.int32)
    targets = jnp.take_along_axis(codes, positions, axis=1)
    stream = table_low[inputs]
    for layer_idx in range(L):
        stream = block(stream, low(qkv_all[layer_idx]), low(out_all[layer_idx]), low(up_all[layer_idx]), low(down_all[layer_idx]), low(vectors[layer_idx]))
    final_low = low(final)
    normed = low(normalize(stream, final_low[0], final_low[1]))
    chosen = jnp.take_along_axis(normed, positions[:, :, None], axis=1)
    logits = low_back(jnp.einsum('bmd,vd->bmv', chosen, table_low, precision=highest) + head_bias)
    peak = lax.optimization_barrier(jnp.max(logits, -1, keepdims=True))
    log_total = peak[..., 0] + jnp.log(lax.optimization_barrier(jnp.sum(jnp.exp(logits - peak), -1)))
    picked = jnp.take_along_axis(logits, targets[:, :, None], axis=2)[..., 0]
    return jnp.sum(valid * (log_total - picked))

def reference(codes, mask_pos, mask_count, table, w_qkv, w_out, w_up, w_down, layer_vecs, final_norm, head_bias, moment_table, moment_qkv, moment_out, moment_up, moment_down, moment_vecs, moment_final, moment_bias, average_table, average_qkv, average_out, average_up, average_down, average_vecs, average_final, average_bias):
    params = (table, w_qkv, w_out, w_up, w_down, layer_vecs, final_norm, head_bias)
    moments = (moment_table, moment_qkv, moment_out, moment_up, moment_down, moment_vecs, moment_final, moment_bias)
    averages = (average_table, average_qkv, average_out, average_up, average_down, average_vecs, average_final, average_bias)
    group = math.gcd(IMAGES, max(1, 4096 // S))
    mask_total = jnp.sum(mask_count.astype(jnp.float32))
    inverse = 1.0 / mask_total
    batches = (codes.reshape(IMAGES // group, group, S), mask_pos.reshape(IMAGES // group, group, M), mask_count.reshape(IMAGES // group, group))

    def group_step(carry, batch):
        grads, loss = carry
        group_codes, group_pos, group_counts = batch
        value, pullback = jax.vjp(lambda weights: forward(weights, group_codes, group_pos, group_counts), params)
        delta = pullback(inverse)[0]
        grads = jax.tree.map(jnp.add, grads, delta)
        return ((grads, loss + value), None)
    zeros = jax.tree.map(jnp.zeros_like, params)
    (grads, loss_sum), unused = lax.scan(group_step, (zeros, jnp.zeros((), jnp.float32)), batches)
    squares = reduce(jnp.add, [jnp.sum(grad * grad) for grad in grads])
    grad_norm = jnp.sqrt(squares)
    factor = jnp.minimum(1.0, clip_bound / (grad_norm + epsilon))
    new_weights = []
    new_moments = []
    new_averages = []
    for weight, moment, average, grad in zip(params, moments, averages, grads):
        clipped = grad * factor
        moment_next = inertia * moment + clipped
        weight_next = weight - step_rate * (clipped + inertia * moment_next)
        new_moments.append(moment_next)
        new_weights.append(weight_next)
        new_averages.append(average_decay * average + (1.0 - average_decay) * weight_next)
    return (loss_sum, mask_total, grad_norm, new_weights[0], new_weights[1], new_weights[2], new_weights[3], new_weights[4], new_weights[5], new_weights[6], new_weights[7], new_moments[0], new_moments[1], new_moments[2], new_moments[3], new_moments[4], new_moments[5], new_moments[6], new_moments[7], new_averages[0], new_averages[1], new_averages[2], new_averages[3], new_averages[4], new_averages[5], new_averages[6], new_averages[7])
```

```python
from functools import partial, reduce

import jax
import jax.numpy as jnp
from jax import lax
from jax.experimental import pallas as pl
from jax.experimental.pallas import tpu as pltpu
from jax.sharding import PartitionSpec as P

D = 768
HEADS = 12
HEAD_DIM = 64
FF = 3072
V = 2026
M = 128
L = 2
UNIT = 384
VPAD = 2304
BOTH = ("dp", "fsdp")


epsilon = 1e-06
step_rate = 10000.0
inertia = 0.5
average_decay = 0.5
clip_bound = 0.01


HOPS = {
    "zhi": ("dp", 4, 8, 0),
    "zlo": ("dp", 2, 8, 1),
    "y": ("dp", 1, 8, 2),
    "x": ("fsdp", 2, 4, 3),
    "core": ("fsdp", 1, 4, None),
}


def swap(tensor, hop):
    axis, flip, size, unused = HOPS[hop]
    return lax.ppermute(tensor, axis, [(i, i ^ flip) for i in range(size)])


def side(hop):
    axis, flip, unused, unused = HOPS[hop]
    return (lax.axis_index(axis) // flip) % 2


def in_order(bit, own, other, axis):
    return jnp.where(
        bit == 0, jnp.concatenate([own, other], axis), jnp.concatenate([other, own], axis)
    )


def pick(tensor, index, axis):
    return lax.dynamic_slice_in_dim(tensor, index, 1, axis)


def gather_chips(tensor, order):
    tensor = tensor[None, None, None, None]
    for hop in order:
        tensor = in_order(side(hop), tensor, swap(tensor, hop), HOPS[hop][3])
    return tensor


def scatter_chips(parts, order):
    for hop in order:
        axis, bit = HOPS[hop][3], side(hop)
        leaving = reduce(jnp.add, [pick(part, 1 - bit, axis).astype(jnp.float32) for part in parts])
        arrived = swap(leaving.astype(jnp.bfloat16), hop)
        parts = [pick(part, bit, axis) for part in parts] + [arrived]
    return reduce(jnp.add, [part.astype(jnp.float32) for part in parts])[0, 0, 0, 0]


def column_units(shard):
    rows, columns = shard.shape
    return shard.reshape(rows, 2, columns // (2 * UNIT), UNIT).transpose(1, 2, 0, 3)


PIECES = {
    "table": [(3, 24)],
    "attention": [(3, 24), (1, 24)],
    "forward": [(1, 96), (4, 24)],
}


def natural_weight(halves, offset, units, rows):
    chips = halves.shape[1]
    block = halves[:, :, offset : offset + units * rows].reshape(2, chips, units, rows, UNIT)
    return block.transpose(1, 3, 0, 2, 4).reshape(chips * rows, 2 * units * UNIT)


def weight_blocks(grad, units, rows):
    chips = grad.shape[0] // rows
    block = grad.reshape(chips, rows, 2, units, UNIT).transpose(2, 0, 3, 1, 4)
    return block.reshape(2, chips, units * rows, UNIT)


TOKENS = 512
SLOTS = 256
ANY = pl.BlockSpec(memory_space=pl.ANY)
SMEM = pl.BlockSpec(memory_space=pltpu.SMEM)
VMEM = pl.BlockSpec(memory_space=pltpu.VMEM)
low = jnp.bfloat16
full = jnp.float32


def dot(left, right):
    return lax.dot_general(left, right, (((1,), (0,)), ((), ())), preferred_element_type=full)


def dot_right(left, right):
    return lax.dot_general(left, right, (((1,), (1,)), ((), ())), preferred_element_type=full)


def dot_left(left, right):
    return lax.dot_general(left, right, (((0,), (0,)), ((), ())), preferred_element_type=full)


def norm_parts(stream):
    centre = stream - jnp.mean(stream, -1, keepdims=True)
    spread = lax.rsqrt(jnp.mean(centre * centre, -1, keepdims=True) + epsilon)
    return centre * spread, spread


def norm_back(upstream, scaled, spread, gain):
    weighted = upstream * gain
    return spread * (
        weighted
        - jnp.mean(weighted, -1, keepdims=True)
        - scaled * jnp.mean(weighted * scaled, -1, keepdims=True)
    )


def rows_sum(tensor):
    return jnp.sum(tensor, 0, keepdims=True)


def columns(start, size):
    return pl.ds(pl.multiple_of(start, 128), size)


def unit_copies(core, halves, at, units, target, sems):
    copies = []
    for which, source in enumerate(halves):
        half = core if which == 0 else 1 - core
        for unit in range(units):
            copies.append(
                pltpu.make_async_copy(
                    source.at[:, pl.ds(at + 48 * unit, 48), :],
                    target.at[:, :, columns((half * units + unit) * UNIT, UNIT)],
                    sems.at[which * units + unit],
                )
            )
    return copies


def flat(block):
    return block.reshape(block.shape[0] * block.shape[1], block.shape[2])


def head_mask(shape, which):
    lane = lax.broadcasted_iota(jnp.int32, shape, 1)
    return lane < HEAD_DIM if which == 0 else lane >= HEAD_DIM


def embed_kernel(at, core, codes, pos, valid, mine, yours, ids, stream, weight, sems):
    copies = unit_copies(core[0], (mine, yours), at, 3, weight, sems)
    for copy in copies:
        copy.start()
    place = lax.broadcasted_iota(jnp.int32, (TOKENS, SLOTS), 0)
    masked = jnp.max(jnp.where(place == pos[...], valid[...], 0.0), -1, keepdims=True)
    tokens = jnp.where(masked > 0, V - 1, codes[...])
    ids[...] = tokens
    for copy in copies:
        copy.wait()
    acc = jnp.zeros((TOKENS, D), full)
    for tile in range(3):
        word = lax.broadcasted_iota(jnp.int32, (TOKENS, D), 1) + tile * D
        hot = jnp.where(word == tokens, 1.0, 0.0).astype(low)
        acc += dot_right(hot, flat(weight[:, :, tile * D : (tile + 1) * D]))
    stream[...] = acc


def attention_kernel(
    at, core, stream, vector, mine, yours, triple, lse, mixed, middle, w_in, w_out, sems
):
    in_copies = unit_copies(core[0], (mine, yours), at, 3, w_in, sems.at[pl.ds(0, 6)])
    out_copies = unit_copies(core[0], (mine, yours), at + 144, 1, w_out, sems.at[pl.ds(6, 2)])
    for copy in in_copies + out_copies:
        copy.start()
    scaled, unused = norm_parts(stream[...])
    normed = (scaled * vector[0:1] + vector[1:2]).astype(low)
    for copy in in_copies:
        copy.wait()
    for part in range(3):
        block = dot(normed, flat(w_in[:, :, part * D : (part + 1) * D]))
        if part == 0:
            block = block + vector[2:3]
        if part == 2:
            block = block + vector[3:4]
        triple[part] = block.astype(low)
    lse[...] = jnp.zeros_like(lse)
    shape = (256, 128)
    lane = lax.broadcasted_iota(jnp.int32, shape, 1)

    def pair(step, carry):
        here = columns(step * 128, 128)
        for image in range(2):
            rows = slice(256 * image, 256 * image + 256)
            queries, key_rows, values = triple[0, rows, here], triple[1, rows, here], triple[2, rows, here]
            results = []
            for which in range(2):
                query = jnp.where(head_mask(shape, which), queries, jnp.zeros_like(queries))
                scores = dot_right(query, key_rows) * HEAD_DIM ** (-0.5)
                peak = jnp.max(scores, -1, keepdims=True)
                raised = jnp.exp(scores - peak)
                total = jnp.sum(raised, -1, keepdims=True)
                probs = (raised * (1.0 / total)).astype(low)
                results.append(dot(probs, values))
                lse[rows] = jnp.where(lane == 2 * step + which, peak + jnp.log(total), lse[rows])
            mixed[rows, here] = jnp.where(head_mask(shape, 0), results[0], results[1]).astype(low)
        return carry

    lax.fori_loop(0, HEADS // 2, pair, 0)
    for copy in out_copies:
        copy.wait()
    middle[...] = stream[...] + dot(mixed[...], flat(w_out[...])) + vector[4:5]


def forward_copies(core, mine, yours, w_up, w_down, sems):
    up = unit_copies(core, (mine, yours), 192, 4, w_up, sems.at[pl.ds(0, 8)])
    down = []
    for tile in range(4):
        chips = pl.ds(4 * lax.rem(2 * core + tile, 4), 4)
        for which, source in enumerate((mine, yours)):
            half = core if which == 0 else 1 - core
            down.append(
                pltpu.make_async_copy(
                    source.at[chips, pl.ds(0, 192), :],
                    w_down.at[chips, :, columns(half * UNIT, UNIT)],
                    sems.at[8 + 2 * tile + which],
                )
            )
    return [up[2 * tile : 2 * tile + 2] + down[2 * tile : 2 * tile + 2] for tile in range(4)]


CURVE = 0.7978845608028654


def forward_kernel(core, middle, vector, mine, yours, hidden, result, w_up, w_down, normed, stage, sems, out_sems):
    copies = forward_copies(core[0], mine, yours, w_up, w_down, sems)
    for group in copies:
        for copy in group:
            copy.start()
    scaled, unused = norm_parts(middle[...])
    normed[...] = (scaled * vector[5:6] + vector[6:7]).astype(low)
    result[...] = middle[...] + vector[7:8]
    sent = []
    for step in range(4):
        tile = lax.rem(2 * core[0] + step, 4)
        for copy in copies[step]:
            copy.wait()
        block = dot(normed[...], flat(w_up[:, :, columns(tile * D, D)])) + vector[pl.ds(8 + tile, 1)]
        if step >= 2:
            sent[step - 2].wait()
        stage[step % 2] = block
        copy = pltpu.make_async_copy(stage.at[step % 2], hidden.at[tile], out_sems.at[step % 2])
        copy.start()
        sent.append(copy)
        bent = jnp.tanh(CURVE * (block + 0.044715 * (block * block * block)))
        active = (0.5 * block * (1.0 + bent)).astype(low)
        result[...] += dot(active, flat(w_down[pl.ds(4 * tile, 4)]))
    for copy in sent[2:]:
        copy.wait()


def head_kernel(
    at,
    core,
    stream,
    final,
    codes,
    pos_column,
    pos_row,
    scale,
    valid,
    bias,
    mine,
    yours,
    upstream,
    chosen_out,
    grad_logits_out,
    bias_grad,
    final_grad,
    loss,
    weight,
    logits,
    sems,
):
    copies = unit_copies(core[0], (mine, yours), at, 3, weight, sems)
    for copy in copies:
        copy.start()
    scaled, spread = norm_parts(stream[...])
    normed = (scaled * final[0:1] + final[1:2]).astype(low)
    picker = lax.broadcasted_iota(jnp.int32, (SLOTS, TOKENS), 1) == pos_column[...]
    target = jnp.sum(jnp.where(picker, codes[...], 0), -1, keepdims=True)
    chosen = dot(picker.astype(full).astype(low), normed).astype(low)
    chosen_out[...] = chosen
    for copy in copies:
        copy.wait()
    peak = jnp.full((SLOTS, 1), -jnp.inf, full)
    picked = jnp.zeros((SLOTS, 1), full)
    for tile in range(3):
        here = slice(tile * D, tile * D + D)
        block = dot(chosen, flat(weight[:, :, here])) + bias[:, here]
        logits[:, here] = block
        peak = jnp.maximum(peak, jnp.max(block, -1, keepdims=True))
        word = lax.broadcasted_iota(jnp.int32, (SLOTS, D), 1) + tile * D
        picked += jnp.sum(jnp.where(word == target, block, 0.0), -1, keepdims=True)
    total = jnp.zeros((SLOTS, 1), full)
    for tile in range(3):
        total += jnp.sum(jnp.exp(logits[:, tile * D : tile * D + D] - peak), -1, keepdims=True)
    log_total = peak + jnp.log(total)
    loss[...] = jnp.broadcast_to(rows_sum(valid[...] * (log_total - picked)), (1, 128))
    grad_chosen = jnp.zeros((SLOTS, D), full)
    for tile in range(3):
        here = slice(tile * D, tile * D + D)
        word = lax.broadcasted_iota(jnp.int32, (SLOTS, D), 1) + tile * D
        chance = jnp.exp(logits[:, here] - log_total)
        block = ((chance - jnp.where(word == target, 1.0, 0.0)) * scale[...]).astype(low)
        grad_logits_out[:, here] = block
        bias_grad[:, here] = rows_sum(block.astype(full))
        grad_chosen += dot_right(block, flat(weight[:, :, here]))
    back = lax.broadcasted_iota(jnp.int32, (TOKENS, SLOTS), 0) == pos_row[...]
    back = back.astype(full).astype(low)
    grad_normed = jnp.zeros((TOKENS, D), full)
    for unused in range(3):
        piece = grad_chosen.astype(low)
        grad_normed += dot(back, piece)
        grad_chosen -= piece.astype(full)
    final_grad[0:1] = rows_sum(grad_normed * scaled)
    final_grad[1:2] = rows_sum(grad_normed)
    upstream[...] = norm_back(grad_normed, scaled, spread, final[0:1])


def leave(core, half, source, keep, send, place, sem):
    @pl.when(half == core)
    def _():
        pltpu.make_async_copy(source, keep.at[place], sem).start()

    @pl.when(half != core)
    def _():
        pltpu.make_async_copy(source, send.at[place], sem).start()


def arrive(source, keep, place, sem):
    pltpu.make_async_copy(source, keep.at[place], sem).wait()


def forward_back_kernel(
    core,
    upstream,
    middle,
    vector,
    hidden,
    mine,
    yours,
    grad_middle,
    vector_grad,
    keep,
    send,
    w_up,
    w_down,
    normed_t,
    branch,
    hidden_tile,
    down_stage,
    up_stage,
    acc,
    sems,
    hidden_sems,
    out_sems,
):
    own = core[0]
    tiles = [lax.rem(2 * own + step, 4) for step in range(4)]
    fetch = [
        pltpu.make_async_copy(hidden.at[tiles[step]], hidden_tile.at[step % 2], hidden_sems.at[step % 2])
        for step in range(4)
    ]
    fetch[0].start()
    copies = forward_copies(own, mine, yours, w_up, w_down, sems)
    for group in copies:
        for copy in group:
            copy.start()
    scaled, spread = norm_parts(middle[...])
    normed_t[...] = (scaled * vector[5:6] + vector[6:7]).T.astype(low)
    branch[...] = upstream[...].astype(low)
    vector_grad[...] = jnp.zeros_like(vector_grad)
    vector_grad[7:8] = rows_sum(branch[...].astype(full))
    acc[...] = jnp.zeros_like(acc)
    every = slice(None)
    flights = []

    def land(step):
        for args in flights[step]:
            arrive(*args)

    for step in range(4):
        tile, slot = tiles[step], step % 2
        if step < 3:
            fetch[step + 1].start()
        for copy in copies[step]:
            copy.wait()
        fetch[step].wait()
        block = hidden_tile[slot]
        square = block * block
        bent = jnp.tanh(CURVE * (block + 0.044715 * (square * block)))
        active = (0.5 * block * (1.0 + bent)).astype(low)
        slope = 0.5 * (1.0 + bent) + 0.5 * block * (1.0 - bent * bent) * (
            CURVE * (1.0 + (3.0 * 0.044715) * square)
        )
        back = dot_right(branch[...], flat(w_down[pl.ds(4 * tile, 4)]))
        grad_hidden = (slope * back).astype(low)
        vector_grad[pl.ds(8 + tile, 1)] = rows_sum(grad_hidden.astype(full))
        if step >= 2:
            land(step - 2)
        grad_down = dot(active.T, branch[...]).astype(low)
        down_stage[slot] = grad_down.reshape(4, 192, D)
        flight = []
        place = (pl.ds(4 * tile, 4), pl.ds(0, 192), every)
        for which, target in enumerate((keep, send)):
            half = own if which == 0 else 1 - own
            source = down_stage.at[slot, :, :, columns(half * UNIT, UNIT)]
            sem = out_sems.at[slot, which]
            pltpu.make_async_copy(source, target.at[place], sem).start()
            flight.append((source, target, place, sem))
        grad_up = dot(normed_t[...], grad_hidden).astype(low)
        up_stage[slot] = grad_up.reshape(16, 48, D)
        target = keep if step < 2 else send
        for unit in range(2):
            source = up_stage.at[slot, :, :, pl.ds(unit * UNIT, UNIT)]
            place = (every, pl.ds(192 + 48 * (2 * slot + unit), 48), every)
            sem = out_sems.at[slot, 2 + unit]
            pltpu.make_async_copy(source, target.at[place], sem).start()
            flight.append((source, target, place, sem))
        flights.append(flight)
        acc[...] += dot_right(grad_hidden, flat(w_up[:, :, columns(tile * D, D)]))
    grad_normed = acc[...]
    scaled, spread = norm_parts(middle[...])
    vector_grad[5:6] = rows_sum(grad_normed * scaled)
    vector_grad[6:7] = rows_sum(grad_normed)
    grad_middle[...] = upstream[...] + norm_back(grad_normed, scaled, spread, vector[5:6])
    land(2)
    land(3)


def attention_back_kernel(
    at,
    core,
    grad_middle,
    stream,
    vector,
    triple,
    lse,
    mixed,
    mine,
    yours,
    upstream,
    vector_grad,
    keep,
    send,
    w_in,
    w_out,
    grad_mixed,
    grad_triple,
    stage,
    sems,
    out_sems,
):
    own = core[0]
    out_copies = unit_copies(own, (mine, yours), at + 144, 1, w_out, sems.at[pl.ds(6, 2)])
    in_copies = unit_copies(own, (mine, yours), at, 3, w_in, sems.at[pl.ds(0, 6)])
    for copy in out_copies + in_copies:
        copy.start()
    every = slice(None)
    grad_out_low = grad_middle[...].astype(low)
    vector_grad[...] = jnp.zeros_like(vector_grad)
    vector_grad[4:5] = rows_sum(grad_out_low.astype(full))
    stage[3] = dot(mixed[...].T, grad_out_low).astype(low).reshape(16, 48, D)
    for half in range(2):
        source = stage.at[3, :, :, pl.ds(half * UNIT, UNIT)]
        leave(own, half, source, keep, send, (every, pl.ds(at + 144, 48), every), out_sems.at[6 + half])
    for copy in out_copies:
        copy.wait()
    grad_mixed[...] = dot_right(grad_out_low, flat(w_out[...])).astype(low)
    shape = (256, 128)
    lane = lax.broadcasted_iota(jnp.int32, shape, 1)

    def pair(step, carry):
        here = columns(step * 128, 128)
        for image in range(2):
            rows = slice(256 * image, 256 * image + 256)
            queries, key_rows, values = triple[0, rows, here], triple[1, rows, here], triple[2, rows, here]
            grads = grad_mixed[rows, here]
            outs = []
            for which in range(2):
                mask = head_mask(shape, which)
                none = jnp.zeros_like(queries)
                scores = dot_right(jnp.where(mask, queries, none), key_rows) * HEAD_DIM ** (-0.5)
                total = jnp.sum(jnp.where(lane == 2 * step + which, lse[rows], 0.0), -1, keepdims=True)
                probs = jnp.exp(scores - total)
                grad_values = dot_left(probs.astype(low), grads)
                grad_probs = dot_right(jnp.where(mask, grads, none), values)
                inner = jnp.sum(probs * grad_probs, -1, keepdims=True)
                grad_scores = (probs * (grad_probs - inner)).astype(low)
                grad_queries = dot(grad_scores, key_rows) * HEAD_DIM ** (-0.5)
                grad_keys = dot_left(grad_scores, queries) * HEAD_DIM ** (-0.5)
                outs.append((grad_queries, grad_keys, grad_values))
            first = head_mask(shape, 0)
            for part in range(3):
                grad_triple[part, rows, here] = jnp.where(first, outs[0][part], outs[1][part]).astype(low)
        return carry

    lax.fori_loop(0, HEADS // 2, pair, 0)
    scaled, spread = norm_parts(stream[...])
    normed_t = (scaled * vector[0:1] + vector[1:2]).T.astype(low)
    for copy in in_copies:
        copy.wait()
    grad_normed = jnp.zeros((TOKENS, D), full)
    for part in range(3):
        block = grad_triple[part]
        if part == 0:
            vector_grad[2:3] = rows_sum(block.astype(full))
        if part == 2:
            vector_grad[3:4] = rows_sum(block.astype(full))
        stage[part] = dot(normed_t, block).astype(low).reshape(16, 48, D)
        for side_unit in range(2):
            unit = 2 * part + side_unit
            source = stage.at[part, :, :, pl.ds(side_unit * UNIT, UNIT)]
            place = (every, pl.ds(at + 48 * (unit % 3), 48), every)
            leave(own, unit // 3, source, keep, send, place, out_sems.at[unit])
        grad_normed += dot_right(block, flat(w_in[:, :, part * D : (part + 1) * D]))
    vector_grad[0:1] = rows_sum(grad_normed * scaled)
    vector_grad[1:2] = rows_sum(grad_normed)
    upstream[...] = grad_middle[...] + norm_back(grad_normed, scaled, spread, vector[0:1])
    for unit in range(6):
        source = stage.at[unit // 2, :, :, pl.ds((unit % 2) * UNIT, UNIT)]
        arrive(source, keep, (every, pl.ds(at + 48 * (unit % 3), 48), every), out_sems.at[unit])
    for half in range(2):
        source = stage.at[3, :, :, pl.ds(half * UNIT, UNIT)]
        arrive(source, keep, (every, pl.ds(at + 144, 48), every), out_sems.at[6 + half])


def embed_back_kernel(
    core, upstream, ids, chosen, grad_logits, small, keep_in, send_in, keep, send, stage, sems
):
    own = core[0]
    every = slice(None)
    for which, target in enumerate((keep, send)):
        half = own if which == 0 else 1 - own
        pltpu.make_async_copy(small.at[half], target.at[:, pl.ds(144, 16), :], sems.at[6 + which]).start()
    stream_t = upstream[...].T.astype(low)
    chosen_t = chosen[...].astype(full).T.astype(low)
    for tile in range(3):
        word = lax.broadcasted_iota(jnp.int32, (TOKENS, D), 1) + tile * D
        hot = jnp.where(word == ids[...], 1.0, 0.0).astype(low)
        block = dot(stream_t, hot) + dot(chosen_t, grad_logits[:, tile * D : tile * D + D])
        stage[tile] = block.astype(low).reshape(16, 48, D)
        for side_unit in range(2):
            unit = 2 * tile + side_unit
            source = stage.at[tile, :, :, pl.ds(side_unit * UNIT, UNIT)]
            place = (every, pl.ds(48 * (unit % 3), 48), every)
            leave(own, unit // 3, source, keep, send, place, sems.at[unit])
    for unit in range(6):
        source = stage.at[unit // 2, :, :, pl.ds((unit % 2) * UNIT, UNIT)]
        arrive(source, keep, (every, pl.ds(48 * (unit % 3), 48), every), sems.at[unit])
    for which, target in enumerate((keep, send)):
        half = own if which == 0 else 1 - own
        pltpu.make_async_copy(small.at[half], target.at[:, pl.ds(144, 16), :], sems.at[6 + which]).wait()


def shape_of(*dims, kind=full):
    return jax.ShapeDtypeStruct(dims, kind)


def call(kernel, outs, out_specs, in_specs, scratch, flops, moved, **more):
    return pl.pallas_call(
        kernel,
        out_shape=outs,
        in_specs=in_specs,
        out_specs=out_specs,
        scratch_shapes=scratch,
        compiler_params=pltpu.CompilerParams(vmem_limit_bytes=56 * 2**20),
        cost_estimate=pl.CostEstimate(flops=flops, bytes_accessed=moved, transcendentals=0),
        **more,
    )


DMA = pltpu.SemaphoreType.DMA
MEG = 10**6
GIG = 10**9


def embed(core, codes, pos, valid, mine, yours, at):
    return call(
        partial(embed_kernel, at),
        (shape_of(TOKENS, 1, kind=jnp.int32), shape_of(TOKENS, D)),
        (VMEM, VMEM),
        [SMEM, VMEM, VMEM, VMEM, ANY, ANY],
        [pltpu.VMEM((16, 48, VPAD), low), DMA((6,))],
        3 * GIG,
        5 * MEG,
    )(core, codes, pos, valid, mine, yours)


def attention(core, stream, vector, mine, yours, at):
    return call(
        partial(attention_kernel, at),
        (
            shape_of(3, TOKENS, D, kind=low),
            shape_of(TOKENS, 128),
            shape_of(TOKENS, D, kind=low),
            shape_of(TOKENS, D),
        ),
        (VMEM,) * 4,
        [SMEM, VMEM, VMEM, ANY, ANY],
        [pltpu.VMEM((16, 48, 3 * D), low), pltpu.VMEM((16, 48, D), low), DMA((8,))],
        8 * GIG,
        12 * MEG,
    )(core, stream, vector, mine, yours)


def feed_forward(core, middle, vector, mine, yours):
    return call(
        forward_kernel,
        (shape_of(4, TOKENS, D), shape_of(TOKENS, D)),
        (ANY, VMEM),
        [SMEM, VMEM, VMEM, ANY, ANY],
        [
            pltpu.VMEM((16, 48, FF), low),
            pltpu.VMEM((16, 192, D), low),
            pltpu.VMEM((TOKENS, D), low),
            pltpu.VMEM((2, TOKENS, D), full),
            DMA((16,)),
            DMA((2,)),
        ],
        8 * GIG,
        20 * MEG,
    )(core, middle, vector, mine, yours)


def head(core, stream, final, codes, pos_column, pos_row, scale, valid, bias, mine, yours, at):
    return call(
        partial(head_kernel, at),
        (
            shape_of(TOKENS, D),
            shape_of(SLOTS, D, kind=low),
            shape_of(SLOTS, VPAD, kind=low),
            shape_of(1, VPAD),
            shape_of(2, D),
            shape_of(1, 128),
        ),
        (VMEM,) * 6,
        [SMEM] + [VMEM] * 8 + [ANY, ANY],
        [pltpu.VMEM((16, 48, VPAD), low), pltpu.VMEM((SLOTS, VPAD), full), DMA((6,))],
        6 * GIG,
        10 * MEG,
    )(core, stream, final, codes, pos_column, pos_row, scale, valid, bias, mine, yours)


def feed_forward_back(core, upstream, middle, vector, hidden, mine, yours):
    return call(
        forward_back_kernel,
        (
            shape_of(TOKENS, D),
            shape_of(12, D),
            shape_of(16, 384, UNIT, kind=low),
            shape_of(16, 384, UNIT, kind=low),
        ),
        (VMEM, VMEM, ANY, ANY),
        [SMEM, VMEM, VMEM, VMEM, ANY, ANY, ANY],
        [
            pltpu.VMEM((16, 48, FF), low),
            pltpu.VMEM((16, 192, D), low),
            pltpu.VMEM((D, TOKENS), low),
            pltpu.VMEM((TOKENS, D), low),
            pltpu.VMEM((2, TOKENS, D), full),
            pltpu.VMEM((2, 4, 192, D), low),
            pltpu.VMEM((2, 16, 48, D), low),
            pltpu.VMEM((TOKENS, D), full),
            DMA((16,)),
            DMA((2,)),
            DMA((2, 4)),
        ],
        16 * GIG,
        30 * MEG,
    )(core, upstream, middle, vector, hidden, mine, yours)


def attention_back(core, grad_middle, stream, vector, triple, lse, mixed, mine, yours, at):
    rows = 192 + at
    return call(
        partial(attention_back_kernel, at),
        (
            shape_of(TOKENS, D),
            shape_of(12, D),
            shape_of(16, rows, UNIT, kind=low),
            shape_of(16, rows, UNIT, kind=low),
        ),
        (VMEM, VMEM, ANY, ANY),
        [SMEM] + [VMEM] * 6 + [ANY, ANY],
        [
            pltpu.VMEM((16, 48, 3 * D), low),
            pltpu.VMEM((16, 48, D), low),
            pltpu.VMEM((TOKENS, D), low),
            pltpu.VMEM((3, TOKENS, D), low),
            pltpu.VMEM((4, 16, 48, D), low),
            DMA((8,)),
            DMA((8,)),
        ],
        18 * GIG,
        20 * MEG,
    )(core, grad_middle, stream, vector, triple, lse, mixed, mine, yours)


def embed_back(core, upstream, ids, chosen, grad_logits, small, keep, send):
    shape = shape_of(*keep.shape, kind=low)
    return call(
        embed_back_kernel,
        (shape, shape),
        (ANY, ANY),
        [SMEM] + [VMEM] * 4 + [ANY] * 3,
        [pltpu.VMEM((3, 16, 48, D), low), DMA((8,))],
        5 * GIG,
        10 * MEG,
        input_output_aliases={6: 0, 7: 1},
    )(core, upstream, ids, chosen, grad_logits, small, keep, send)


def update(weight, moment, average, grad, factor):
    clipped = grad * factor
    moment_next = inertia * moment + clipped
    weight_next = weight - step_rate * (clipped + inertia * moment_next)
    return (weight_next, moment_next, average_decay * average + (1.0 - average_decay) * weight_next)


def pack_small(vecs, final_norm, counts):
    own = jnp.concatenate(
        [vecs[0], vecs[1], final_norm[0], final_norm[1], counts.astype(full)]
    ).astype(low)
    own = jnp.pad(own, (0, 2 * UNIT - own.shape[0])).reshape(2, UNIT)
    return jnp.pad(own, ((0, 14), (0, 0)))


def body(hops, *arguments):
    codes, mask_pos, mask_count, table, w_qkv, w_out, w_up, w_down = arguments[:8]
    layer_vecs, final_norm, head_bias = arguments[8:11]
    moments, averages = arguments[11:19], arguments[19:27]
    core = side("core") if hops else jnp.zeros((), jnp.int32)
    own = core.astype(jnp.int32).reshape(1)
    images, seq_len = codes.shape
    table_t = jnp.pad(table.T, ((0, 0), (0, VPAD - V)))
    shards = {"table": [table_t]}
    for l in range(L):
        shards["attention", l] = [w_qkv[l], w_out[l]]
        shards["forward", l] = [w_down[l], w_up[l]]
    if hops:

        def chip_rows(name):
            pieces = PIECES[name if isinstance(name, str) else name[0]]
            halves = [column_units(shard).reshape(2, -1, UNIT) for shard in shards[name]]
            halves = jnp.concatenate(halves, 1).astype(low)
            mine_half = pick(halves, core, 0)[0]
            other = swap(pick(halves, 1 - core, 0)[0], "core")
            blocks, start = [], 0
            for units, rows in pieces:
                size = units * rows
                mine = mine_half[start : start + size].reshape(units, 1, rows, UNIT)
                yours = other[start : start + size].reshape(units, 1, rows, UNIT)
                blocks.append(in_order(core, mine, yours, 1).reshape(-1, UNIT))
                start += size
            return jnp.concatenate(blocks)

        def gathered(chunk, order):
            mine = gather_chips(chunk, order)
            yours = swap(mine, "core")
            return mine.reshape(16, -1, UNIT), yours.reshape(16, -1, UNIT)

        first, second = ("zlo", "zhi", "y", "x"), ("zlo", "zhi", "x", "y")
        small_part = pack_small(layer_vecs, final_norm, mask_count)
        chunk = jnp.concatenate([chip_rows("table"), small_part, chip_rows(("attention", 0))])
        pair_zero = gathered(chunk, first)
        forward_pairs = [gathered(chip_rows(("forward", 0)), second)]
        attention_pairs = [pair_zero, gathered(chip_rows(("attention", 1)), first)]
        forward_pairs.append(gathered(chip_rows(("forward", 1)), second))
        table_pair = pair_zero
        small = [part[:, 144:146].reshape(16, 1, 2 * UNIT) for part in pair_zero]
        small = in_order(core, small[0], small[1], 1).reshape(32, 2 * UNIT).astype(full)
        vectors = [small[:, 288 * l : 288 * l + 288].reshape(12, D) for l in range(L)]
        final_float = small[:, 576:624].reshape(32, 2, 24).transpose(1, 0, 2).reshape(2, D)
        mask_total = jnp.sum(small[:, 624 : 624 + images])
    else:

        def everywhere(shard):
            return lax.all_gather(shard.astype(low), BOTH, axis=0, tiled=True)

        def pair_of(name):
            pieces = PIECES[name if isinstance(name, str) else name[0]]
            blocks = [
                weight_blocks(everywhere(shard), units, 2 * rows)
                for shard, (units, rows) in zip(shards[name], pieces)
            ]
            blocks = jnp.concatenate(blocks, 2)
            return blocks[0], blocks[1]

        table_pair = pair_of("table")
        attention_pairs = [
            tuple(jnp.pad(part, ((0, 0), (160 * (1 - l), 0), (0, 0))) for part in pair_of(("attention", l)))
            for l in range(L)
        ]
        forward_pairs = [pair_of(("forward", l)) for l in range(L)]
        vectors = [everywhere(layer_vecs[l]).astype(full).reshape(12, D) for l in range(L)]
        final_float = everywhere(final_norm.T).T.astype(full)
        mask_total = lax.psum(jnp.sum(mask_count.astype(full)), BOTH)

    slots = jnp.arange(M, dtype=jnp.int32)
    valid = (slots[None, :] < mask_count[:, None]).astype(full)
    places = mask_pos + seq_len * jnp.arange(images, dtype=jnp.int32)[:, None]
    codes_row, codes_column = codes.reshape(1, TOKENS), codes.reshape(TOKENS, 1)
    pos_row, pos_column = places.reshape(1, SLOTS), places.reshape(SLOTS, 1)
    valid_row, valid_column = valid.reshape(1, SLOTS), valid.reshape(SLOTS, 1)
    scale = valid_column * (1.0 / mask_total)
    bias = jnp.pad(head_bias, (0, VPAD - V), constant_values=-1e30).reshape(1, VPAD)

    starts = (160, 0)
    ids, stream = embed(own, codes_column, pos_row, valid_row, *table_pair, 0)
    kept = []
    for l in range(L):
        triple, lse, mixed, middle = attention(own, stream, vectors[l], *attention_pairs[l], starts[l])
        hidden, result = feed_forward(own, middle, vectors[l], *forward_pairs[l])
        kept.append((stream, triple, lse, mixed, middle, hidden))
        stream = result
    upstream, chosen, grad_logits, bias_grad, final_grad, loss = head(
        own, stream, final_float, codes_row, pos_column, pos_row, scale, valid_column, bias, *table_pair, 0
    )

    def scattered(keep, send, order):
        shape = (2, 2, 2, 2) + keep.shape[1:]
        return scatter_chips([keep.reshape(shape), swap(send, "core").reshape(shape)], order)

    back_first, back_second = ("x", "y", "zhi", "zlo"), ("y", "x", "zhi", "zlo")
    reduced, blocks, vector_grads = {}, {}, [None] * L
    for l in reversed(range(L)):
        stream, triple, lse, mixed, middle, hidden = kept[l]
        grad_middle, late, keep, send = feed_forward_back(
            own, upstream, middle, vectors[l], hidden, *forward_pairs[l]
        )
        blocks["forward", l] = keep, send
        if hops:
            reduced["forward", l] = scattered(keep, send, back_second)
        upstream, early, keep, send = attention_back(
            own, grad_middle, stream, vectors[l], triple, lse, mixed, *attention_pairs[l], starts[l]
        )
        blocks["attention", l] = keep, send
        if hops and l:
            reduced["attention", l] = scattered(keep, send, back_first)
        vector_grads[l] = (early + late).reshape(-1)
    small_grads = [vector_grads[0], vector_grads[1], final_grad[0], final_grad[1]]
    if hops:
        small_grads.append(bias_grad[0, :2048])
        small_grads = jnp.concatenate([grad.reshape(32, -1) for grad in small_grads], 1)
        small_grads = jnp.pad(small_grads, ((0, 0), (0, 2 * UNIT - 688))).astype(low)
        small_grads = small_grads.reshape(16, 2, 2, UNIT).transpose(1, 0, 2, 3)
        small_grads = jnp.pad(small_grads, ((0, 0), (0, 0), (0, 14), (0, 0)))
    else:
        head_grad, loss_sum = lax.psum((bias_grad[0, :V], loss[0, 0]), BOTH)
        small_sum = [lax.psum_scatter(g, BOTH, scatter_dimension=0, tiled=True) for g in small_grads]
        small_sum = jnp.concatenate(small_sum)
        small_grads = jnp.zeros((2, 16, 16, UNIT), low)
    keep, send = embed_back(own, upstream, ids, chosen, grad_logits, small_grads, *blocks["attention", 0])
    if hops:
        zero = scattered(keep, send, back_first)
        reduced["table"] = zero[:144]
        reduced["attention", 0] = zero[160:]
        small_sum = zero[144:146].reshape(-1)
    else:
        blocks["table"] = keep[:, :144], send[:, :144]
        blocks["attention", 0] = keep[:, 160:], send[:, 160:]

    def own_rows(name):
        pieces = PIECES[name if isinstance(name, str) else name[0]]
        if not hops:
            total = jnp.stack(blocks[name])
            pairs, start = [], 0
            for units, rows in pieces:
                whole = natural_weight(total, start, units, 2 * rows).astype(full)
                pairs.append(lax.psum_scatter(whole, BOTH, scatter_dimension=0, tiled=True))
                start += 2 * units * rows
            return pairs
        total = reduced[name]
        mine, leaving, start = [], [], 0
        for units, rows in pieces:
            block = total[start : start + 2 * units * rows].reshape(units, 2, rows, UNIT)
            mine.append(pick(block, core, 1).reshape(-1, UNIT))
            leaving.append(pick(block, 1 - core, 1).reshape(-1, UNIT))
            start += 2 * units * rows
        mine, arrived = jnp.concatenate(mine), swap(jnp.concatenate(leaving), "core")
        both = in_order(core, mine[None], arrived[None], 0)
        pairs, start = [], 0
        for units, rows in pieces:
            block = both[:, start : start + units * rows].reshape(2, units, rows, UNIT)
            pairs.append(block.transpose(2, 0, 1, 3).reshape(rows, 2 * units * UNIT))
            start += units * rows
        return pairs

    attention_shares = [own_rows(("attention", l)) for l in range(L)]
    forward_shares = [own_rows(("forward", l)) for l in range(L)]
    width, narrow = layer_vecs.shape[1], final_norm.shape[1]
    shares = [
        own_rows("table")[0][:, :V].T,
        jnp.stack([attention_shares[l][0] for l in range(L)]),
        jnp.stack([attention_shares[l][1] for l in range(L)]),
        jnp.stack([forward_shares[l][1] for l in range(L)]),
        jnp.stack([forward_shares[l][0] for l in range(L)]),
        small_sum[: 2 * width].reshape(L, width),
        small_sum[2 * width : 2 * width + 2 * narrow].reshape(2, narrow),
    ]
    squares = reduce(jnp.add, [jnp.sum(share * share) for share in shares])
    if hops:
        bias_share = small_sum[624:688]
        squares = squares + jnp.sum(bias_share * bias_share)
        tail = jnp.concatenate([bias_share, squares[None], loss[0, :1], jnp.zeros(62)])
        tail = tail.reshape(1, 1, 1, 1, 1, 128)
        for hop in ("core", "x", "y", "zlo", "zhi"):
            axis = HOPS[hop][3]
            tail = in_order(side(hop), tail, swap(tail, hop), 4 if axis is None else axis)
        tail = tail.reshape(32, 128)
        head_grad = tail[:, :64].reshape(-1)[:V]
        squares, loss_sum = jnp.sum(tail[:, 64]), jnp.sum(tail[:, 65])
    else:
        squares = lax.psum(squares, BOTH) + jnp.sum(head_grad * head_grad)
    grad_norm = jnp.sqrt(squares)
    factor = jnp.minimum(1.0, clip_bound / (grad_norm + epsilon))
    results = [
        update(weight, moment, average, grad, factor)
        for weight, moment, average, grad in zip(arguments[3:11], moments, averages, shares + [head_grad])
    ]
    return (
        (loss_sum, mask_total, grad_norm)
        + tuple(result[0] for result in results)
        + tuple(result[1] for result in results)
        + tuple(result[2] for result in results)
    )


def solution(mesh):
    return jax.shard_map(
        partial(body, mesh.shape["dp"] == 8 and mesh.shape["fsdp"] == 4),
        mesh=mesh,
        in_specs=(
            P(("dp", "fsdp"), None),
            P(("dp", "fsdp"), None),
            P(("dp", "fsdp")),
            P(None, ("dp", "fsdp")),
            P(None, ("dp", "fsdp"), None),
            P(None, ("dp", "fsdp"), None),
            P(None, ("dp", "fsdp"), None),
            P(None, ("dp", "fsdp"), None),
            P(None, ("dp", "fsdp")),
            P(None, ("dp", "fsdp")),
            P(),
            P(None, ("dp", "fsdp")),
            P(None, ("dp", "fsdp"), None),
            P(None, ("dp", "fsdp"), None),
            P(None, ("dp", "fsdp"), None),
            P(None, ("dp", "fsdp"), None),
            P(None, ("dp", "fsdp")),
            P(None, ("dp", "fsdp")),
            P(),
            P(None, ("dp", "fsdp")),
            P(None, ("dp", "fsdp"), None),
            P(None, ("dp", "fsdp"), None),
            P(None, ("dp", "fsdp"), None),
            P(None, ("dp", "fsdp"), None),
            P(None, ("dp", "fsdp")),
            P(None, ("dp", "fsdp")),
            P(),
        ),
        out_specs=(
            P(),
            P(),
            P(),
            P(None, ("dp", "fsdp")),
            P(None, ("dp", "fsdp"), None),
            P(None, ("dp", "fsdp"), None),
            P(None, ("dp", "fsdp"), None),
            P(None, ("dp", "fsdp"), None),
            P(None, ("dp", "fsdp")),
            P(None, ("dp", "fsdp")),
            P(),
            P(None, ("dp", "fsdp")),
            P(None, ("dp", "fsdp"), None),
            P(None, ("dp", "fsdp"), None),
            P(None, ("dp", "fsdp"), None),
            P(None, ("dp", "fsdp"), None),
            P(None, ("dp", "fsdp")),
            P(None, ("dp", "fsdp")),
            P(),
            P(None, ("dp", "fsdp")),
            P(None, ("dp", "fsdp"), None),
            P(None, ("dp", "fsdp"), None),
            P(None, ("dp", "fsdp"), None),
            P(None, ("dp", "fsdp"), None),
            P(None, ("dp", "fsdp")),
            P(None, ("dp", "fsdp")),
            P(),
        ),
        check_vma=False,
    )
```

```python
from functools import partial, reduce

import jax
import jax.numpy as jnp
from jax import lax
from jax.experimental import pallas as pl
from jax.experimental.pallas import tpu as pltpu
from jax.sharding import PartitionSpec as P

D = 768
HEADS = 12
HEAD_DIM = 64
FF = 3072
V = 2026
M = 128
L = 2
UNIT = 384
VPAD = 2304
BOTH = ("dp", "fsdp")


epsilon = 1e-06
step_rate = 10000.0
inertia = 0.5
average_decay = 0.5
clip_bound = 0.01


HOPS = {
    "zhi": ("dp", 4, 8, 0),
    "zlo": ("dp", 2, 8, 1),
    "y": ("dp", 1, 8, 2),
    "x": ("fsdp", 2, 4, 3),
    "core": ("fsdp", 1, 4, None),
}

PIECES = {"T": (160, ((3, 24),))}
for layer in range(L):
    PIECES.update(
        {
            f"Q{layer}": (144, ((3, 24),)),
            f"O{layer}": (48, ((1, 24),)),
            f"D{layer}": (192, ((1, 96),)),
            f"E{layer}": (96, ((2, 24),)),
            f"F{layer}": (96, ((2, 24),)),
        }
    )

GATHER = {
    "t": ("T",),
    "a": ("Q0", "O0"),
    "d": ("D0",),
    "u": ("E0", "F0"),
    "l": ("Q1", "O1", "D1", "E1", "F1"),
}
GATHER_WAY = {
    "t": ("zlo", "zhi", "y", "x"),
    "a": ("zlo", "zhi", "x", "y"),
    "d": ("zlo", "zhi", "y", "x"),
    "u": ("zlo", "zhi", "x", "y"),
}
SCATTER = {
    "l": ("Q1", "O1", "D1", "E1", "F1"),
    "d": ("D0",),
    "u": ("E0", "F0"),
    "a": ("Q0", "O0"),
    "t": ("T",),
}
SCATTER_WAY = {
    "d": ("x", "y", "zhi", "zlo"),
    "u": ("y", "zhi", "zlo", "x"),
    "a": ("y", "x", "zhi", "zlo"),
    "t": ("x", "zhi", "zlo", "y"),
}
FORWARD_ORDER = (
    ("t", "a", "d", "u", "t", "a", "t", "a", "d", "u", "t", "a", "embed", "d", "u", "attention0", "d", "u")
    + ("forward0", "attention1", "forward1", "head")
)
BACKWARD_ORDER = (
    ("forward1", "attention1", "forward0", "attention0", "u", "d", "a", "embed", "t", "u", "d", "t", "a")
    + ("u", "d", "u", "a", "t", "u", "d", "t", "d", "a", "t", "a")
)
LAST = (("l", "u"), ("d", "t", "a"))


def placed(layout):
    places = {}
    for name, pieces in layout.items():
        start = 0
        for piece in pieces:
            places[piece] = (name, start)
            start += PIECES[piece][0]
    return places


def height(pieces):
    return sum(PIECES[piece][0] for piece in pieces)


def swap(tensor, hop):
    axis, flip, size, unused = HOPS[hop]
    return lax.ppermute(tensor, axis, [(i, i ^ flip) for i in range(size)])


def side(hop):
    axis, flip, unused, unused = HOPS[hop]
    return (lax.axis_index(axis) // flip) % 2


def in_order(bit, own, other, axis):
    return jnp.where(
        bit == 0, jnp.concatenate([own, other], axis), jnp.concatenate([other, own], axis)
    )


def pick(tensor, index, axis):
    return lax.dynamic_slice_in_dim(tensor, index, 1, axis)


def column_units(shard):
    rows, width = shard.shape
    return shard.reshape(rows, 2, width // (2 * UNIT), UNIT).transpose(1, 2, 0, 3)


def natural_weight(halves, units, rows):
    chips = halves.shape[1]
    block = halves.reshape(2, chips, units, rows, UNIT)
    return block.transpose(1, 3, 0, 2, 4).reshape(chips * rows, 2 * units * UNIT)


def weight_blocks(grad, units, rows):
    chips = grad.shape[0] // rows
    block = grad.reshape(chips, rows, 2, units, UNIT).transpose(2, 0, 3, 1, 4)
    return block.reshape(2, chips, units * rows, UNIT)


TOKENS = 512
SLOTS = 256
ANY = pl.BlockSpec(memory_space=pl.ANY)
SMEM = pl.BlockSpec(memory_space=pltpu.SMEM)
VMEM = pl.BlockSpec(memory_space=pltpu.VMEM)
low = jnp.bfloat16
full = jnp.float32


def dot(left, right):
    return lax.dot_general(left, right, (((1,), (0,)), ((), ())), preferred_element_type=full)


def dot_right(left, right):
    return lax.dot_general(left, right, (((1,), (1,)), ((), ())), preferred_element_type=full)


def dot_left(left, right):
    return lax.dot_general(left, right, (((0,), (0,)), ((), ())), preferred_element_type=full)


def norm_parts(stream):
    centre = stream - jnp.mean(stream, -1, keepdims=True)
    spread = lax.rsqrt(jnp.mean(centre * centre, -1, keepdims=True) + epsilon)
    return centre * spread, spread


def norm_back(upstream, scaled, spread, gain):
    weighted = upstream * gain
    return spread * (
        weighted
        - jnp.mean(weighted, -1, keepdims=True)
        - scaled * jnp.mean(weighted * scaled, -1, keepdims=True)
    )


def rows_sum(tensor):
    return jnp.sum(tensor, 0, keepdims=True)


def columns(start, size):
    return pl.ds(pl.multiple_of(start, 128), size)


def unit_copies(core, halves, at, units, first, half_units, target, sems):
    copies = []
    for which, source in enumerate(halves):
        half = core if which == 0 else 1 - core
        if len(source.shape) == 4:
            source = source.at[:, half]
        for unit in range(units):
            copies.append(
                pltpu.make_async_copy(
                    source.at[:, pl.ds(at + 48 * unit, 48), :],
                    target.at[:, :, columns((half * half_units + first + unit) * UNIT, UNIT)],
                    sems.at[which * units + unit],
                )
            )
    return copies


def flat(block):
    return block.reshape(block.shape[0] * block.shape[1], block.shape[2])


def head_mask(shape, which):
    lane = lax.broadcasted_iota(jnp.int32, shape, 1)
    return lane < HEAD_DIM if which == 0 else lane >= HEAD_DIM


def embed_kernel(at, core, codes, pos, valid, mine, yours, ids, stream, weight, sems):
    copies = unit_copies(core[0], (mine, yours), at, 3, 0, 3, weight, sems)
    for copy in copies:
        copy.start()
    place = lax.broadcasted_iota(jnp.int32, (TOKENS, SLOTS), 0)
    masked = jnp.max(jnp.where(place == pos[...], valid[...], 0.0), -1, keepdims=True)
    tokens = jnp.where(masked > 0, V - 1, codes[...])
    ids[...] = tokens
    for copy in copies:
        copy.wait()
    acc = jnp.zeros((TOKENS, D), full)
    for tile in range(3):
        word = lax.broadcasted_iota(jnp.int32, (TOKENS, D), 1) + tile * D
        hot = jnp.where(word == tokens, 1.0, 0.0).astype(low)
        acc += dot_right(hot, flat(weight[:, :, tile * D : (tile + 1) * D]))
    stream[...] = acc


def attention_kernel(
    ats, core, stream, vector, *refs
):
    in_pair, out_pair = refs[0:2], refs[2:4]
    triple, lse, mixed, middle, w_in, w_out, sems = refs[4:]
    in_copies = unit_copies(core[0], in_pair, ats[0], 3, 0, 3, w_in, sems.at[pl.ds(0, 6)])
    out_copies = unit_copies(core[0], out_pair, ats[1], 1, 0, 1, w_out, sems.at[pl.ds(6, 2)])
    for copy in in_copies + out_copies:
        copy.start()
    scaled, unused = norm_parts(stream[...])
    normed = (scaled * vector[0:1] + vector[1:2]).astype(low)
    for copy in in_copies:
        copy.wait()
    for part in range(3):
        block = dot(normed, flat(w_in[:, :, part * D : (part + 1) * D]))
        if part == 0:
            block = block + vector[2:3]
        if part == 2:
            block = block + vector[3:4]
        triple[part] = block.astype(low)
    lse[...] = jnp.zeros_like(lse)
    shape = (256, 128)
    lane = lax.broadcasted_iota(jnp.int32, shape, 1)

    def pair(step, carry):
        here = columns(step * 128, 128)
        for image in range(2):
            rows = slice(256 * image, 256 * image + 256)
            queries, key_rows, values = triple[0, rows, here], triple[1, rows, here], triple[2, rows, here]
            results = []
            for which in range(2):
                query = jnp.where(head_mask(shape, which), queries, jnp.zeros_like(queries))
                scores = dot_right(query, key_rows) * HEAD_DIM ** (-0.5)
                peak = jnp.max(scores, -1, keepdims=True)
                raised = jnp.exp(scores - peak)
                total = jnp.sum(raised, -1, keepdims=True)
                probs = (raised * (1.0 / total)).astype(low)
                results.append(dot(probs, values))
                lse[rows] = jnp.where(lane == 2 * step + which, peak + jnp.log(total), lse[rows])
            mixed[rows, here] = jnp.where(head_mask(shape, 0), results[0], results[1]).astype(low)
        return carry

    lax.fori_loop(0, HEADS // 2, pair, 0)
    for copy in out_copies:
        copy.wait()
    middle[...] = stream[...] + dot(mixed[...], flat(w_out[...])) + vector[4:5]


def forward_copies(core, ats, pairs, w_up, w_down, sems):
    first = unit_copies(core, pairs[1], ats[1], 2, 0, 4, w_up, sems.at[pl.ds(0, 4)])
    second = unit_copies(core, pairs[2], ats[2], 2, 2, 4, w_up, sems.at[pl.ds(4, 4)])
    up = first[:2] + second[:2] + first[2:] + second[2:]
    down = []
    for tile in range(4):
        chips = pl.ds(4 * lax.rem(2 * core + tile, 4), 4)
        for which, source in enumerate(pairs[0]):
            half = core if which == 0 else 1 - core
            if len(source.shape) == 4:
                source = source.at[:, half]
            down.append(
                pltpu.make_async_copy(
                    source.at[chips, pl.ds(ats[0], 192), :],
                    w_down.at[chips, :, columns(half * UNIT, UNIT)],
                    sems.at[8 + 2 * tile + which],
                )
            )
    return [up[2 * tile : 2 * tile + 2] + down[2 * tile : 2 * tile + 2] for tile in range(4)]


CURVE = 0.7978845608028654


def forward_kernel(ats, core, middle, vector, *refs):
    pairs = [refs[0:2], refs[2:4], refs[4:6]]
    hidden, result, w_up, w_down, normed, stage, sems, out_sems = refs[6:]
    copies = forward_copies(core[0], ats, pairs, w_up, w_down, sems)
    for group in copies:
        for copy in group:
            copy.start()
    scaled, unused = norm_parts(middle[...])
    normed[...] = (scaled * vector[5:6] + vector[6:7]).astype(low)
    result[...] = middle[...] + vector[7:8]
    sent = []
    for step in range(4):
        tile = lax.rem(2 * core[0] + step, 4)
        for copy in copies[step]:
            copy.wait()
        block = dot(normed[...], flat(w_up[:, :, columns(tile * D, D)])) + vector[pl.ds(8 + tile, 1)]
        if step >= 2:
            sent[step - 2].wait()
        stage[step % 2] = block
        copy = pltpu.make_async_copy(stage.at[step % 2], hidden.at[tile], out_sems.at[step % 2])
        copy.start()
        sent.append(copy)
        bent = jnp.tanh(CURVE * (block + 0.044715 * (block * block * block)))
        active = (0.5 * block * (1.0 + bent)).astype(low)
        result[...] += dot(active, flat(w_down[pl.ds(4 * tile, 4)]))
    for copy in sent[2:]:
        copy.wait()


def head_kernel(
    at,
    core,
    stream,
    final,
    codes,
    pos_column,
    pos_row,
    scale,
    valid,
    bias,
    mine,
    yours,
    upstream,
    chosen_out,
    grad_logits_out,
    bias_grad,
    final_grad,
    loss,
    weight,
    logits,
    sems,
):
    copies = unit_copies(core[0], (mine, yours), at, 3, 0, 3, weight, sems)
    for copy in copies:
        copy.start()
    scaled, spread = norm_parts(stream[...])
    normed = (scaled * final[0:1] + final[1:2]).astype(low)
    picker = lax.broadcasted_iota(jnp.int32, (SLOTS, TOKENS), 1) == pos_column[...]
    target = jnp.sum(jnp.where(picker, codes[...], 0), -1, keepdims=True)
    chosen = dot(picker.astype(full).astype(low), normed).astype(low)
    chosen_out[...] = chosen
    for copy in copies:
        copy.wait()
    peak = jnp.full((SLOTS, 1), -jnp.inf, full)
    picked = jnp.zeros((SLOTS, 1), full)
    for tile in range(3):
        here = slice(tile * D, tile * D + D)
        block = dot(chosen, flat(weight[:, :, here])) + bias[:, here]
        logits[:, here] = block
        peak = jnp.maximum(peak, jnp.max(block, -1, keepdims=True))
        word = lax.broadcasted_iota(jnp.int32, (SLOTS, D), 1) + tile * D
        picked += jnp.sum(jnp.where(word == target, block, 0.0), -1, keepdims=True)
    total = jnp.zeros((SLOTS, 1), full)
    for tile in range(3):
        total += jnp.sum(jnp.exp(logits[:, tile * D : tile * D + D] - peak), -1, keepdims=True)
    log_total = peak + jnp.log(total)
    loss[...] = jnp.broadcast_to(rows_sum(valid[...] * (log_total - picked)), (1, 128))
    grad_chosen = jnp.zeros((SLOTS, D), full)
    for tile in range(3):
        here = slice(tile * D, tile * D + D)
        word = lax.broadcasted_iota(jnp.int32, (SLOTS, D), 1) + tile * D
        chance = jnp.exp(logits[:, here] - log_total)
        block = ((chance - jnp.where(word == target, 1.0, 0.0)) * scale[...]).astype(low)
        grad_logits_out[:, here] = block
        bias_grad[:, here] = rows_sum(block.astype(full))
        grad_chosen += dot_right(block, flat(weight[:, :, here]))
    back = lax.broadcasted_iota(jnp.int32, (TOKENS, SLOTS), 0) == pos_row[...]
    back = back.astype(full).astype(low)
    grad_normed = jnp.zeros((TOKENS, D), full)
    for unused in range(3):
        piece = grad_chosen.astype(low)
        grad_normed += dot(back, piece)
        grad_chosen -= piece.astype(full)
    final_grad[0:1] = rows_sum(grad_normed * scaled)
    final_grad[1:2] = rows_sum(grad_normed)
    upstream[...] = norm_back(grad_normed, scaled, spread, final[0:1])


def leave(source, target, half, at, sem):
    return pltpu.make_async_copy(source, target.at[:, half, pl.ds(at, 48), :], sem)


def forward_back_kernel(ats, outs, carried, core, upstream, middle, vector, hidden, *refs):
    pairs = [refs[0:2], refs[2:4], refs[4:6]]
    refs = refs[6 + carried :]
    grad_middle, vector_grad = refs[0:2]
    targets = refs[2:-11]
    w_up, w_down, normed_t, branch, hidden_tile, down_stage, up_stage, acc = refs[-11:-3]
    sems, hidden_sems, out_sems = refs[-3:]
    own = core[0]
    tiles = [lax.rem(2 * own + step, 4) for step in range(4)]
    fetch = [
        pltpu.make_async_copy(hidden.at[tiles[step]], hidden_tile.at[step % 2], hidden_sems.at[step % 2])
        for step in range(4)
    ]
    fetch[0].start()
    copies = forward_copies(own, ats, pairs, w_up, w_down, sems)
    for group in copies:
        for copy in group:
            copy.start()
    scaled, spread = norm_parts(middle[...])
    normed_t[...] = (scaled * vector[5:6] + vector[6:7]).T.astype(low)
    branch[...] = upstream[...].astype(low)
    vector_grad[...] = jnp.zeros_like(vector_grad)
    vector_grad[7:8] = rows_sum(branch[...].astype(full))
    acc[...] = jnp.zeros_like(acc)
    every = slice(None)
    flights = []

    def land(step):
        for copy in flights[step]:
            copy.wait()

    for step in range(4):
        tile, slot = tiles[step], step % 2
        if step < 3:
            fetch[step + 1].start()
        for copy in copies[step]:
            copy.wait()
        fetch[step].wait()
        block = hidden_tile[slot]
        square = block * block
        bent = jnp.tanh(CURVE * (block + 0.044715 * (square * block)))
        active = (0.5 * block * (1.0 + bent)).astype(low)
        slope = 0.5 * (1.0 + bent) + 0.5 * block * (1.0 - bent * bent) * (
            CURVE * (1.0 + (3.0 * 0.044715) * square)
        )
        back = dot_right(branch[...], flat(w_down[pl.ds(4 * tile, 4)]))
        grad_hidden = (slope * back).astype(low)
        vector_grad[pl.ds(8 + tile, 1)] = rows_sum(grad_hidden.astype(full))
        if step >= 2:
            land(step - 2)
        grad_down = dot(active.T, branch[...]).astype(low)
        down_stage[slot] = grad_down.reshape(4, 192, D)
        flight = []
        for half in range(2):
            place = targets[outs[0][0]].at[pl.ds(4 * tile, 4), half, pl.ds(outs[0][1], 192), :]
            source = down_stage.at[slot, :, :, pl.ds(half * UNIT, UNIT)]
            flight.append(pltpu.make_async_copy(source, place, out_sems.at[slot, half]))
        grad_up = dot(normed_t[...], grad_hidden).astype(low)
        up_stage[slot] = grad_up.reshape(16, 48, D)
        half = own if step < 2 else 1 - own
        for unit in range(2):
            source = up_stage.at[slot, :, :, pl.ds(unit * UNIT, UNIT)]
            at = outs[1 + slot][1] + 48 * unit
            flight.append(leave(source, targets[outs[1 + slot][0]], half, at, out_sems.at[slot, 2 + unit]))
        for copy in flight:
            copy.start()
        flights.append(flight)
        acc[...] += dot_right(grad_hidden, flat(w_up[:, :, columns(tile * D, D)]))
    grad_normed = acc[...]
    scaled, spread = norm_parts(middle[...])
    vector_grad[5:6] = rows_sum(grad_normed * scaled)
    vector_grad[6:7] = rows_sum(grad_normed)
    grad_middle[...] = upstream[...] + norm_back(grad_normed, scaled, spread, vector[5:6])
    land(2)
    land(3)


def attention_back_kernel(
    ats, outs, carried, core, grad_middle, stream, vector, triple, lse, mixed, *refs
):
    in_pair, out_pair = refs[0:2], refs[2:4]
    refs = refs[4 + carried :]
    upstream, vector_grad = refs[0:2]
    targets = refs[2:-7]
    w_in, w_out, grad_mixed, grad_triple, stage, sems, out_sems = refs[-7:]
    target, at = targets[outs[0][0]], outs[0][1]
    out_target, out_at = targets[outs[1][0]], outs[1][1]
    leaving = []
    own = core[0]
    out_copies = unit_copies(own, out_pair, ats[1], 1, 0, 1, w_out, sems.at[pl.ds(6, 2)])
    in_copies = unit_copies(own, in_pair, ats[0], 3, 0, 3, w_in, sems.at[pl.ds(0, 6)])
    for copy in out_copies + in_copies:
        copy.start()
    every = slice(None)
    grad_out_low = grad_middle[...].astype(low)
    vector_grad[...] = jnp.zeros_like(vector_grad)
    vector_grad[4:5] = rows_sum(grad_out_low.astype(full))
    stage[3] = dot(mixed[...].T, grad_out_low).astype(low).reshape(16, 48, D)
    for half in range(2):
        source = stage.at[3, :, :, pl.ds(half * UNIT, UNIT)]
        leaving.append(leave(source, out_target, half, out_at, out_sems.at[6 + half]))
        leaving[-1].start()
    for copy in out_copies:
        copy.wait()
    grad_mixed[...] = dot_right(grad_out_low, flat(w_out[...])).astype(low)
    shape = (256, 128)
    lane = lax.broadcasted_iota(jnp.int32, shape, 1)

    def pair(step, carry):
        here = columns(step * 128, 128)
        for image in range(2):
            rows = slice(256 * image, 256 * image + 256)
            queries, key_rows, values = triple[0, rows, here], triple[1, rows, here], triple[2, rows, here]
            grads = grad_mixed[rows, here]
            outs = []
            for which in range(2):
                mask = head_mask(shape, which)
                none = jnp.zeros_like(queries)
                scores = dot_right(jnp.where(mask, queries, none), key_rows) * HEAD_DIM ** (-0.5)
                total = jnp.sum(jnp.where(lane == 2 * step + which, lse[rows], 0.0), -1, keepdims=True)
                probs = jnp.exp(scores - total)
                grad_values = dot_left(probs.astype(low), grads)
                grad_probs = dot_right(jnp.where(mask, grads, none), values)
                inner = jnp.sum(probs * grad_probs, -1, keepdims=True)
                grad_scores = (probs * (grad_probs - inner)).astype(low)
                grad_queries = dot(grad_scores, key_rows) * HEAD_DIM ** (-0.5)
                grad_keys = dot_left(grad_scores, queries) * HEAD_DIM ** (-0.5)
                outs.append((grad_queries, grad_keys, grad_values))
            first = head_mask(shape, 0)
            for part in range(3):
                grad_triple[part, rows, here] = jnp.where(first, outs[0][part], outs[1][part]).astype(low)
        return carry

    lax.fori_loop(0, HEADS // 2, pair, 0)
    scaled, spread = norm_parts(stream[...])
    normed_t = (scaled * vector[0:1] + vector[1:2]).T.astype(low)
    for copy in in_copies:
        copy.wait()
    grad_normed = jnp.zeros((TOKENS, D), full)
    for part in range(3):
        block = grad_triple[part]
        if part == 0:
            vector_grad[2:3] = rows_sum(block.astype(full))
        if part == 2:
            vector_grad[3:4] = rows_sum(block.astype(full))
        stage[part] = dot(normed_t, block).astype(low).reshape(16, 48, D)
        for side_unit in range(2):
            unit = 2 * part + side_unit
            source = stage.at[part, :, :, pl.ds(side_unit * UNIT, UNIT)]
            leaving.append(leave(source, target, unit // 3, at + 48 * (unit % 3), out_sems.at[unit]))
            leaving[-1].start()
        grad_normed += dot_right(block, flat(w_in[:, :, part * D : (part + 1) * D]))
    vector_grad[0:1] = rows_sum(grad_normed * scaled)
    vector_grad[1:2] = rows_sum(grad_normed)
    upstream[...] = grad_middle[...] + norm_back(grad_normed, scaled, spread, vector[0:1])
    for copy in leaving:
        copy.wait()


def embed_back_kernel(at, carried, upstream, ids, chosen, grad_logits, small, *refs):
    target, stage, sems = refs[carried:]
    leaving = [pltpu.make_async_copy(small, target.at[:, :, pl.ds(at + 144, 16), :], sems.at[6])]
    leaving[0].start()
    stream_t = upstream[...].T.astype(low)
    chosen_t = chosen[...].astype(full).T.astype(low)
    for tile in range(3):
        word = lax.broadcasted_iota(jnp.int32, (TOKENS, D), 1) + tile * D
        hot = jnp.where(word == ids[...], 1.0, 0.0).astype(low)
        block = dot(stream_t, hot) + dot(chosen_t, grad_logits[:, tile * D : tile * D + D])
        stage[tile] = block.astype(low).reshape(16, 48, D)
        for side_unit in range(2):
            unit = 2 * tile + side_unit
            source = stage.at[tile, :, :, pl.ds(side_unit * UNIT, UNIT)]
            leaving.append(leave(source, target, unit // 3, at + 48 * (unit % 3), sems.at[unit]))
            leaving[-1].start()
    for copy in leaving:
        copy.wait()


def shape_of(*dims, kind=full):
    return jax.ShapeDtypeStruct(dims, kind)


class Line:
    def __init__(self, token):
        self.token = token

    def call(self, kernel, operands, in_specs, outs, out_specs, scratch, grid=None, prefetch=0, aliases=None, cost=0):
        def ordered(*refs):
            return kernel(*refs[:prefetch], *refs[prefetch + 1 :])

        in_specs = [ANY] + in_specs
        if grid is None:
            how = dict(in_specs=in_specs, out_specs=out_specs, scratch_shapes=scratch)
        else:
            spec = pltpu.PrefetchScalarGridSpec(
                num_scalar_prefetch=prefetch,
                grid=grid,
                in_specs=in_specs,
                out_specs=out_specs,
                scratch_shapes=scratch,
            )
            how = dict(grid_spec=spec)
        results = pl.pallas_call(
            ordered,
            out_shape=outs,
            compiler_params=pltpu.CompilerParams(vmem_limit_bytes=56 * 2**20),
            cost_estimate=pl.CostEstimate(flops=1000 + int(cost * 1.15e9), bytes_accessed=1000, transcendentals=0),
            input_output_aliases={source + 1: target for source, target in (aliases or {}).items()},
            **how,
        )(*operands[:prefetch], self.token, *operands[prefetch:])
        self.token = results[0]
        return results


DMA = pltpu.SemaphoreType.DMA
MERGE_COST, JOIN_COST = 3, 3


def embed(line, core, codes, pos, valid, pair, at):
    return line.call(
        partial(embed_kernel, at),
        (core, codes, pos, valid, *pair),
        [SMEM, VMEM, VMEM, VMEM, ANY, ANY],
        (shape_of(TOKENS, 1, kind=jnp.int32), shape_of(TOKENS, D)),
        (VMEM, VMEM),
        [pltpu.VMEM((16, 48, VPAD), low), DMA((6,))],
        cost=6,
    )


def attention(line, core, stream, vector, pairs, ats):
    return line.call(
        partial(attention_kernel, ats),
        (core, stream, vector, *pairs[0], *pairs[1]),
        [SMEM, VMEM, VMEM] + [ANY] * 4,
        (
            shape_of(3, TOKENS, D, kind=low),
            shape_of(TOKENS, 128),
            shape_of(TOKENS, D, kind=low),
            shape_of(TOKENS, D),
        ),
        (VMEM,) * 4,
        [pltpu.VMEM((16, 48, 3 * D), low), pltpu.VMEM((16, 48, D), low), DMA((8,))],
        cost=15,
    )


def feed_forward(line, core, middle, vector, pairs, ats):
    return line.call(
        partial(forward_kernel, ats),
        (core, middle, vector, *pairs[0], *pairs[1], *pairs[2]),
        [SMEM, VMEM, VMEM] + [ANY] * 6,
        (shape_of(4, TOKENS, D), shape_of(TOKENS, D)),
        (ANY, VMEM),
        [
            pltpu.VMEM((16, 48, FF), low),
            pltpu.VMEM((16, 192, D), low),
            pltpu.VMEM((TOKENS, D), low),
            pltpu.VMEM((2, TOKENS, D), full),
            DMA((16,)),
            DMA((2,)),
        ],
        cost=12,
    )


def head(line, core, stream, final, codes, pos_column, pos_row, scale, valid, bias, pair, at):
    return line.call(
        partial(head_kernel, at),
        (core, stream, final, codes, pos_column, pos_row, scale, valid, bias, *pair),
        [SMEM] + [VMEM] * 8 + [ANY, ANY],
        (
            shape_of(TOKENS, D),
            shape_of(SLOTS, D, kind=low),
            shape_of(SLOTS, VPAD, kind=low),
            shape_of(1, VPAD),
            shape_of(2, D),
            shape_of(1, 128),
        ),
        (VMEM,) * 6,
        [pltpu.VMEM((16, 48, VPAD), low), pltpu.VMEM((SLOTS, VPAD), full), DMA((6,))],
        cost=10,
    )


class Grads:
    def __init__(self):
        self.places, self.arrays = placed(SCATTER), {}

    def results(self, pieces, before, first):
        names = sorted({self.places[piece][0] for piece in pieces})
        operands, shapes, aliases = [], [], {}
        for name in names:
            if name in self.arrays:
                aliases[before + len(operands)] = first + len(shapes)
                operands.append(self.arrays[name])
            shapes.append(shape_of(16, 2, height(SCATTER[name]), UNIT, kind=low))
        spots = tuple((names.index(self.places[piece][0]), self.places[piece][1]) for piece in pieces)
        return names, operands, shapes, aliases, spots


def feed_forward_back(line, grads, layer, core, upstream, middle, vector, hidden, pairs, ats):
    names, more, shapes, aliases, spots = grads.results((f"D{layer}", f"E{layer}", f"F{layer}"), 11, 2)
    results = line.call(
        partial(forward_back_kernel, ats, spots, len(more)),
        (core, upstream, middle, vector, hidden, *pairs[0], *pairs[1], *pairs[2], *more),
        [SMEM, VMEM, VMEM, VMEM] + [ANY] * (7 + len(more)),
        (shape_of(TOKENS, D), shape_of(12, D), *shapes),
        (VMEM, VMEM) + (ANY,) * len(shapes),
        [
            pltpu.VMEM((16, 48, FF), low),
            pltpu.VMEM((16, 192, D), low),
            pltpu.VMEM((D, TOKENS), low),
            pltpu.VMEM((TOKENS, D), low),
            pltpu.VMEM((2, TOKENS, D), full),
            pltpu.VMEM((2, 4, 192, D), low),
            pltpu.VMEM((2, 16, 48, D), low),
            pltpu.VMEM((TOKENS, D), full),
            DMA((16,)),
            DMA((2,)),
            DMA((2, 4)),
        ],
        aliases=aliases,
        cost=22,
    )
    grads.arrays.update(zip(names, results[2:]))
    return results[:2]


def attention_back(line, grads, layer, core, grad_middle, stream, vector, triple, lse, mixed, pairs, ats):
    names, more, shapes, aliases, spots = grads.results((f"Q{layer}", f"O{layer}"), 11, 2)
    results = line.call(
        partial(attention_back_kernel, ats, spots, len(more)),
        (core, grad_middle, stream, vector, triple, lse, mixed, *pairs[0], *pairs[1], *more),
        [SMEM] + [VMEM] * 6 + [ANY] * (4 + len(more)),
        (shape_of(TOKENS, D), shape_of(12, D), *shapes),
        (VMEM, VMEM) + (ANY,) * len(shapes),
        [
            pltpu.VMEM((16, 48, 3 * D), low),
            pltpu.VMEM((16, 48, D), low),
            pltpu.VMEM((TOKENS, D), low),
            pltpu.VMEM((3, TOKENS, D), low),
            pltpu.VMEM((4, 16, 48, D), low),
            DMA((8,)),
            DMA((8,)),
        ],
        aliases=aliases,
        cost=24,
    )
    grads.arrays.update(zip(names, results[2:]))
    return results[:2]


def embed_back(line, grads, upstream, ids, chosen, grad_logits, small):
    names, more, shapes, aliases, spots = grads.results(("T",), 5, 0)
    results = line.call(
        partial(embed_back_kernel, spots[0][1], len(more)),
        (upstream, ids, chosen, grad_logits, small, *more),
        [VMEM] * 4 + [ANY] * (1 + len(more)),
        tuple(shapes),
        (ANY,) * len(shapes),
        [pltpu.VMEM((3, 16, 48, D), low), DMA((8,))],
        aliases=aliases,
        cost=15,
    )
    grads.arrays.update(zip(names, results))


def join(line, bits, axis, own, other):
    dims = list(own.shape)
    dims[axis] = 2
    cut = next((i for i in range(4) if own.shape[i] == 2), None)
    steps = 1 if cut is None else 2

    def kernel(bits_ref, own_ref, other_ref, out, stage, in_sems, out_sems):
        loads, stores = [], []
        for step in range(steps):
            for which, source in enumerate((own_ref, other_ref)):
                slot = 2 * step + which
                part = [slice(None)] * 4
                if cut is not None:
                    part[cut] = pl.ds(step, 1)
                loads.append(pltpu.make_async_copy(source.at[tuple(part)], stage.at[slot], in_sems.at[slot]))
                place = bits_ref[axis] if which == 0 else 1 - bits_ref[axis]
                part[axis] = pl.ds(place, 1)
                stores.append(pltpu.make_async_copy(stage.at[slot], out.at[tuple(part)], out_sems.at[slot]))
        for copy in loads:
            copy.start()
        for load, store in zip(loads, stores):
            load.wait()
            store.start()
        for copy in stores:
            copy.wait()

    block = [1 if i == cut else size for i, size in enumerate(own.shape)]
    scratch = [pltpu.VMEM((2 * steps, *block), low), DMA((2 * steps,)), DMA((2 * steps,))]
    operands = (bits, own, other)
    return line.call(kernel, operands, [SMEM, ANY, ANY], (shape_of(*dims, kind=low),), (ANY,), scratch, cost=JOIN_COST)[0]


def merge(line, bits, parts, gone, axis, kind=None):
    rows = parts[-1].shape[-2]
    open_axes = [i for i in range(4) if i not in gone and i != axis]
    dims = [2 if i in open_axes else 1 for i in range(4)]
    kind = kind or (full if axis is None else low)
    cut = open_axes[0] if open_axes else None
    block = [1 if i == cut else size for i, size in enumerate(dims)]

    def spec(shape):
        def index(step, bits_ref):
            place = []
            for i in range(4):
                if i == cut:
                    place.append(step)
                elif shape[i] == 1 or i in open_axes:
                    place.append(0)
                else:
                    place.append(1 - bits_ref[i] if i == axis else bits_ref[i])
            if len(shape) == 7:
                place.append(bits_ref[4])
            return (*place, 0, 0)

        return pl.BlockSpec((*block, *(None,) * (len(shape) - 6), rows, UNIT), index)

    def kernel(bits_ref, *refs):
        total = refs[0][...].astype(full)
        for ref in refs[1:-1]:
            total += ref[...].astype(full)
        refs[-1][...] = total.astype(kind)

    return line.call(
        kernel,
        (bits, *parts),
        [spec(part.shape) for part in parts],
        (shape_of(*dims, rows, UNIT, kind=kind),),
        (spec((*dims, rows, UNIT)),),
        [],
        grid=(1 if cut is None else 2,),
        prefetch=1,
        cost=MERGE_COST,
    )[0]


def update(weight, moment, average, grad, factor):
    clipped = grad * factor
    moment_next = inertia * moment + clipped
    weight_next = weight - step_rate * (clipped + inertia * moment_next)
    return (weight_next, moment_next, average_decay * average + (1.0 - average_decay) * weight_next)


def pack_small(vecs, final_norm, counts):
    own = jnp.concatenate(
        [vecs[0], vecs[1], final_norm[0], final_norm[1], counts.astype(full)]
    ).astype(low)
    own = jnp.pad(own, (0, 2 * UNIT - own.shape[0])).reshape(2, UNIT)
    return jnp.pad(own, ((0, 14), (0, 0)))


def body(hops, *arguments):
    codes, mask_pos, mask_count, table, w_qkv, w_out, w_up, w_down = arguments[:8]
    layer_vecs, final_norm, head_bias = arguments[8:11]
    moments, averages = arguments[11:19], arguments[19:27]
    images, seq_len = codes.shape
    core = side("core") if hops else jnp.zeros((), jnp.int32)
    own = core.astype(jnp.int32).reshape(1)
    line = Line(own)
    places = placed(GATHER)
    table_t = jnp.pad(table.T, ((0, 0), (0, VPAD - V)))
    shards = {"T": table_t}
    for l in range(L):
        shards[f"Q{l}"], shards[f"O{l}"], shards[f"D{l}"] = w_qkv[l], w_out[l], w_down[l]
        shards[f"U{l}"] = w_up[l]

    def split_up(make):
        out = {}
        for name, shard in shards.items():
            if name[0] == "U":
                block = make(shard, 4, PIECES["E0"][1][0][1])
                half = block.shape[-2] // 2
                out["E" + name[1]], out["F" + name[1]] = block[..., :half, :], block[..., half:, :]
            else:
                out[name] = make(shard, *PIECES[name][1][0])
        return out

    if hops:
        bits = jnp.stack([side(hop) for hop in ("zhi", "zlo", "y", "x", "core")]).astype(jnp.int32)
        local = split_up(lambda shard, units, rows: column_units(shard).reshape(2, -1, UNIT).astype(low))
        pieces = [piece for name in GATHER for piece in GATHER[name]]
        halves = jnp.concatenate([local[piece] for piece in pieces], 1)
        mine_half = pick(halves, core, 0)[0]
        other_half = swap(pick(halves, 1 - core, 0)[0], "core")
        whole, start = {}, 0
        for piece in pieces:
            units, rows = PIECES[piece][1][0]
            mine = mine_half[start : start + units * rows].reshape(units, 1, rows, UNIT)
            yours = other_half[start : start + units * rows].reshape(units, 1, rows, UNIT)
            whole[piece] = in_order(core, mine, yours, 1).reshape(-1, UNIT)
            start += units * rows
        whole["T"] = jnp.concatenate([whole["T"], pack_small(layer_vecs, final_norm, mask_count)])
        flying, done, pairs = {}, {}, {}
        for name in GATHER:
            chunk = jnp.concatenate([whole[piece] for piece in GATHER[name]])
            if name not in GATHER_WAY:
                chunk = lax.all_gather(chunk, BOTH, axis=0)
                pairs[name] = [chunk.reshape(16, 2, *chunk.shape[1:])] * 2
                continue
            chunk = chunk[None, None, None, None]
            flying[name], done[name] = (chunk, swap(chunk, GATHER_WAY[name][0])), 0

        def next_hop(name):
            way = GATHER_WAY[name]
            chunk = join(line, bits, HOPS[way[done[name]]][3], *flying[name])
            done[name] += 1
            if done[name] < len(way):
                flying[name] = chunk, swap(chunk, way[done[name]])
            else:
                pairs[name] = [part.reshape(16, -1, UNIT) for part in (chunk, swap(chunk, "core"))]
    else:

        def everywhere(shard):
            return lax.all_gather(shard.astype(low), BOTH, axis=0, tiled=True)

        blocks = split_up(lambda shard, units, rows: weight_blocks(everywhere(shard), units, 2 * rows))
        pairs = {}
        for name in GATHER:
            chunk = jnp.concatenate([blocks[piece] for piece in GATHER[name]], 2)
            pairs[name] = [chunk[0], chunk[1]]
        vectors = [everywhere(layer_vecs[l]).astype(full).reshape(12, D) for l in range(L)]
        final_float = everywhere(final_norm.T).T.astype(full)
        mask_total = lax.psum(jnp.sum(mask_count.astype(full)), BOTH)

    slots = jnp.arange(M, dtype=jnp.int32)
    valid = (slots[None, :] < mask_count[:, None]).astype(full)
    spots = mask_pos + seq_len * jnp.arange(images, dtype=jnp.int32)[:, None]
    codes_row, codes_column = codes.reshape(1, TOKENS), codes.reshape(TOKENS, 1)
    pos_row, pos_column = spots.reshape(1, SLOTS), spots.reshape(SLOTS, 1)
    valid_row, valid_column = valid.reshape(1, SLOTS), valid.reshape(SLOTS, 1)
    bias = jnp.pad(head_bias, (0, VPAD - V), constant_values=-1e30).reshape(1, VPAD)

    def sources(*names):
        return [pairs[places[name][0]] for name in names], tuple(places[name][1] for name in names)

    kept = [None] * L
    for step in FORWARD_ORDER:
        if step in GATHER_WAY:
            if hops:
                next_hop(step)
        elif step == "embed":
            (pair,), (at,) = sources("T")
            ids, stream = embed(line, own, codes_column, pos_row, valid_row, pair, at)
            if hops:
                small = [part[:, at + 144 : at + 146].reshape(16, 1, 2 * UNIT) for part in pair]
                small = in_order(core, small[0], small[1], 1).reshape(32, 2 * UNIT).astype(full)
                vectors = [small[:, 288 * l : 288 * l + 288].reshape(12, D) for l in range(L)]
                final_float = small[:, 576:624].reshape(32, 2, 24).transpose(1, 0, 2).reshape(2, D)
                mask_total = jnp.sum(small[:, 624 : 624 + images])
        elif step == "head":
            scale = valid_column * (1.0 / mask_total)
            (pair,), (at,) = sources("T")
            upstream, chosen, grad_logits, bias_grad, final_grad, loss = head(
                line, own, stream, final_float, codes_row, pos_column, pos_row, scale, valid_column, bias, pair, at
            )
        elif step[:-1] == "attention":
            l = int(step[-1])
            two, ats = sources(f"Q{l}", f"O{l}")
            triple, lse, mixed, middle = attention(line, own, stream, vectors[l], two, ats)
            kept[l] = stream, triple, lse, mixed, middle
        else:
            l = int(step[-1])
            three, ats = sources(f"D{l}", f"E{l}", f"F{l}")
            hidden, stream = feed_forward(line, own, kept[l][4], vectors[l], three, ats)
            kept[l] = kept[l] + (hidden,)

    grads = Grads()
    vector_grads = [0.0] * L
    parts, gone, totals = {}, {}, {}

    def small_blocks():
        small = [vector_grads[0].reshape(-1), vector_grads[1].reshape(-1), final_grad[0], final_grad[1]]
        if not hops:
            return small, jnp.zeros((16, 2, 16, UNIT), low)
        small.append(bias_grad[0, :2048])
        small = jnp.concatenate([grad.reshape(32, -1) for grad in small], 1)
        small = jnp.pad(small, ((0, 0), (0, 2 * UNIT - 688))).astype(low)
        small = small.reshape(16, 2, 2, UNIT)
        return small, jnp.pad(small, ((0, 0), (0, 0), (0, 14), (0, 0)))

    def ready(names):
        for name in names:
            grad = grads.arrays[name]
            if name in SCATTER_WAY:
                shape = (2, 2, 2, 2) + grad.shape[1:]
                arrived = swap(pick(grad, 1 - core, 1)[:, 0], "core")
                parts[name], gone[name] = [grad.reshape(shape), arrived.reshape(shape[:4] + shape[5:])], []
            else:
                grad = grad.reshape(32, -1, UNIT)
                total = lax.psum_scatter(grad, BOTH, scatter_dimension=0, tiled=False)
                parts[name], totals[name] = None, total.astype(full)

    complete = {name: [p for p in SCATTER[name]] for name in SCATTER}

    def finished(pieces):
        for piece in pieces:
            complete[grads.places[piece][0]].remove(piece)
        names = [name for name in SCATTER if name in grads.arrays and not complete[name] and name not in parts]
        if hops:
            ready(names)

    for step in BACKWARD_ORDER:
        if step in SCATTER_WAY:
            if not hops:
                continue
            way = SCATTER_WAY[step]
            if len(gone[step]) == len(way):
                totals[step] = merge(line, bits, parts[step], gone[step], None)[0, 0, 0, 0]
                continue
            hop = way[len(gone[step])]
            axis = HOPS[hop][3]
            parts[step].append(swap(merge(line, bits, parts[step], gone[step], axis), hop))
            gone[step].append(axis)
        elif step == "embed":
            small_grads, block = small_blocks()
            embed_back(line, grads, upstream, ids, chosen, grad_logits, block)
            finished(("T",))
        elif step[:-1] == "attention":
            l = int(step[-1])
            stream, triple, lse, mixed = kept[l][:4]
            two, ats = sources(f"Q{l}", f"O{l}")
            upstream, early = attention_back(
                line, grads, l, own, grad_middle, stream, vectors[l], triple, lse, mixed, two, ats
            )
            vector_grads[l] += early
            finished((f"Q{l}", f"O{l}"))
        else:
            l = int(step[-1])
            three, ats = sources(f"D{l}", f"E{l}", f"F{l}")
            grad_middle, late = feed_forward_back(
                line, grads, l, own, upstream, kept[l][4], vectors[l], kept[l][5], three, ats
            )
            vector_grads[l] += late
            finished((f"D{l}", f"E{l}", f"F{l}"))

    shares = {}
    if hops:
        for names in LAST:
            mine, leaving, where = [], [], []
            for name in names:
                start = 0
                for piece in SCATTER[name]:
                    units, rows = PIECES[piece][1][0]
                    block = totals[name][start : start + 2 * units * rows].reshape(units, 2, rows, UNIT)
                    mine.append(pick(block, core, 1).reshape(-1, UNIT))
                    leaving.append(pick(block, 1 - core, 1).reshape(-1, UNIT))
                    where.append((piece, units, rows))
                    start += PIECES[piece][0]
            mine, arrived = jnp.concatenate(mine), swap(jnp.concatenate(leaving), "core")
            both = in_order(core, mine[None], arrived[None], 0)
            start = 0
            for piece, units, rows in where:
                block = both[:, start : start + units * rows].reshape(2, units, rows, UNIT)
                shares[piece] = block
                start += units * rows
        for l in range(L):
            shares[f"U{l}"] = jnp.concatenate([shares[f"E{l}"], shares[f"F{l}"]], 1)
        for piece in list(shares):
            block = shares[piece]
            shares[piece] = block.transpose(2, 0, 1, 3).reshape(block.shape[2], -1)
        at = grads.places["T"][1] + 144
        small_sum = totals[grads.places["T"][0]][at : at + 2].reshape(-1)
    else:
        head_grad, loss_sum = lax.psum((bias_grad[0, :V], loss[0, 0]), BOTH)
        small_sum = [lax.psum_scatter(g, BOTH, scatter_dimension=0, tiled=True) for g in small_grads]
        small_sum = jnp.concatenate(small_sum)
        for piece, (name, start) in grads.places.items():
            size = 144 if piece == "T" else PIECES[piece][0]
            shares[piece] = grads.arrays[name][:, :, start : start + size].transpose(1, 0, 2, 3)
        for l in range(L):
            shares[f"U{l}"] = jnp.concatenate([shares[f"E{l}"], shares[f"F{l}"]], 2)
        for piece, block in shares.items():
            units, rows = (4, 24) if piece[0] == "U" else PIECES[piece][1][0]
            weight = natural_weight(block, units, 2 * rows).astype(full)
            shares[piece] = lax.psum_scatter(weight, BOTH, scatter_dimension=0, tiled=True)
    width, narrow = layer_vecs.shape[1], final_norm.shape[1]
    grads_own = [shares["T"][:, :V].T]
    grads_own += [jnp.stack([shares[f"{kind}{l}"] for l in range(L)]) for kind in "QOUD"]
    grads_own += [
        small_sum[: 2 * width].reshape(L, width),
        small_sum[2 * width : 2 * width + 2 * narrow].reshape(2, narrow),
    ]
    squares = reduce(jnp.add, [jnp.sum(share * share) for share in grads_own])
    if hops:
        bias_share = small_sum[624:688]
        squares = squares + jnp.sum(bias_share * bias_share)
        tail = jnp.concatenate([bias_share, squares[None], loss[0, :1], jnp.zeros(62)])
        tail = tail.reshape(1, 1, 1, 1, 1, 128)
        for hop in ("core", "x", "y", "zlo", "zhi"):
            axis = HOPS[hop][3]
            tail = in_order(side(hop), tail, swap(tail, hop), 4 if axis is None else axis)
        tail = tail.reshape(32, 128)
        head_grad = tail[:, :64].reshape(-1)[:V]
        squares, loss_sum = jnp.sum(tail[:, 64]), jnp.sum(tail[:, 65])
    else:
        squares = lax.psum(squares, BOTH) + jnp.sum(head_grad * head_grad)
    grad_norm = jnp.sqrt(squares)
    factor = jnp.minimum(1.0, clip_bound / (grad_norm + epsilon))
    results = [
        update(weight, moment, average, grad, factor)
        for weight, moment, average, grad in zip(arguments[3:11], moments, averages, grads_own + [head_grad])
    ]
    return (
        (loss_sum, mask_total, grad_norm)
        + tuple(result[0] for result in results)
        + tuple(result[1] for result in results)
        + tuple(result[2] for result in results)
    )


def solution(mesh):
    return jax.shard_map(
        partial(body, mesh.shape["dp"] == 8 and mesh.shape["fsdp"] == 4),
        mesh=mesh,
        in_specs=(
            P(("dp", "fsdp"), None),
            P(("dp", "fsdp"), None),
            P(("dp", "fsdp")),
            P(None, ("dp", "fsdp")),
            P(None, ("dp", "fsdp"), None),
            P(None, ("dp", "fsdp"), None),
            P(None, ("dp", "fsdp"), None),
            P(None, ("dp", "fsdp"), None),
            P(None, ("dp", "fsdp")),
            P(None, ("dp", "fsdp")),
            P(),
            P(None, ("dp", "fsdp")),
            P(None, ("dp", "fsdp"), None),
            P(None, ("dp", "fsdp"), None),
            P(None, ("dp", "fsdp"), None),
            P(None, ("dp", "fsdp"), None),
            P(None, ("dp", "fsdp")),
            P(None, ("dp", "fsdp")),
            P(),
            P(None, ("dp", "fsdp")),
            P(None, ("dp", "fsdp"), None),
            P(None, ("dp", "fsdp"), None),
            P(None, ("dp", "fsdp"), None),
            P(None, ("dp", "fsdp"), None),
            P(None, ("dp", "fsdp")),
            P(None, ("dp", "fsdp")),
            P(),
        ),
        out_specs=(
            P(),
            P(),
            P(),
            P(None, ("dp", "fsdp")),
            P(None, ("dp", "fsdp"), None),
            P(None, ("dp", "fsdp"), None),
            P(None, ("dp", "fsdp"), None),
            P(None, ("dp", "fsdp"), None),
            P(None, ("dp", "fsdp")),
            P(None, ("dp", "fsdp")),
            P(),
            P(None, ("dp", "fsdp")),
            P(None, ("dp", "fsdp"), None),
            P(None, ("dp", "fsdp"), None),
            P(None, ("dp", "fsdp"), None),
            P(None, ("dp", "fsdp"), None),
            P(None, ("dp", "fsdp")),
            P(None, ("dp", "fsdp")),
            P(),
            P(None, ("dp", "fsdp")),
            P(None, ("dp", "fsdp"), None),
            P(None, ("dp", "fsdp"), None),
            P(None, ("dp", "fsdp"), None),
            P(None, ("dp", "fsdp"), None),
            P(None, ("dp", "fsdp")),
            P(None, ("dp", "fsdp")),
            P(),
        ),
        check_vma=False,
    )
```

```python
from functools import partial, reduce

import jax
import jax.numpy as jnp
from jax import lax
from jax.experimental import pallas as pl
from jax.experimental.pallas import tpu as pltpu
from jax.sharding import PartitionSpec as P

D = 768
HEADS = 12
HEAD_DIM = 64
FF = 3072
V = 2026
M = 128
L = 2
UNIT = 384
VPAD = 2304
BOTH = ("dp", "fsdp")


epsilon = 1e-06
step_rate = 10000.0
inertia = 0.5
average_decay = 0.5
clip_bound = 0.01


HOPS = {
    "zhi": ("dp", 4, 8, 0),
    "zlo": ("dp", 2, 8, 1),
    "y": ("dp", 1, 8, 2),
    "x": ("fsdp", 2, 4, 3),
    "core": ("fsdp", 1, 4, None),
}

PIECES = {"T": (160, ((3, 24),))}
for layer in range(L):
    PIECES.update(
        {
            f"Q{layer}": (144, ((3, 24),)),
            f"O{layer}": (48, ((1, 24),)),
            f"D{layer}": (192, ((1, 96),)),
            f"E{layer}": (96, ((2, 24),)),
            f"F{layer}": (96, ((2, 24),)),
        }
    )

GATHER = {
    "t": ("T",),
    "a": ("Q0", "O0"),
    "d": ("D0",),
    "u": ("E0", "F0"),
    "l": ("Q1", "O1", "D1", "E1", "F1"),
}
GATHER_WAY = {
    "t": ("zlo", "zhi", "y", "x"),
    "a": ("zlo", "zhi", "x", "y"),
    "d": ("zlo", "zhi", "y", "x"),
    "u": ("zlo", "zhi", "x", "y"),
}
SCATTER = {
    "c": ("D1", "E1", "F1"),
    "b": ("Q1", "O1"),
    "d": ("D0",),
    "u": ("E0", "F0"),
    "a": ("Q0", "O0"),
    "t": ("T",),
}
SCATTER_WAY = {
    "b": ("x", "y", "zhi", "zlo"),
    "d": ("x", "y", "zhi", "zlo"),
    "u": ("y", "x", "zhi", "zlo"),
    "a": ("y", "x", "zhi", "zlo"),
    "t": ("x", "y", "zhi", "zlo"),
}
FORWARD_ORDER = (
    ("l", "t", "a", "d", "u", "t", "a", "t", "a", "d", "u", "t", "a", "embed", "d", "u", "attention0", "d", "u")
    + ("forward0", "attention1", "forward1", "head")
)
BACKWARD_ORDER = (
    ("forward1", "attention1", "forward0", "b", "attention0", "b", "u", "d", "a", "embed", "u", "d", "t")
    + ("b", "a", "t", "u", "d", "b", "u", "a", "t", "d", "b", "u", "t", "d", "a", "t", "a")
)
LONG = {5: 14, 10: 14, 11: 14}
SETTLED = 15
LAST = (("c", "b"), ("u", "d", "t", "a"))


def placed(layout):
    places = {}
    for name, pieces in layout.items():
        start = 0
        for piece in pieces:
            places[piece] = (name, start)
            start += PIECES[piece][0]
    return places


def height(pieces):
    return sum(PIECES[piece][0] for piece in pieces)


def swap(tensor, hop):
    axis, flip, size, unused = HOPS[hop]
    return lax.ppermute(tensor, axis, [(i, i ^ flip) for i in range(size)])


def swap_both(tensor, hops):
    flips = [HOPS[hop] for hop in hops]
    if flips[0][0] == flips[1][0]:
        axis, flip, size = flips[0][0], flips[0][1] ^ flips[1][1], flips[0][2]
        return lax.ppermute(tensor, axis, [(i, i ^ flip) for i in range(size)])
    return swap(swap(tensor, hops[0]), hops[1])


def side(hop):
    axis, flip, unused, unused = HOPS[hop]
    return (lax.axis_index(axis) // flip) % 2


def in_order(bit, own, other, axis):
    return jnp.where(
        bit == 0, jnp.concatenate([own, other], axis), jnp.concatenate([other, own], axis)
    )


def pick(tensor, index, axis):
    return lax.dynamic_slice_in_dim(tensor, index, 1, axis)


def column_units(shard):
    rows, width = shard.shape
    return shard.reshape(rows, 2, width // (2 * UNIT), UNIT).transpose(1, 2, 0, 3)


def natural_weight(halves, units, rows):
    chips = halves.shape[1]
    block = halves.reshape(2, chips, units, rows, UNIT)
    return block.transpose(1, 3, 0, 2, 4).reshape(chips * rows, 2 * units * UNIT)


def weight_blocks(grad, units, rows):
    chips = grad.shape[0] // rows
    block = grad.reshape(chips, rows, 2, units, UNIT).transpose(2, 0, 3, 1, 4)
    return block.reshape(2, chips, units * rows, UNIT)


TOKENS = 512
SLOTS = 256
ANY = pl.BlockSpec(memory_space=pl.ANY)
SMEM = pl.BlockSpec(memory_space=pltpu.SMEM)
VMEM = pl.BlockSpec(memory_space=pltpu.VMEM)
low = jnp.bfloat16
full = jnp.float32


def dot(left, right):
    return lax.dot_general(left, right, (((1,), (0,)), ((), ())), preferred_element_type=full)


def dot_right(left, right):
    return lax.dot_general(left, right, (((1,), (1,)), ((), ())), preferred_element_type=full)


def dot_left(left, right):
    return lax.dot_general(left, right, (((0,), (0,)), ((), ())), preferred_element_type=full)


def norm_parts(stream):
    centre = stream - jnp.mean(stream, -1, keepdims=True)
    spread = lax.rsqrt(jnp.mean(centre * centre, -1, keepdims=True) + epsilon)
    return centre * spread, spread


def norm_back(upstream, scaled, spread, gain):
    weighted = upstream * gain
    return spread * (
        weighted
        - jnp.mean(weighted, -1, keepdims=True)
        - scaled * jnp.mean(weighted * scaled, -1, keepdims=True)
    )


def rows_sum(tensor):
    return jnp.sum(tensor, 0, keepdims=True)


def columns(start, size):
    return pl.ds(pl.multiple_of(start, 128), size)


def unit_copies(core, halves, at, units, first, half_units, target, sems):
    copies = []
    for which, source in enumerate(halves):
        half = core if which == 0 else 1 - core
        if len(source.shape) == 4:
            source = source.at[:, half]
        for unit in range(units):
            copies.append(
                pltpu.make_async_copy(
                    source.at[:, pl.ds(at + 48 * unit, 48), :],
                    target.at[:, :, columns((half * half_units + first + unit) * UNIT, UNIT)],
                    sems.at[which * units + unit],
                )
            )
    return copies


def flat(block):
    return block.reshape(block.shape[0] * block.shape[1], block.shape[2])


def head_mask(shape, which):
    lane = lax.broadcasted_iota(jnp.int32, shape, 1)
    return lane < HEAD_DIM if which == 0 else lane >= HEAD_DIM


def embed_kernel(at, core, codes, pos, valid, mine, yours, ids, stream, weight, sems):
    copies = unit_copies(core[0], (mine, yours), at, 3, 0, 3, weight, sems)
    for copy in copies:
        copy.start()
    place = lax.broadcasted_iota(jnp.int32, (TOKENS, SLOTS), 0)
    masked = jnp.max(jnp.where(place == pos[...], valid[...], 0.0), -1, keepdims=True)
    tokens = jnp.where(masked > 0, V - 1, codes[...])
    ids[...] = tokens
    for copy in copies:
        copy.wait()
    acc = jnp.zeros((TOKENS, D), full)
    for tile in range(3):
        word = lax.broadcasted_iota(jnp.int32, (TOKENS, D), 1) + tile * D
        hot = jnp.where(word == tokens, 1.0, 0.0).astype(low)
        acc += dot_right(hot, flat(weight[:, :, tile * D : (tile + 1) * D]))
    stream[...] = acc


def attention_kernel(
    ats, core, stream, vector, *refs
):
    in_pair, out_pair = refs[0:2], refs[2:4]
    triple, lse, mixed, middle, w_in, w_out, sems = refs[4:]
    in_copies = unit_copies(core[0], in_pair, ats[0], 3, 0, 3, w_in, sems.at[pl.ds(0, 6)])
    out_copies = unit_copies(core[0], out_pair, ats[1], 1, 0, 1, w_out, sems.at[pl.ds(6, 2)])
    for copy in in_copies + out_copies:
        copy.start()
    scaled, unused = norm_parts(stream[...])
    normed = (scaled * vector[0:1] + vector[1:2]).astype(low)
    for copy in in_copies:
        copy.wait()
    for part in range(3):
        block = dot(normed, flat(w_in[:, :, part * D : (part + 1) * D]))
        if part == 0:
            block = block + vector[2:3]
        if part == 2:
            block = block + vector[3:4]
        triple[part] = block.astype(low)
    lse[...] = jnp.zeros_like(lse)
    shape = (256, 128)
    lane = lax.broadcasted_iota(jnp.int32, shape, 1)

    def pair(step, carry):
        here = columns(step * 128, 128)
        for image in range(2):
            rows = slice(256 * image, 256 * image + 256)
            queries, key_rows, values = triple[0, rows, here], triple[1, rows, here], triple[2, rows, here]
            results = []
            for which in range(2):
                query = jnp.where(head_mask(shape, which), queries, jnp.zeros_like(queries))
                scores = dot_right(query, key_rows) * HEAD_DIM ** (-0.5)
                peak = jnp.max(scores, -1, keepdims=True)
                raised = jnp.exp(scores - peak)
                total = jnp.sum(raised, -1, keepdims=True)
                probs = (raised * (1.0 / total)).astype(low)
                results.append(dot(probs, values))
                lse[rows] = jnp.where(lane == 2 * step + which, peak + jnp.log(total), lse[rows])
            mixed[rows, here] = jnp.where(head_mask(shape, 0), results[0], results[1]).astype(low)
        return carry

    lax.fori_loop(0, HEADS // 2, pair, 0)
    for copy in out_copies:
        copy.wait()
    middle[...] = stream[...] + dot(mixed[...], flat(w_out[...])) + vector[4:5]


def forward_copies(core, ats, pairs, w_up, w_down, sems):
    first = unit_copies(core, pairs[1], ats[1], 2, 0, 4, w_up, sems.at[pl.ds(0, 4)])
    second = unit_copies(core, pairs[2], ats[2], 2, 2, 4, w_up, sems.at[pl.ds(4, 4)])
    up = first[:2] + second[:2] + first[2:] + second[2:]
    down = []
    for tile in range(4):
        chips = pl.ds(4 * lax.rem(2 * core + tile, 4), 4)
        for which, source in enumerate(pairs[0]):
            half = core if which == 0 else 1 - core
            if len(source.shape) == 4:
                source = source.at[:, half]
            down.append(
                pltpu.make_async_copy(
                    source.at[chips, pl.ds(ats[0], 192), :],
                    w_down.at[chips, :, columns(half * UNIT, UNIT)],
                    sems.at[8 + 2 * tile + which],
                )
            )
    return [up[2 * tile : 2 * tile + 2] + down[2 * tile : 2 * tile + 2] for tile in range(4)]


CURVE = 0.7978845608028654


def forward_kernel(ats, core, middle, vector, *refs):
    pairs = [refs[0:2], refs[2:4], refs[4:6]]
    hidden, result, w_up, w_down, normed, stage, sems, out_sems = refs[6:]
    copies = forward_copies(core[0], ats, pairs, w_up, w_down, sems)
    for group in copies:
        for copy in group:
            copy.start()
    scaled, unused = norm_parts(middle[...])
    normed[...] = (scaled * vector[5:6] + vector[6:7]).astype(low)
    result[...] = middle[...] + vector[7:8]
    sent = []
    for step in range(4):
        tile = lax.rem(2 * core[0] + step, 4)
        for copy in copies[step]:
            copy.wait()
        block = dot(normed[...], flat(w_up[:, :, columns(tile * D, D)])) + vector[pl.ds(8 + tile, 1)]
        if step >= 2:
            sent[step - 2].wait()
        stage[step % 2] = block
        copy = pltpu.make_async_copy(stage.at[step % 2], hidden.at[tile], out_sems.at[step % 2])
        copy.start()
        sent.append(copy)
        bent = jnp.tanh(CURVE * (block + 0.044715 * (block * block * block)))
        active = (0.5 * block * (1.0 + bent)).astype(low)
        result[...] += dot(active, flat(w_down[pl.ds(4 * tile, 4)]))
    for copy in sent[2:]:
        copy.wait()


def head_kernel(
    at,
    core,
    stream,
    final,
    codes,
    pos_column,
    pos_row,
    scale,
    valid,
    bias,
    mine,
    yours,
    upstream,
    chosen_out,
    grad_logits_out,
    bias_grad,
    final_grad,
    loss,
    weight,
    logits,
    sems,
):
    copies = unit_copies(core[0], (mine, yours), at, 3, 0, 3, weight, sems)
    for copy in copies:
        copy.start()
    scaled, spread = norm_parts(stream[...])
    normed = (scaled * final[0:1] + final[1:2]).astype(low)
    picker = lax.broadcasted_iota(jnp.int32, (SLOTS, TOKENS), 1) == pos_column[...]
    target = jnp.sum(jnp.where(picker, codes[...], 0), -1, keepdims=True)
    chosen = dot(picker.astype(full).astype(low), normed).astype(low)
    chosen_out[...] = chosen
    for copy in copies:
        copy.wait()
    peak = jnp.full((SLOTS, 1), -jnp.inf, full)
    picked = jnp.zeros((SLOTS, 1), full)
    for tile in range(3):
        here = slice(tile * D, tile * D + D)
        block = dot(chosen, flat(weight[:, :, here])) + bias[:, here]
        logits[:, here] = block
        peak = jnp.maximum(peak, jnp.max(block, -1, keepdims=True))
        word = lax.broadcasted_iota(jnp.int32, (SLOTS, D), 1) + tile * D
        picked += jnp.sum(jnp.where(word == target, block, 0.0), -1, keepdims=True)
    total = jnp.zeros((SLOTS, 1), full)
    for tile in range(3):
        total += jnp.sum(jnp.exp(logits[:, tile * D : tile * D + D] - peak), -1, keepdims=True)
    log_total = peak + jnp.log(total)
    loss[...] = jnp.broadcast_to(rows_sum(valid[...] * (log_total - picked)), (1, 128))
    grad_chosen = jnp.zeros((SLOTS, D), full)
    for tile in range(3):
        here = slice(tile * D, tile * D + D)
        word = lax.broadcasted_iota(jnp.int32, (SLOTS, D), 1) + tile * D
        chance = jnp.exp(logits[:, here] - log_total)
        block = ((chance - jnp.where(word == target, 1.0, 0.0)) * scale[...]).astype(low)
        grad_logits_out[:, here] = block
        bias_grad[:, here] = rows_sum(block.astype(full))
        grad_chosen += dot_right(block, flat(weight[:, :, here]))
    back = lax.broadcasted_iota(jnp.int32, (TOKENS, SLOTS), 0) == pos_row[...]
    back = back.astype(full).astype(low)
    grad_normed = jnp.zeros((TOKENS, D), full)
    for unused in range(3):
        piece = grad_chosen.astype(low)
        grad_normed += dot(back, piece)
        grad_chosen -= piece.astype(full)
    final_grad[0:1] = rows_sum(grad_normed * scaled)
    final_grad[1:2] = rows_sum(grad_normed)
    upstream[...] = norm_back(grad_normed, scaled, spread, final[0:1])


def leave(source, target, half, at, sem):
    return pltpu.make_async_copy(source, target.at[:, half, pl.ds(at, 48), :], sem)


def forward_back_kernel(ats, outs, carried, core, upstream, middle, vector, hidden, *refs):
    pairs = [refs[0:2], refs[2:4], refs[4:6]]
    refs = refs[6 + carried :]
    grad_middle, vector_grad = refs[0:2]
    targets = refs[2:-11]
    w_up, w_down, normed_t, branch, hidden_tile, down_stage, up_stage, acc = refs[-11:-3]
    sems, hidden_sems, out_sems = refs[-3:]
    own = core[0]
    tiles = [lax.rem(2 * own + step, 4) for step in range(4)]
    fetch = [
        pltpu.make_async_copy(hidden.at[tiles[step]], hidden_tile.at[step % 2], hidden_sems.at[step % 2])
        for step in range(4)
    ]
    fetch[0].start()
    copies = forward_copies(own, ats, pairs, w_up, w_down, sems)
    for group in copies:
        for copy in group:
            copy.start()
    scaled, spread = norm_parts(middle[...])
    normed_t[...] = (scaled * vector[5:6] + vector[6:7]).astype(low).T
    branch[...] = upstream[...].astype(low)
    vector_grad[...] = jnp.zeros_like(vector_grad)
    vector_grad[7:8] = rows_sum(branch[...].astype(full))
    acc[...] = jnp.zeros_like(acc)
    every = slice(None)
    flights = []

    def land(step):
        for copy in flights[step]:
            copy.wait()

    for step in range(4):
        tile, slot = tiles[step], step % 2
        if step < 3:
            fetch[step + 1].start()
        for copy in copies[step]:
            copy.wait()
        fetch[step].wait()
        block = hidden_tile[slot]
        square = block * block
        bent = jnp.tanh(CURVE * (block + 0.044715 * (square * block)))
        active = (0.5 * block * (1.0 + bent)).astype(low)
        slope = 0.5 * (1.0 + bent) + 0.5 * block * (1.0 - bent * bent) * (
            CURVE * (1.0 + (3.0 * 0.044715) * square)
        )
        back = dot_right(branch[...], flat(w_down[pl.ds(4 * tile, 4)]))
        grad_hidden = (slope * back).astype(low)
        vector_grad[pl.ds(8 + tile, 1)] = rows_sum(grad_hidden.astype(full))
        if step >= 2:
            land(step - 2)
        grad_down = dot(active.T, branch[...]).astype(low)
        for half in range(2):
            down_stage[slot, half] = grad_down[:, half * UNIT : half * UNIT + UNIT].reshape(4, 192, UNIT)
        flight = []
        for half in range(2):
            place = targets[outs[0][0]].at[pl.ds(4 * tile, 4), half, pl.ds(outs[0][1], 192), :]
            source = down_stage.at[slot, half]
            flight.append(pltpu.make_async_copy(source, place, out_sems.at[slot, half]))
        grad_up = dot(normed_t[...], grad_hidden).astype(low)
        for unit in range(2):
            up_stage[slot, unit] = grad_up[:, unit * UNIT : unit * UNIT + UNIT].reshape(16, 48, UNIT)
        half = own if step < 2 else 1 - own
        for unit in range(2):
            source = up_stage.at[slot, unit]
            at = outs[1 + slot][1] + 48 * unit
            flight.append(leave(source, targets[outs[1 + slot][0]], half, at, out_sems.at[slot, 2 + unit]))
        for copy in flight:
            copy.start()
        flights.append(flight)
        acc[...] += dot_right(grad_hidden, flat(w_up[:, :, columns(tile * D, D)]))
    grad_normed = acc[...]
    scaled, spread = norm_parts(middle[...])
    vector_grad[5:6] = rows_sum(grad_normed * scaled)
    vector_grad[6:7] = rows_sum(grad_normed)
    grad_middle[...] = upstream[...] + norm_back(grad_normed, scaled, spread, vector[5:6])
    land(2)
    land(3)


def attention_back_kernel(
    ats, outs, carried, core, grad_middle, stream, vector, triple, lse, mixed, *refs
):
    in_pair, out_pair = refs[0:2], refs[2:4]
    refs = refs[4 + carried :]
    upstream, vector_grad = refs[0:2]
    targets = refs[2:-7]
    w_in, w_out, grad_mixed, grad_triple, stage, sems, out_sems = refs[-7:]
    target, at = targets[outs[0][0]], outs[0][1]
    out_target, out_at = targets[outs[1][0]], outs[1][1]
    leaving = []
    own = core[0]
    out_copies = unit_copies(own, out_pair, ats[1], 1, 0, 1, w_out, sems.at[pl.ds(6, 2)])
    in_copies = unit_copies(own, in_pair, ats[0], 3, 0, 3, w_in, sems.at[pl.ds(0, 6)])
    for copy in out_copies + in_copies:
        copy.start()
    every = slice(None)
    grad_out_low = grad_middle[...].astype(low)
    vector_grad[...] = jnp.zeros_like(vector_grad)
    vector_grad[4:5] = rows_sum(grad_out_low.astype(full))
    grad_out = dot(mixed[...].T, grad_out_low).astype(low)
    for half in range(2):
        stage[3, half] = grad_out[:, half * UNIT : half * UNIT + UNIT].reshape(16, 48, UNIT)
        source = stage.at[3, half]
        leaving.append(leave(source, out_target, half, out_at, out_sems.at[6 + half]))
        leaving[-1].start()
    for copy in out_copies:
        copy.wait()
    grad_mixed[...] = dot_right(grad_out_low, flat(w_out[...])).astype(low)
    shape = (256, 128)
    lane = lax.broadcasted_iota(jnp.int32, shape, 1)

    def pair(step, carry):
        here = columns(step * 128, 128)
        for image in range(2):
            rows = slice(256 * image, 256 * image + 256)
            queries, key_rows, values = triple[0, rows, here], triple[1, rows, here], triple[2, rows, here]
            grads = grad_mixed[rows, here]
            outs = []
            for which in range(2):
                mask = head_mask(shape, which)
                none = jnp.zeros_like(queries)
                scores = dot_right(jnp.where(mask, queries, none), key_rows) * HEAD_DIM ** (-0.5)
                total = jnp.sum(jnp.where(lane == 2 * step + which, lse[rows], 0.0), -1, keepdims=True)
                probs = jnp.exp(scores - total)
                grad_values = dot_left(probs.astype(low), grads)
                grad_probs = dot_right(jnp.where(mask, grads, none), values)
                inner = jnp.sum(probs * grad_probs, -1, keepdims=True)
                grad_scores = (probs * (grad_probs - inner)).astype(low)
                grad_queries = dot(grad_scores, key_rows) * HEAD_DIM ** (-0.5)
                grad_keys = dot_left(grad_scores, queries) * HEAD_DIM ** (-0.5)
                outs.append((grad_queries, grad_keys, grad_values))
            first = head_mask(shape, 0)
            for part in range(3):
                grad_triple[part, rows, here] = jnp.where(first, outs[0][part], outs[1][part]).astype(low)
        return carry

    lax.fori_loop(0, HEADS // 2, pair, 0)
    scaled, spread = norm_parts(stream[...])
    normed_t = (scaled * vector[0:1] + vector[1:2]).astype(low).T
    for copy in in_copies:
        copy.wait()
    grad_normed = jnp.zeros((TOKENS, D), full)
    for part in range(3):
        block = grad_triple[part]
        if part == 0:
            vector_grad[2:3] = rows_sum(block.astype(full))
        if part == 2:
            vector_grad[3:4] = rows_sum(block.astype(full))
        grad_in = dot(normed_t, block).astype(low)
        for side_unit in range(2):
            unit = 2 * part + side_unit
            stage[part, side_unit] = grad_in[:, side_unit * UNIT : side_unit * UNIT + UNIT].reshape(16, 48, UNIT)
            source = stage.at[part, side_unit]
            leaving.append(leave(source, target, unit // 3, at + 48 * (unit % 3), out_sems.at[unit]))
            leaving[-1].start()
        grad_normed += dot_right(block, flat(w_in[:, :, part * D : (part + 1) * D]))
    vector_grad[0:1] = rows_sum(grad_normed * scaled)
    vector_grad[1:2] = rows_sum(grad_normed)
    upstream[...] = grad_middle[...] + norm_back(grad_normed, scaled, spread, vector[0:1])
    for copy in leaving:
        copy.wait()


def embed_back_kernel(at, carried, upstream, ids, chosen, grad_logits, small, *refs):
    target, stage, sems = refs[carried:]
    leaving = [pltpu.make_async_copy(small, target.at[:, :, pl.ds(at + 144, 16), :], sems.at[6])]
    leaving[0].start()
    stream_t = upstream[...].astype(low).T
    chosen_t = chosen[...].T
    for tile in range(3):
        word = lax.broadcasted_iota(jnp.int32, (TOKENS, D), 1) + tile * D
        hot = jnp.where(word == ids[...], 1.0, 0.0).astype(low)
        block = dot(stream_t, hot) + dot(chosen_t, grad_logits[:, tile * D : tile * D + D])
        for side_unit in range(2):
            unit = 2 * tile + side_unit
            part = block[:, side_unit * UNIT : side_unit * UNIT + UNIT].astype(low)
            stage[tile, side_unit] = part.reshape(16, 48, UNIT)
            source = stage.at[tile, side_unit]
            leaving.append(leave(source, target, unit // 3, at + 48 * (unit % 3), sems.at[unit]))
            leaving[-1].start()
    for copy in leaving:
        copy.wait()


def shape_of(*dims, kind=full):
    return jax.ShapeDtypeStruct(dims, kind)


class Line:
    def __init__(self, token):
        self.tokens = [token]

    def wait(self, array):
        self.tokens.append(array)

    def call(self, kernel, operands, in_specs, outs, out_specs, scratch, grid=None, prefetch=0, aliases=None, cost=0):
        tokens, extra = self.tokens, len(self.tokens)

        def ordered(*refs):
            return kernel(*refs[:prefetch], *refs[prefetch + extra :])

        in_specs = [ANY] * extra + in_specs
        if grid is None:
            how = dict(in_specs=in_specs, out_specs=out_specs, scratch_shapes=scratch)
        else:
            spec = pltpu.PrefetchScalarGridSpec(
                num_scalar_prefetch=prefetch,
                grid=grid,
                in_specs=in_specs,
                out_specs=out_specs,
                scratch_shapes=scratch,
            )
            how = dict(grid_spec=spec)
        results = pl.pallas_call(
            ordered,
            out_shape=outs,
            compiler_params=pltpu.CompilerParams(vmem_limit_bytes=63 * 2**20),
            cost_estimate=pl.CostEstimate(flops=1000 + int(cost * 1.15e9), bytes_accessed=1000, transcendentals=0),
            input_output_aliases={source + extra: target for source, target in (aliases or {}).items()},
            **how,
        )(*operands[:prefetch], *tokens, *operands[prefetch:])
        if not aliases or aliases.get(0) != 0:
            self.tokens = [results[0]]
        return results


DMA = pltpu.SemaphoreType.DMA
JOIN_COST = 3


def embed(line, core, codes, pos, valid, pair, at):
    return line.call(
        partial(embed_kernel, at),
        (core, codes, pos, valid, *pair),
        [SMEM, VMEM, VMEM, VMEM, ANY, ANY],
        (shape_of(TOKENS, 1, kind=jnp.int32), shape_of(TOKENS, D)),
        (VMEM, VMEM),
        [pltpu.VMEM((16, 48, VPAD), low), DMA((6,))],
        cost=6,
    )


def attention(line, core, stream, vector, pairs, ats):
    return line.call(
        partial(attention_kernel, ats),
        (core, stream, vector, *pairs[0], *pairs[1]),
        [SMEM, VMEM, VMEM] + [ANY] * 4,
        (
            shape_of(3, TOKENS, D, kind=low),
            shape_of(TOKENS, 128),
            shape_of(TOKENS, D, kind=low),
            shape_of(TOKENS, D),
        ),
        (VMEM,) * 4,
        [pltpu.VMEM((16, 48, 3 * D), low), pltpu.VMEM((16, 48, D), low), DMA((8,))],
        cost=15,
    )


def feed_forward(line, core, middle, vector, pairs, ats):
    return line.call(
        partial(forward_kernel, ats),
        (core, middle, vector, *pairs[0], *pairs[1], *pairs[2]),
        [SMEM, VMEM, VMEM] + [ANY] * 6,
        (shape_of(4, TOKENS, D), shape_of(TOKENS, D)),
        (ANY, VMEM),
        [
            pltpu.VMEM((16, 48, FF), low),
            pltpu.VMEM((16, 192, D), low),
            pltpu.VMEM((TOKENS, D), low),
            pltpu.VMEM((2, TOKENS, D), full),
            DMA((16,)),
            DMA((2,)),
        ],
        cost=12,
    )


def head(line, core, stream, final, codes, pos_column, pos_row, scale, valid, bias, pair, at):
    return line.call(
        partial(head_kernel, at),
        (core, stream, final, codes, pos_column, pos_row, scale, valid, bias, *pair),
        [SMEM] + [VMEM] * 8 + [ANY, ANY],
        (
            shape_of(TOKENS, D),
            shape_of(SLOTS, D, kind=low),
            shape_of(SLOTS, VPAD, kind=low),
            shape_of(1, VPAD),
            shape_of(2, D),
            shape_of(1, 128),
        ),
        (VMEM,) * 6,
        [pltpu.VMEM((16, 48, VPAD), low), pltpu.VMEM((SLOTS, VPAD), full), DMA((6,))],
        cost=10,
    )


class Grads:
    def __init__(self):
        self.places, self.arrays = placed(SCATTER), {}

    def results(self, pieces, before, first):
        names = sorted({self.places[piece][0] for piece in pieces})
        operands, shapes, aliases = [], [], {}
        for name in names:
            if name in self.arrays:
                aliases[before + len(operands)] = first + len(shapes)
                operands.append(self.arrays[name])
            shapes.append(shape_of(16, 2, height(SCATTER[name]), UNIT, kind=low))
        spots = tuple((names.index(self.places[piece][0]), self.places[piece][1]) for piece in pieces)
        return names, operands, shapes, aliases, spots


def feed_forward_back(line, grads, layer, core, upstream, middle, vector, hidden, pairs, ats):
    names, more, shapes, aliases, spots = grads.results((f"D{layer}", f"E{layer}", f"F{layer}"), 11, 2)
    results = line.call(
        partial(forward_back_kernel, ats, spots, len(more)),
        (core, upstream, middle, vector, hidden, *pairs[0], *pairs[1], *pairs[2], *more),
        [SMEM, VMEM, VMEM, VMEM] + [ANY] * (7 + len(more)),
        (shape_of(TOKENS, D), shape_of(12, D), *shapes),
        (VMEM, VMEM) + (ANY,) * len(shapes),
        [
            pltpu.VMEM((16, 48, FF), low),
            pltpu.VMEM((16, 192, D), low),
            pltpu.VMEM((D, TOKENS), low),
            pltpu.VMEM((TOKENS, D), low),
            pltpu.VMEM((2, TOKENS, D), full),
            pltpu.VMEM((2, 2, 4, 192, UNIT), low),
            pltpu.VMEM((2, 2, 16, 48, UNIT), low),
            pltpu.VMEM((TOKENS, D), full),
            DMA((16,)),
            DMA((2,)),
            DMA((2, 4)),
        ],
        aliases=aliases,
        cost=1,
    )
    grads.arrays.update(zip(names, results[2:]))
    return results[:2]


def attention_back(line, grads, layer, core, grad_middle, stream, vector, triple, lse, mixed, pairs, ats):
    names, more, shapes, aliases, spots = grads.results((f"Q{layer}", f"O{layer}"), 11, 2)
    results = line.call(
        partial(attention_back_kernel, ats, spots, len(more)),
        (core, grad_middle, stream, vector, triple, lse, mixed, *pairs[0], *pairs[1], *more),
        [SMEM] + [VMEM] * 6 + [ANY] * (4 + len(more)),
        (shape_of(TOKENS, D), shape_of(12, D), *shapes),
        (VMEM, VMEM) + (ANY,) * len(shapes),
        [
            pltpu.VMEM((16, 48, 3 * D), low),
            pltpu.VMEM((16, 48, D), low),
            pltpu.VMEM((TOKENS, D), low),
            pltpu.VMEM((3, TOKENS, D), low),
            pltpu.VMEM((4, 2, 16, 48, UNIT), low),
            DMA((8,)),
            DMA((8,)),
        ],
        aliases=aliases,
        cost=1,
    )
    grads.arrays.update(zip(names, results[2:]))
    return results[:2]


def embed_back(line, grads, upstream, ids, chosen, grad_logits, small):
    names, more, shapes, aliases, spots = grads.results(("T",), 5, 0)
    results = line.call(
        partial(embed_back_kernel, spots[0][1], len(more)),
        (upstream, ids, chosen, grad_logits, small, *more),
        [VMEM] * 4 + [ANY] * (1 + len(more)),
        tuple(shapes),
        (ANY,) * len(shapes),
        [pltpu.VMEM((3, 2, 16, 48, UNIT), low), DMA((8,))],
        aliases=aliases,
        cost=1,
    )
    grads.arrays.update(zip(names, results))


def pass_on(line, array):
    def kernel(unused, out):
        pass

    shape = (shape_of(*array.shape, kind=array.dtype),)
    return line.call(kernel, (array,), [ANY], shape, (ANY,), [], aliases={0: 0})[0]


def join(line, bits, axis, own, other):
    dims = list(own.shape)
    dims[axis] = 2
    cut = next((i for i in range(4) if own.shape[i] == 2), None)
    steps = 1 if cut is None else 2

    def kernel(bits_ref, own_ref, other_ref, out, stage, in_sems, out_sems):
        loads, stores = [], []
        for step in range(steps):
            for which, source in enumerate((own_ref, other_ref)):
                slot = 2 * step + which
                part = [slice(None)] * 4
                if cut is not None:
                    part[cut] = pl.ds(step, 1)
                loads.append(pltpu.make_async_copy(source.at[tuple(part)], stage.at[slot], in_sems.at[slot]))
                place = bits_ref[axis] if which == 0 else 1 - bits_ref[axis]
                part[axis] = pl.ds(place, 1)
                stores.append(pltpu.make_async_copy(stage.at[slot], out.at[tuple(part)], out_sems.at[slot]))
        for copy in loads:
            copy.start()
        for load, store in zip(loads, stores):
            load.wait()
            store.start()
        for copy in stores:
            copy.wait()

    block = [1 if i == cut else size for i, size in enumerate(own.shape)]
    scratch = [pltpu.VMEM((2 * steps, *block), low), DMA((2 * steps,)), DMA((2 * steps,))]
    operands = (bits, own, other)
    return line.call(kernel, operands, [SMEM, ANY, ANY], (shape_of(*dims, kind=low),), (ANY,), scratch, cost=JOIN_COST)[0]


def merge(line, bits, parts, gone, axis, cost=2):
    rows = parts[-1].shape[-2]
    open_axes = [i for i in range(4) if i not in gone and i != axis]
    dims = [2 if i in open_axes else 1 for i in range(4)]
    kind = full if axis is None else low
    cut = open_axes[0] if open_axes else None
    block = [1 if i == cut else size for i, size in enumerate(dims)]

    def spec(shape):
        def index(step, bits_ref):
            place = []
            for i in range(4):
                if i == cut:
                    place.append(step)
                elif shape[i] == 1 or i in open_axes:
                    place.append(0)
                else:
                    place.append(1 - bits_ref[i] if i == axis else bits_ref[i])
            if len(shape) == 7:
                place.append(bits_ref[4])
            return (*place, 0, 0)

        return pl.BlockSpec((*block, *(None,) * (len(shape) - 6), rows, UNIT), index)

    def kernel(bits_ref, *refs):
        total = refs[0][...].astype(full)
        for ref in refs[1:-1]:
            total += ref[...].astype(full)
        refs[-1][...] = total.astype(kind)

    return line.call(
        kernel,
        (bits, *parts),
        [spec(part.shape) for part in parts],
        (shape_of(*dims, rows, UNIT, kind=kind),),
        (spec((*dims, rows, UNIT)),),
        [],
        grid=(1 if cut is None else 2,),
        prefetch=1,
        cost=cost,
    )[0]


def update(weight, moment, average, grad, factor):
    clipped = grad * factor
    moment_next = inertia * moment + clipped
    weight_next = weight - step_rate * (clipped + inertia * moment_next)
    return (weight_next, moment_next, average_decay * average + (1.0 - average_decay) * weight_next)


def pack_small(vecs, final_norm, counts):
    own = jnp.concatenate(
        [vecs[0], vecs[1], final_norm[0], final_norm[1], counts.astype(full)]
    ).astype(low)
    own = jnp.pad(own, (0, 2 * UNIT - own.shape[0])).reshape(2, UNIT)
    return jnp.pad(own, ((0, 14), (0, 0)))


def body(hops, *arguments):
    codes, mask_pos, mask_count, table, w_qkv, w_out, w_up, w_down = arguments[:8]
    layer_vecs, final_norm, head_bias = arguments[8:11]
    moments, averages = arguments[11:19], arguments[19:27]
    images, seq_len = codes.shape
    core = side("core") if hops else jnp.zeros((), jnp.int32)
    own = core.astype(jnp.int32).reshape(1)
    line = Line(own)
    places = placed(GATHER)
    table_t = jnp.pad(table.T, ((0, 0), (0, VPAD - V)))
    shards = {"T": table_t}
    for l in range(L):
        shards[f"Q{l}"], shards[f"O{l}"], shards[f"D{l}"] = w_qkv[l], w_out[l], w_down[l]
        shards[f"U{l}"] = w_up[l]

    def split_up(make):
        out = {}
        for name, shard in shards.items():
            if name[0] == "U":
                block = make(shard, 4, PIECES["E0"][1][0][1])
                half = block.shape[-2] // 2
                out["E" + name[1]], out["F" + name[1]] = block[..., :half, :], block[..., half:, :]
            else:
                out[name] = make(shard, *PIECES[name][1][0])
        return out

    if hops:
        bits = jnp.stack([side(hop) for hop in ("zhi", "zlo", "y", "x", "core")]).astype(jnp.int32)
        local = split_up(lambda shard, units, rows: column_units(shard).reshape(2, -1, UNIT).astype(low))
        pieces = [piece for name in GATHER for piece in GATHER[name]]
        halves = jnp.concatenate([local[piece] for piece in pieces], 1)
        mine_half = pick(halves, core, 0)[0]
        other_half = swap(pick(halves, 1 - core, 0)[0], "core")
        whole, start = {}, 0
        for piece in pieces:
            units, rows = PIECES[piece][1][0]
            mine = mine_half[start : start + units * rows].reshape(units, 1, rows, UNIT)
            yours = other_half[start : start + units * rows].reshape(units, 1, rows, UNIT)
            whole[piece] = in_order(core, mine, yours, 1).reshape(-1, UNIT)
            start += units * rows
        whole["T"] = jnp.concatenate([whole["T"], pack_small(layer_vecs, final_norm, mask_count)])
        flying, done, pairs = {}, {}, {}
        for name in GATHER:
            chunk = jnp.concatenate([whole[piece] for piece in GATHER[name]])
            if name not in GATHER_WAY:
                whole[name] = chunk
                continue
            chunk = chunk[None, None, None, None]
            flying[name], done[name] = (chunk, swap(chunk, GATHER_WAY[name][0])), 0

        def next_hop(name):
            way = GATHER_WAY[name]
            chunk = join(line, bits, HOPS[way[done[name]]][3], *flying[name])
            done[name] += 1
            if done[name] < len(way):
                flying[name] = chunk, swap(chunk, way[done[name]])
            else:
                pairs[name] = [part.reshape(16, -1, UNIT) for part in (chunk, swap(chunk, "core"))]
    else:

        def everywhere(shard):
            return lax.all_gather(shard.astype(low), BOTH, axis=0, tiled=True)

        blocks = split_up(lambda shard, units, rows: weight_blocks(everywhere(shard), units, 2 * rows))
        pairs = {}
        for name in GATHER:
            chunk = jnp.concatenate([blocks[piece] for piece in GATHER[name]], 2)
            pairs[name] = [chunk[0], chunk[1]]
        vectors = [everywhere(layer_vecs[l]).astype(full).reshape(12, D) for l in range(L)]
        final_float = everywhere(final_norm.T).T.astype(full)
        mask_total = lax.psum(jnp.sum(mask_count.astype(full)), BOTH)

    slots = jnp.arange(M, dtype=jnp.int32)
    valid = (slots[None, :] < mask_count[:, None]).astype(full)
    spots = mask_pos + seq_len * jnp.arange(images, dtype=jnp.int32)[:, None]
    codes_row, codes_column = codes.reshape(1, TOKENS), codes.reshape(TOKENS, 1)
    pos_row, pos_column = spots.reshape(1, SLOTS), spots.reshape(SLOTS, 1)
    valid_row, valid_column = valid.reshape(1, SLOTS), valid.reshape(SLOTS, 1)
    bias = jnp.pad(head_bias, (0, VPAD - V), constant_values=-1e30).reshape(1, VPAD)

    def sources(*names):
        return [pairs[places[name][0]] for name in names], tuple(places[name][1] for name in names)

    kept = [None] * L
    for step in FORWARD_ORDER:
        if step in GATHER:
            if hops and step in GATHER_WAY:
                next_hop(step)
            elif hops:
                chunk = lax.all_gather(pass_on(line, whole[step]), BOTH, axis=0)
                pairs[step] = [chunk.reshape(16, 2, *chunk.shape[1:])] * 2
        elif step == "embed":
            (pair,), (at,) = sources("T")
            ids, stream = embed(line, own, codes_column, pos_row, valid_row, pair, at)
            if hops:
                small = [part[:, at + 144 : at + 146].reshape(16, 1, 2 * UNIT) for part in pair]
                small = in_order(core, small[0], small[1], 1).reshape(32, 2 * UNIT).astype(full)
                vectors = [small[:, 288 * l : 288 * l + 288].reshape(12, D) for l in range(L)]
                final_float = small[:, 576:624].reshape(32, 2, 24).transpose(1, 0, 2).reshape(2, D)
                mask_total = jnp.sum(small[:, 624 : 624 + images])
        elif step == "head":
            scale = valid_column * (1.0 / mask_total)
            (pair,), (at,) = sources("T")
            upstream, chosen, grad_logits, bias_grad, final_grad, loss = head(
                line, own, stream, final_float, codes_row, pos_column, pos_row, scale, valid_column, bias, pair, at
            )
        elif step[:-1] == "attention":
            l = int(step[-1])
            two, ats = sources(f"Q{l}", f"O{l}")
            triple, lse, mixed, middle = attention(line, own, stream, vectors[l], two, ats)
            kept[l] = stream, triple, lse, mixed, middle
        else:
            l = int(step[-1])
            three, ats = sources(f"D{l}", f"E{l}", f"F{l}")
            hidden, stream = feed_forward(line, own, kept[l][4], vectors[l], three, ats)
            kept[l] = kept[l] + (hidden,)

    grads = Grads()
    vector_grads = [0.0] * L
    parts, gone, totals, settled = {}, {}, {}, None

    def small_blocks():
        small = [vector_grads[0].reshape(-1), vector_grads[1].reshape(-1), final_grad[0], final_grad[1]]
        if not hops:
            return small, jnp.zeros((16, 2, 16, UNIT), low)
        small.append(bias_grad[0, :2048])
        small = jnp.concatenate([grad.reshape(32, -1) for grad in small], 1)
        small = jnp.pad(small, ((0, 0), (0, 2 * UNIT - 688))).astype(low)
        small = small.reshape(16, 2, 2, UNIT)
        return small, jnp.pad(small, ((0, 0), (0, 0), (0, 14), (0, 0)))

    def ready(names):
        for name in names:
            grad = grads.arrays[name]
            if name in SCATTER_WAY:
                shape = (2, 2, 2, 2) + grad.shape[1:]
                arrived = swap(pick(grad, 1 - core, 1)[:, 0], "core")
                parts[name], gone[name] = [grad.reshape(shape), arrived.reshape(shape[:4] + shape[5:])], []
            else:
                grad = grad.reshape(32, -1, UNIT)
                total = lax.psum_scatter(grad, BOTH, scatter_dimension=0, tiled=False)
                parts[name], totals[name] = None, total.astype(full)
                return total

    complete = {name: [p for p in SCATTER[name]] for name in SCATTER}

    def finished(pieces):
        for piece in pieces:
            complete[grads.places[piece][0]].remove(piece)
        names = [name for name in SCATTER if name in grads.arrays and not complete[name] and name not in parts]
        return ready(names) if hops else None

    for at, step in enumerate(BACKWARD_ORDER):
        if step in SCATTER_WAY:
            if not hops:
                continue
            way = SCATTER_WAY[step]
            if len(gone[step]) == len(way):
                totals[step] = merge(line, bits, parts[step], gone[step], None)[0, 0, 0, 0]
                continue
            hop = way[len(gone[step])]
            axis = HOPS[hop][3]
            cost = LONG.get(at, 2)
            if at == SETTLED:
                line.wait(settled)
            parts[step].append(swap(merge(line, bits, parts[step], gone[step], axis, cost), hop))
            gone[step].append(axis)
        elif step == "embed":
            small_grads, block = small_blocks()
            embed_back(line, grads, upstream, ids, chosen, grad_logits, block)
            finished(("T",))
        elif step[:-1] == "attention":
            l = int(step[-1])
            stream, triple, lse, mixed = kept[l][:4]
            two, ats = sources(f"Q{l}", f"O{l}")
            upstream, early = attention_back(
                line, grads, l, own, grad_middle, stream, vectors[l], triple, lse, mixed, two, ats
            )
            vector_grads[l] += early
            finished((f"Q{l}", f"O{l}"))
        else:
            l = int(step[-1])
            three, ats = sources(f"D{l}", f"E{l}", f"F{l}")
            grad_middle, late = feed_forward_back(
                line, grads, l, own, upstream, kept[l][4], vectors[l], kept[l][5], three, ats
            )
            vector_grads[l] += late
            total = finished((f"D{l}", f"E{l}", f"F{l}"))
            settled = settled if total is None else total

    shares = {}
    if hops:
        for names in LAST:
            mine, leaving, where = [], [], []
            for name in names:
                start = 0
                for piece in SCATTER[name]:
                    units, rows = PIECES[piece][1][0]
                    block = totals[name][start : start + 2 * units * rows].reshape(units, 2, rows, UNIT)
                    mine.append(pick(block, core, 1).reshape(-1, UNIT))
                    leaving.append(pick(block, 1 - core, 1).reshape(-1, UNIT))
                    where.append((piece, units, rows))
                    start += PIECES[piece][0]
            mine, arrived = jnp.concatenate(mine), swap(jnp.concatenate(leaving), "core")
            both = in_order(core, mine[None], arrived[None], 0)
            start = 0
            for piece, units, rows in where:
                block = both[:, start : start + units * rows].reshape(2, units, rows, UNIT)
                shares[piece] = block
                start += units * rows
        for l in range(L):
            shares[f"U{l}"] = jnp.concatenate([shares[f"E{l}"], shares[f"F{l}"]], 1)
        for piece in list(shares):
            block = shares[piece]
            shares[piece] = block.transpose(2, 0, 1, 3).reshape(block.shape[2], -1)
        small_sum = totals[grads.places["T"][0]][144:146].reshape(-1)
    else:
        head_grad, loss_sum = lax.psum((bias_grad[0, :V], loss[0, 0]), BOTH)
        small_sum = [lax.psum_scatter(g, BOTH, scatter_dimension=0, tiled=True) for g in small_grads]
        small_sum = jnp.concatenate(small_sum)
        for piece, (name, start) in grads.places.items():
            size = 144 if piece == "T" else PIECES[piece][0]
            shares[piece] = grads.arrays[name][:, :, start : start + size].transpose(1, 0, 2, 3)
        for l in range(L):
            shares[f"U{l}"] = jnp.concatenate([shares[f"E{l}"], shares[f"F{l}"]], 2)
        for piece, block in shares.items():
            units, rows = (4, 24) if piece[0] == "U" else PIECES[piece][1][0]
            weight = natural_weight(block, units, 2 * rows).astype(full)
            shares[piece] = lax.psum_scatter(weight, BOTH, scatter_dimension=0, tiled=True)
    width, narrow = layer_vecs.shape[1], final_norm.shape[1]
    grads_own = [shares["T"][:, :V].T]
    grads_own += [jnp.stack([shares[f"{kind}{l}"] for l in range(L)]) for kind in "QOUD"]
    grads_own += [
        small_sum[: 2 * width].reshape(L, width),
        small_sum[2 * width : 2 * width + 2 * narrow].reshape(2, narrow),
    ]
    if hops:
        squares = reduce(jnp.add, [jnp.sum(totals[name] * totals[name]) for name in SCATTER])
        bias_share = small_sum[624:688]
        tail = jnp.concatenate([bias_share, squares[None], loss[0, :1], jnp.zeros(62)])
        tail = tail.reshape(1, 1, 1, 1, 1, 128)
        for group in (("core",), ("x", "y"), ("zhi", "zlo")):
            if len(group) == 1:
                tail = jnp.concatenate([tail, swap(tail, group[0])], 4)
                continue
            axis, flips = [HOPS[hop][3] for hop in group], [swap(tail, hop) for hop in group]
            across = swap_both(tail, group)
            tail = jnp.concatenate(
                [jnp.concatenate([tail, flips[1]], axis[1]), jnp.concatenate([flips[0], across], axis[1])], axis[0]
            )
        for hop, axis in (("core", 4), ("x", 3), ("y", 2), ("zlo", 1), ("zhi", 0)):
            tail = jnp.where(side(hop) == 0, tail, jnp.flip(tail, axis))
        tail = tail.reshape(32, 128)
        head_grad = tail[:, :64].reshape(-1)[:V]
        squares, loss_sum = jnp.sum(tail[:, 64]), jnp.sum(tail[:, 65])
    else:
        squares = reduce(jnp.add, [jnp.sum(share * share) for share in grads_own])
        squares = lax.psum(squares, BOTH) + jnp.sum(head_grad * head_grad)
    grad_norm = jnp.sqrt(squares)
    factor = jnp.minimum(1.0, clip_bound / (grad_norm + epsilon))
    results = [
        update(weight, moment, average, grad, factor)
        for weight, moment, average, grad in zip(arguments[3:11], moments, averages, grads_own + [head_grad])
    ]
    return (
        (loss_sum, mask_total, grad_norm)
        + tuple(result[0] for result in results)
        + tuple(result[1] for result in results)
        + tuple(result[2] for result in results)
    )


def solution(mesh):
    return jax.shard_map(
        partial(body, mesh.shape["dp"] == 8 and mesh.shape["fsdp"] == 4),
        mesh=mesh,
        in_specs=(
            P(("dp", "fsdp"), None),
            P(("dp", "fsdp"), None),
            P(("dp", "fsdp")),
            P(None, ("dp", "fsdp")),
            P(None, ("dp", "fsdp"), None),
            P(None, ("dp", "fsdp"), None),
            P(None, ("dp", "fsdp"), None),
            P(None, ("dp", "fsdp"), None),
            P(None, ("dp", "fsdp")),
            P(None, ("dp", "fsdp")),
            P(),
            P(None, ("dp", "fsdp")),
            P(None, ("dp", "fsdp"), None),
            P(None, ("dp", "fsdp"), None),
            P(None, ("dp", "fsdp"), None),
            P(None, ("dp", "fsdp"), None),
            P(None, ("dp", "fsdp")),
            P(None, ("dp", "fsdp")),
            P(),
            P(None, ("dp", "fsdp")),
            P(None, ("dp", "fsdp"), None),
            P(None, ("dp", "fsdp"), None),
            P(None, ("dp", "fsdp"), None),
            P(None, ("dp", "fsdp"), None),
            P(None, ("dp", "fsdp")),
            P(None, ("dp", "fsdp")),
            P(),
        ),
        out_specs=(
            P(),
            P(),
            P(),
            P(None, ("dp", "fsdp")),
            P(None, ("dp", "fsdp"), None),
            P(None, ("dp", "fsdp"), None),
            P(None, ("dp", "fsdp"), None),
            P(None, ("dp", "fsdp"), None),
            P(None, ("dp", "fsdp")),
            P(None, ("dp", "fsdp")),
            P(),
            P(None, ("dp", "fsdp")),
            P(None, ("dp", "fsdp"), None),
            P(None, ("dp", "fsdp"), None),
            P(None, ("dp", "fsdp"), None),
            P(None, ("dp", "fsdp"), None),
            P(None, ("dp", "fsdp")),
            P(None, ("dp", "fsdp")),
            P(),
            P(None, ("dp", "fsdp")),
            P(None, ("dp", "fsdp"), None),
            P(None, ("dp", "fsdp"), None),
            P(None, ("dp", "fsdp"), None),
            P(None, ("dp", "fsdp"), None),
            P(None, ("dp", "fsdp")),
            P(None, ("dp", "fsdp")),
            P(),
        ),
        check_vma=False,
    )
```

```python
from functools import partial, reduce

import jax
import jax.numpy as jnp
from jax import lax
from jax.experimental import pallas as pl
from jax.experimental.pallas import tpu as pltpu
from jax.sharding import PartitionSpec as P

D = 768
HEADS = 12
HEAD_DIM = 64
FF = 3072
V = 2026
M = 128
L = 2
UNIT = 384
VPAD = 2304
BOTH = ("dp", "fsdp")


epsilon = 1e-06
step_rate = 10000.0
inertia = 0.5
average_decay = 0.5
clip_bound = 0.01


HOPS = {
    "zhi": ("dp", 4, 8, 0),
    "zlo": ("dp", 2, 8, 1),
    "y": ("dp", 1, 8, 2),
    "x": ("fsdp", 2, 4, 3),
    "core": ("fsdp", 1, 4, None),
}

PIECES = {"T": (160, ((3, 24),))}
for layer in range(L):
    PIECES.update(
        {
            f"Q{layer}": (144, ((3, 24),)),
            f"O{layer}": (48, ((1, 24),)),
            f"D{layer}": (192, ((1, 96),)),
            f"E{layer}": (96, ((2, 24),)),
            f"F{layer}": (96, ((2, 24),)),
        }
    )

GATHER = {
    "t": ("T",),
    "a": ("Q0", "O0"),
    "d": ("D0",),
    "u": ("E0", "F0"),
    "l": ("Q1", "O1", "D1", "E1", "F1"),
}
GATHER_WAY = {
    "t": ("zlo", "zhi", "y", "x"),
    "a": ("zlo", "zhi", "x", "y"),
    "d": ("zlo", "zhi", "y", "x"),
    "u": ("zlo", "zhi", "x", "y"),
}
SCATTER = {
    "c": ("D1", "E1", "F1"),
    "b": ("Q1", "O1"),
    "d": ("D0",),
    "u": ("E0", "F0"),
    "a": ("Q0", "O0"),
    "t": ("T",),
}
SCATTER_WAY = {
    "b": ("x", "y", "zhi", "zlo"),
    "d": ("x", "y", "zhi", "zlo"),
    "u": ("y", "x", "zhi", "zlo"),
    "a": ("y", "x", "zhi", "zlo"),
    "t": ("x", "y", "zhi", "zlo"),
}
FORWARD_ORDER = (
    ("l", "t", "a", "d", "u", "t", "a", "t", "a", "d", "u", "t", "a", "embed", "d", "u", "attention0", "d", "u")
    + ("forward0", "attention1", "forward1", "head")
)
BACKWARD_ORDER = (
    ("forward1", "attention1", "forward0", "b", "attention0", "u", "d", "b", "a", "embed", "u", "d", "t")
    + ("b", "a", "t", "u", "d", "b", "u", "a", "t", "d", "b", "u", "t", "d", "a", "t", "a")
)
LONG = {7: 14, 10: 14, 11: 14}
SETTLED = 15
LAST = (("c", "b"), ("u", "d", "t", "a"))


def placed(layout):
    places = {}
    for name, pieces in layout.items():
        start = 0
        for piece in pieces:
            places[piece] = (name, start)
            start += PIECES[piece][0]
    return places


def height(pieces):
    return sum(PIECES[piece][0] for piece in pieces)


def swap(tensor, hop):
    axis, flip, size, unused = HOPS[hop]
    return lax.ppermute(tensor, axis, [(i, i ^ flip) for i in range(size)])


def swap_both(tensor, hops):
    flips = [HOPS[hop] for hop in hops]
    if flips[0][0] == flips[1][0]:
        axis, flip, size = flips[0][0], flips[0][1] ^ flips[1][1], flips[0][2]
        return lax.ppermute(tensor, axis, [(i, i ^ flip) for i in range(size)])
    return swap(swap(tensor, hops[0]), hops[1])


def side(hop):
    axis, flip, unused, unused = HOPS[hop]
    return (lax.axis_index(axis) // flip) % 2


def in_order(bit, own, other, axis):
    return jnp.where(
        bit == 0, jnp.concatenate([own, other], axis), jnp.concatenate([other, own], axis)
    )


def pick(tensor, index, axis):
    return lax.dynamic_slice_in_dim(tensor, index, 1, axis)


def column_units(shard):
    rows, width = shard.shape
    return shard.reshape(rows, 2, width // (2 * UNIT), UNIT).transpose(1, 2, 0, 3)


def natural_weight(halves, units, rows):
    chips = halves.shape[1]
    block = halves.reshape(2, chips, units, rows, UNIT)
    return block.transpose(1, 3, 0, 2, 4).reshape(chips * rows, 2 * units * UNIT)


def weight_blocks(grad, units, rows):
    chips = grad.shape[0] // rows
    block = grad.reshape(chips, rows, 2, units, UNIT).transpose(2, 0, 3, 1, 4)
    return block.reshape(2, chips, units * rows, UNIT)


TOKENS = 512
SLOTS = 256
ANY = pl.BlockSpec(memory_space=pl.ANY)
SMEM = pl.BlockSpec(memory_space=pltpu.SMEM)
VMEM = pl.BlockSpec(memory_space=pltpu.VMEM)
low = jnp.bfloat16
full = jnp.float32


def dot(left, right):
    return lax.dot_general(left, right, (((1,), (0,)), ((), ())), preferred_element_type=full)


def dot_right(left, right):
    return lax.dot_general(left, right, (((1,), (1,)), ((), ())), preferred_element_type=full)


def dot_left(left, right):
    return lax.dot_general(left, right, (((0,), (0,)), ((), ())), preferred_element_type=full)


def norm_parts(stream):
    centre = stream - jnp.mean(stream, -1, keepdims=True)
    spread = lax.rsqrt(jnp.mean(centre * centre, -1, keepdims=True) + epsilon)
    return centre * spread, spread


def norm_back(upstream, scaled, spread, gain):
    weighted = upstream * gain
    return spread * (
        weighted
        - jnp.mean(weighted, -1, keepdims=True)
        - scaled * jnp.mean(weighted * scaled, -1, keepdims=True)
    )


def rows_sum(tensor):
    return jnp.sum(tensor, 0, keepdims=True)


def columns(start, size):
    return pl.ds(pl.multiple_of(start, 128), size)


def unit_copies(core, halves, at, units, first, half_units, target, sems):
    copies = []
    for which, source in enumerate(halves):
        half = core if which == 0 else 1 - core
        if len(source.shape) == 4:
            source = source.at[:, half]
        for unit in range(units):
            copies.append(
                pltpu.make_async_copy(
                    source.at[:, pl.ds(at + 48 * unit, 48), :],
                    target.at[:, :, columns((half * half_units + first + unit) * UNIT, UNIT)],
                    sems.at[which * units + unit],
                )
            )
    return copies


def flat(block):
    return block.reshape(block.shape[0] * block.shape[1], block.shape[2])


def head_mask(shape, which):
    lane = lax.broadcasted_iota(jnp.int32, shape, 1)
    return lane < HEAD_DIM if which == 0 else lane >= HEAD_DIM


def embed_kernel(at, core, codes, pos, valid, mine, yours, ids, stream, weight, sems):
    copies = unit_copies(core[0], (mine, yours), at, 3, 0, 3, weight, sems)
    for copy in copies:
        copy.start()
    place = lax.broadcasted_iota(jnp.int32, (TOKENS, SLOTS), 0)
    masked = jnp.max(jnp.where(place == pos[...], valid[...], 0.0), -1, keepdims=True)
    tokens = jnp.where(masked > 0, V - 1, codes[...])
    ids[...] = tokens
    for copy in copies:
        copy.wait()
    acc = jnp.zeros((TOKENS, D), full)
    for tile in range(3):
        word = lax.broadcasted_iota(jnp.int32, (TOKENS, D), 1) + tile * D
        hot = jnp.where(word == tokens, 1.0, 0.0).astype(low)
        acc += dot_right(hot, flat(weight[:, :, tile * D : (tile + 1) * D]))
    stream[...] = acc


def attention_kernel(
    ats, core, stream, vector, *refs
):
    in_pair, out_pair = refs[0:2], refs[2:4]
    triple, lse, mixed, middle, w_in, w_out, sems = refs[4:]
    in_copies = unit_copies(core[0], in_pair, ats[0], 3, 0, 3, w_in, sems.at[pl.ds(0, 6)])
    out_copies = unit_copies(core[0], out_pair, ats[1], 1, 0, 1, w_out, sems.at[pl.ds(6, 2)])
    for copy in in_copies + out_copies:
        copy.start()
    scaled, unused = norm_parts(stream[...])
    normed = (scaled * vector[0:1] + vector[1:2]).astype(low)
    for copy in in_copies:
        copy.wait()
    for part in range(3):
        block = dot(normed, flat(w_in[:, :, part * D : (part + 1) * D]))
        if part == 0:
            block = block + vector[2:3]
        if part == 2:
            block = block + vector[3:4]
        triple[part] = block.astype(low)
    lse[...] = jnp.zeros_like(lse)
    shape = (256, 128)
    lane = lax.broadcasted_iota(jnp.int32, shape, 1)

    def pair(step, carry):
        here = columns(step * 128, 128)
        for image in range(2):
            rows = slice(256 * image, 256 * image + 256)
            queries, key_rows, values = triple[0, rows, here], triple[1, rows, here], triple[2, rows, here]
            results = []
            for which in range(2):
                query = jnp.where(head_mask(shape, which), queries, jnp.zeros_like(queries))
                scores = dot_right(query, key_rows) * HEAD_DIM ** (-0.5)
                peak = jnp.max(scores, -1, keepdims=True)
                raised = jnp.exp(scores - peak)
                total = jnp.sum(raised, -1, keepdims=True)
                probs = (raised * (1.0 / total)).astype(low)
                results.append(dot(probs, values))
                lse[rows] = jnp.where(lane == 2 * step + which, peak + jnp.log(total), lse[rows])
            mixed[rows, here] = jnp.where(head_mask(shape, 0), results[0], results[1]).astype(low)
        return carry

    lax.fori_loop(0, HEADS // 2, pair, 0)
    for copy in out_copies:
        copy.wait()
    middle[...] = stream[...] + dot(mixed[...], flat(w_out[...])) + vector[4:5]


def forward_copies(core, ats, pairs, w_up, w_down, sems):
    first = unit_copies(core, pairs[1], ats[1], 2, 0, 4, w_up, sems.at[pl.ds(0, 4)])
    second = unit_copies(core, pairs[2], ats[2], 2, 2, 4, w_up, sems.at[pl.ds(4, 4)])
    up = first[:2] + second[:2] + first[2:] + second[2:]
    down = []
    for tile in range(4):
        chips = pl.ds(4 * lax.rem(2 * core + tile, 4), 4)
        for which, source in enumerate(pairs[0]):
            half = core if which == 0 else 1 - core
            if len(source.shape) == 4:
                source = source.at[:, half]
            down.append(
                pltpu.make_async_copy(
                    source.at[chips, pl.ds(ats[0], 192), :],
                    w_down.at[chips, :, columns(half * UNIT, UNIT)],
                    sems.at[8 + 2 * tile + which],
                )
            )
    return [up[2 * tile : 2 * tile + 2] + down[2 * tile : 2 * tile + 2] for tile in range(4)]


CURVE = 0.7978845608028654


def forward_kernel(ats, core, middle, vector, *refs):
    pairs = [refs[0:2], refs[2:4], refs[4:6]]
    hidden, result, w_up, w_down, normed, stage, sems, out_sems = refs[6:]
    copies = forward_copies(core[0], ats, pairs, w_up, w_down, sems)
    for group in copies:
        for copy in group:
            copy.start()
    scaled, unused = norm_parts(middle[...])
    normed[...] = (scaled * vector[5:6] + vector[6:7]).astype(low)
    result[...] = middle[...] + vector[7:8]
    sent = []
    for step in range(4):
        tile = lax.rem(2 * core[0] + step, 4)
        for copy in copies[step]:
            copy.wait()
        block = dot(normed[...], flat(w_up[:, :, columns(tile * D, D)])) + vector[pl.ds(8 + tile, 1)]
        if step >= 2:
            sent[step - 2].wait()
        stage[step % 2] = block
        copy = pltpu.make_async_copy(stage.at[step % 2], hidden.at[tile], out_sems.at[step % 2])
        copy.start()
        sent.append(copy)
        bent = jnp.tanh(CURVE * (block + 0.044715 * (block * block * block)))
        active = (0.5 * block * (1.0 + bent)).astype(low)
        result[...] += dot(active, flat(w_down[pl.ds(4 * tile, 4)]))
    for copy in sent[2:]:
        copy.wait()


def head_kernel(
    at,
    core,
    stream,
    final,
    codes,
    pos_column,
    pos_row,
    scale,
    valid,
    bias,
    mine,
    yours,
    upstream,
    chosen_out,
    grad_logits_out,
    bias_grad,
    final_grad,
    loss,
    weight,
    logits,
    sems,
):
    copies = unit_copies(core[0], (mine, yours), at, 3, 0, 3, weight, sems)
    for copy in copies:
        copy.start()
    scaled, spread = norm_parts(stream[...])
    normed = (scaled * final[0:1] + final[1:2]).astype(low)
    picker = lax.broadcasted_iota(jnp.int32, (SLOTS, TOKENS), 1) == pos_column[...]
    target = jnp.sum(jnp.where(picker, codes[...], 0), -1, keepdims=True)
    chosen = dot(picker.astype(full).astype(low), normed).astype(low)
    chosen_out[...] = chosen
    for copy in copies:
        copy.wait()
    peak = jnp.full((SLOTS, 1), -jnp.inf, full)
    picked = jnp.zeros((SLOTS, 1), full)
    for tile in range(3):
        here = slice(tile * D, tile * D + D)
        block = dot(chosen, flat(weight[:, :, here])) + bias[:, here]
        logits[:, here] = block
        peak = jnp.maximum(peak, jnp.max(block, -1, keepdims=True))
        word = lax.broadcasted_iota(jnp.int32, (SLOTS, D), 1) + tile * D
        picked += jnp.sum(jnp.where(word == target, block, 0.0), -1, keepdims=True)
    total = jnp.zeros((SLOTS, 1), full)
    for tile in range(3):
        total += jnp.sum(jnp.exp(logits[:, tile * D : tile * D + D] - peak), -1, keepdims=True)
    log_total = peak + jnp.log(total)
    loss[...] = jnp.broadcast_to(rows_sum(valid[...] * (log_total - picked)), (1, 128))
    grad_chosen = jnp.zeros((SLOTS, D), full)
    for tile in range(3):
        here = slice(tile * D, tile * D + D)
        word = lax.broadcasted_iota(jnp.int32, (SLOTS, D), 1) + tile * D
        chance = jnp.exp(logits[:, here] - log_total)
        block = ((chance - jnp.where(word == target, 1.0, 0.0)) * scale[...]).astype(low)
        grad_logits_out[:, here] = block
        bias_grad[:, here] = rows_sum(block.astype(full))
        grad_chosen += dot_right(block, flat(weight[:, :, here]))
    back = lax.broadcasted_iota(jnp.int32, (TOKENS, SLOTS), 0) == pos_row[...]
    back = back.astype(full).astype(low)
    grad_normed = jnp.zeros((TOKENS, D), full)
    for unused in range(3):
        piece = grad_chosen.astype(low)
        grad_normed += dot(back, piece)
        grad_chosen -= piece.astype(full)
    final_grad[0:1] = rows_sum(grad_normed * scaled)
    final_grad[1:2] = rows_sum(grad_normed)
    upstream[...] = norm_back(grad_normed, scaled, spread, final[0:1])


class Leaving:
    def __init__(self, own, half, source, target, chips, rows, sem, which=None):
        self.branch = None
        if len(target) == 1:
            self.copies = [pltpu.make_async_copy(source, target[0].at[chips, half, rows, :], sem)]
        elif which is not None:
            self.copies = [pltpu.make_async_copy(source, target[which].at[chips, rows, :], sem)]
        else:
            self.copies = [pltpu.make_async_copy(source, part.at[chips, rows, :], sem) for part in target]
            self.branch = own, half

    def start(self):
        if self.branch is None:
            self.copies[0].start()
            return
        own, half = self.branch
        pl.when(half == own)(self.copies[0].start)
        pl.when(half != own)(self.copies[1].start)

    def wait(self):
        self.copies[0].wait()


def split_targets(refs, sizes):
    targets, start = [], 0
    for size in sizes:
        targets.append(refs[start : start + size])
        start += size
    return targets


def forward_back_kernel(ats, outs, sizes, carried, core, upstream, middle, vector, hidden, *refs):
    pairs = [refs[0:2], refs[2:4], refs[4:6]]
    refs = refs[6 + carried :]
    grad_middle, vector_grad = refs[0:2]
    targets = split_targets(refs[2:-11], sizes)
    w_up, w_down, normed_t, branch, hidden_tile, down_stage, up_stage, acc = refs[-11:-3]
    sems, hidden_sems, out_sems = refs[-3:]
    own = core[0]
    tiles = [lax.rem(2 * own + step, 4) for step in range(4)]
    fetch = [
        pltpu.make_async_copy(hidden.at[tiles[step]], hidden_tile.at[step % 2], hidden_sems.at[step % 2])
        for step in range(4)
    ]
    fetch[0].start()
    copies = forward_copies(own, ats, pairs, w_up, w_down, sems)
    for group in copies:
        for copy in group:
            copy.start()
    scaled, spread = norm_parts(middle[...])
    normed_t[...] = (scaled * vector[5:6] + vector[6:7]).astype(low).T
    branch[...] = upstream[...].astype(low)
    vector_grad[...] = jnp.zeros_like(vector_grad)
    vector_grad[7:8] = rows_sum(branch[...].astype(full))
    acc[...] = jnp.zeros_like(acc)
    every = slice(None)
    flights = []

    def land(step):
        for copy in flights[step]:
            copy.wait()

    for step in range(4):
        tile, slot = tiles[step], step % 2
        if step < 3:
            fetch[step + 1].start()
        for copy in copies[step]:
            copy.wait()
        fetch[step].wait()
        block = hidden_tile[slot]
        square = block * block
        bent = jnp.tanh(CURVE * (block + 0.044715 * (square * block)))
        active = (0.5 * block * (1.0 + bent)).astype(low)
        slope = 0.5 * (1.0 + bent) + 0.5 * block * (1.0 - bent * bent) * (
            CURVE * (1.0 + (3.0 * 0.044715) * square)
        )
        back = dot_right(branch[...], flat(w_down[pl.ds(4 * tile, 4)]))
        grad_hidden = (slope * back).astype(low)
        vector_grad[pl.ds(8 + tile, 1)] = rows_sum(grad_hidden.astype(full))
        if step >= 2:
            land(step - 2)
        grad_down = dot(active.T, branch[...]).astype(low)
        for half in range(2):
            down_stage[slot, half] = grad_down[:, half * UNIT : half * UNIT + UNIT].reshape(4, 192, UNIT)
        flight = []
        for half in range(2):
            rows, target = pl.ds(outs[0][1], 192), targets[outs[0][0]]
            source, sem = down_stage.at[slot, half], out_sems.at[slot, half]
            flight.append(Leaving(own, half, source, target, pl.ds(4 * tile, 4), rows, sem))
        grad_up = dot(normed_t[...], grad_hidden).astype(low)
        for unit in range(2):
            up_stage[slot, unit] = grad_up[:, unit * UNIT : unit * UNIT + UNIT].reshape(16, 48, UNIT)
        half = own if step < 2 else 1 - own
        for unit in range(2):
            rows, target = pl.ds(outs[1 + slot][1] + 48 * unit, 48), targets[outs[1 + slot][0]]
            source, sem = up_stage.at[slot, unit], out_sems.at[slot, 2 + unit]
            flight.append(Leaving(own, half, source, target, every, rows, sem, step // 2))
        for copy in flight:
            copy.start()
        flights.append(flight)
        acc[...] += dot_right(grad_hidden, flat(w_up[:, :, columns(tile * D, D)]))
    grad_normed = acc[...]
    scaled, spread = norm_parts(middle[...])
    vector_grad[5:6] = rows_sum(grad_normed * scaled)
    vector_grad[6:7] = rows_sum(grad_normed)
    grad_middle[...] = upstream[...] + norm_back(grad_normed, scaled, spread, vector[5:6])
    land(2)
    land(3)


def attention_back_kernel(
    ats, outs, sizes, carried, core, grad_middle, stream, vector, triple, lse, mixed, *refs
):
    in_pair, out_pair = refs[0:2], refs[2:4]
    refs = refs[4 + carried :]
    upstream, vector_grad = refs[0:2]
    targets = split_targets(refs[2:-7], sizes)
    w_in, w_out, grad_mixed, grad_triple, stage, sems, out_sems = refs[-7:]
    target, at = targets[outs[0][0]], outs[0][1]
    out_target, out_at = targets[outs[1][0]], outs[1][1]
    leaving = []
    own = core[0]
    out_copies = unit_copies(own, out_pair, ats[1], 1, 0, 1, w_out, sems.at[pl.ds(6, 2)])
    in_copies = unit_copies(own, in_pair, ats[0], 3, 0, 3, w_in, sems.at[pl.ds(0, 6)])
    for copy in out_copies + in_copies:
        copy.start()
    every = slice(None)
    grad_out_low = grad_middle[...].astype(low)
    vector_grad[...] = jnp.zeros_like(vector_grad)
    vector_grad[4:5] = rows_sum(grad_out_low.astype(full))
    grad_out = dot(mixed[...].T, grad_out_low).astype(low)
    for half in range(2):
        stage[3, half] = grad_out[:, half * UNIT : half * UNIT + UNIT].reshape(16, 48, UNIT)
        source = stage.at[3, half]
        leaving.append(Leaving(own, half, source, out_target, every, pl.ds(out_at, 48), out_sems.at[6 + half]))
        leaving[-1].start()
    for copy in out_copies:
        copy.wait()
    grad_mixed[...] = dot_right(grad_out_low, flat(w_out[...])).astype(low)
    shape = (256, 128)
    lane = lax.broadcasted_iota(jnp.int32, shape, 1)

    def pair(step, carry):
        here = columns(step * 128, 128)
        for image in range(2):
            rows = slice(256 * image, 256 * image + 256)
            queries, key_rows, values = triple[0, rows, here], triple[1, rows, here], triple[2, rows, here]
            grads = grad_mixed[rows, here]
            outs = []
            for which in range(2):
                mask = head_mask(shape, which)
                none = jnp.zeros_like(queries)
                scores = dot_right(jnp.where(mask, queries, none), key_rows) * HEAD_DIM ** (-0.5)
                total = jnp.sum(jnp.where(lane == 2 * step + which, lse[rows], 0.0), -1, keepdims=True)
                probs = jnp.exp(scores - total)
                grad_values = dot_left(probs.astype(low), grads)
                grad_probs = dot_right(jnp.where(mask, grads, none), values)
                inner = jnp.sum(probs * grad_probs, -1, keepdims=True)
                grad_scores = (probs * (grad_probs - inner)).astype(low)
                grad_queries = dot(grad_scores, key_rows) * HEAD_DIM ** (-0.5)
                grad_keys = dot_left(grad_scores, queries) * HEAD_DIM ** (-0.5)
                outs.append((grad_queries, grad_keys, grad_values))
            first = head_mask(shape, 0)
            for part in range(3):
                grad_triple[part, rows, here] = jnp.where(first, outs[0][part], outs[1][part]).astype(low)
        return carry

    lax.fori_loop(0, HEADS // 2, pair, 0)
    scaled, spread = norm_parts(stream[...])
    normed_t = (scaled * vector[0:1] + vector[1:2]).astype(low).T
    for copy in in_copies:
        copy.wait()
    grad_normed = jnp.zeros((TOKENS, D), full)
    for part in range(3):
        block = grad_triple[part]
        if part == 0:
            vector_grad[2:3] = rows_sum(block.astype(full))
        if part == 2:
            vector_grad[3:4] = rows_sum(block.astype(full))
        grad_in = dot(normed_t, block).astype(low)
        for side_unit in range(2):
            unit = 2 * part + side_unit
            stage[part, side_unit] = grad_in[:, side_unit * UNIT : side_unit * UNIT + UNIT].reshape(16, 48, UNIT)
            source = stage.at[part, side_unit]
            rows = pl.ds(at + 48 * (unit % 3), 48)
            leaving.append(Leaving(own, unit // 3, source, target, every, rows, out_sems.at[unit]))
            leaving[-1].start()
        grad_normed += dot_right(block, flat(w_in[:, :, part * D : (part + 1) * D]))
    vector_grad[0:1] = rows_sum(grad_normed * scaled)
    vector_grad[1:2] = rows_sum(grad_normed)
    upstream[...] = grad_middle[...] + norm_back(grad_normed, scaled, spread, vector[0:1])
    for copy in leaving:
        copy.wait()


def embed_back_kernel(at, size, carried, core, upstream, ids, chosen, grad_logits, small, *refs):
    target = refs[carried:-2]
    stage, sems = refs[-2:]
    own, every = core[0], slice(None)
    leaving = []
    for which in range(2):
        half = own if which == 0 else 1 - own
        rows, sem = pl.ds(at + 144, 16), sems.at[6 + which]
        leaving.append(Leaving(own, half, small.at[:, half], target, every, rows, sem, which))
        leaving[-1].start()
    stream_t = upstream[...].astype(low).T
    chosen_t = chosen[...].T
    for tile in range(3):
        word = lax.broadcasted_iota(jnp.int32, (TOKENS, D), 1) + tile * D
        hot = jnp.where(word == ids[...], 1.0, 0.0).astype(low)
        block = dot(stream_t, hot) + dot(chosen_t, grad_logits[:, tile * D : tile * D + D])
        for side_unit in range(2):
            unit = 2 * tile + side_unit
            part = block[:, side_unit * UNIT : side_unit * UNIT + UNIT].astype(low)
            stage[tile, side_unit] = part.reshape(16, 48, UNIT)
            source = stage.at[tile, side_unit]
            rows = pl.ds(at + 48 * (unit % 3), 48)
            leaving.append(Leaving(own, unit // 3, source, target, every, rows, sems.at[unit]))
            leaving[-1].start()
    for copy in leaving:
        copy.wait()


def shape_of(*dims, kind=full):
    return jax.ShapeDtypeStruct(dims, kind)


class Line:
    def __init__(self, token):
        self.tokens = [token]

    def wait(self, array):
        self.tokens.append(array)

    def call(self, kernel, operands, in_specs, outs, out_specs, scratch, grid=None, prefetch=0, aliases=None, cost=0):
        tokens, extra = self.tokens, len(self.tokens)

        def ordered(*refs):
            return kernel(*refs[:prefetch], *refs[prefetch + extra :])

        in_specs = [ANY] * extra + in_specs
        if grid is None:
            how = dict(in_specs=in_specs, out_specs=out_specs, scratch_shapes=scratch)
        else:
            spec = pltpu.PrefetchScalarGridSpec(
                num_scalar_prefetch=prefetch,
                grid=grid,
                in_specs=in_specs,
                out_specs=out_specs,
                scratch_shapes=scratch,
            )
            how = dict(grid_spec=spec)
        results = pl.pallas_call(
            ordered,
            out_shape=outs,
            compiler_params=pltpu.CompilerParams(vmem_limit_bytes=63 * 2**20),
            cost_estimate=pl.CostEstimate(flops=1000 + int(cost * 1.15e9), bytes_accessed=1000, transcendentals=0),
            input_output_aliases={source + extra: target for source, target in (aliases or {}).items()},
            **how,
        )(*operands[:prefetch], *tokens, *operands[prefetch:])
        if not aliases or aliases.get(0) != 0:
            self.tokens = [results[0]]
        return results


DMA = pltpu.SemaphoreType.DMA
JOIN_COST = 3


def embed(line, core, codes, pos, valid, pair, at):
    return line.call(
        partial(embed_kernel, at),
        (core, codes, pos, valid, *pair),
        [SMEM, VMEM, VMEM, VMEM, ANY, ANY],
        (shape_of(TOKENS, 1, kind=jnp.int32), shape_of(TOKENS, D)),
        (VMEM, VMEM),
        [pltpu.VMEM((16, 48, VPAD), low), DMA((6,))],
        cost=6,
    )


def attention(line, core, stream, vector, pairs, ats):
    return line.call(
        partial(attention_kernel, ats),
        (core, stream, vector, *pairs[0], *pairs[1]),
        [SMEM, VMEM, VMEM] + [ANY] * 4,
        (
            shape_of(3, TOKENS, D, kind=low),
            shape_of(TOKENS, 128),
            shape_of(TOKENS, D, kind=low),
            shape_of(TOKENS, D),
        ),
        (VMEM,) * 4,
        [pltpu.VMEM((16, 48, 3 * D), low), pltpu.VMEM((16, 48, D), low), DMA((8,))],
        cost=15,
    )


def feed_forward(line, core, middle, vector, pairs, ats):
    return line.call(
        partial(forward_kernel, ats),
        (core, middle, vector, *pairs[0], *pairs[1], *pairs[2]),
        [SMEM, VMEM, VMEM] + [ANY] * 6,
        (shape_of(4, TOKENS, D), shape_of(TOKENS, D)),
        (ANY, VMEM),
        [
            pltpu.VMEM((16, 48, FF), low),
            pltpu.VMEM((16, 192, D), low),
            pltpu.VMEM((TOKENS, D), low),
            pltpu.VMEM((2, TOKENS, D), full),
            DMA((16,)),
            DMA((2,)),
        ],
        cost=12,
    )


def head(line, core, stream, final, codes, pos_column, pos_row, scale, valid, bias, pair, at):
    return line.call(
        partial(head_kernel, at),
        (core, stream, final, codes, pos_column, pos_row, scale, valid, bias, *pair),
        [SMEM] + [VMEM] * 8 + [ANY, ANY],
        (
            shape_of(TOKENS, D),
            shape_of(SLOTS, D, kind=low),
            shape_of(SLOTS, VPAD, kind=low),
            shape_of(1, VPAD),
            shape_of(2, D),
            shape_of(1, 128),
        ),
        (VMEM,) * 6,
        [pltpu.VMEM((16, 48, VPAD), low), pltpu.VMEM((SLOTS, VPAD), full), DMA((6,))],
        cost=10,
    )


class Grads:
    def __init__(self):
        self.places, self.arrays = placed(SCATTER), {}

    def results(self, pieces, before, first):
        names = sorted({self.places[piece][0] for piece in pieces})
        operands, shapes, aliases, sizes = [], [], {}, []
        for name in names:
            middle = [] if name in SCATTER_WAY else [2]
            sizes.append(2 if name in SCATTER_WAY else 1)
            for which in range(sizes[-1]):
                if name in self.arrays:
                    aliases[before + len(operands)] = first + len(shapes)
                    operands.append(self.arrays[name][which])
                shapes.append(shape_of(16, *middle, height(SCATTER[name]), UNIT, kind=low))
        spots = tuple((names.index(self.places[piece][0]), self.places[piece][1]) for piece in pieces)
        return names, operands, shapes, aliases, (spots, tuple(sizes))

    def take(self, names, sizes, results):
        self.arrays.update(zip(names, split_targets(results, sizes)))


def feed_forward_back(line, grads, layer, core, upstream, middle, vector, hidden, pairs, ats):
    names, more, shapes, aliases, spots = grads.results((f"D{layer}", f"E{layer}", f"F{layer}"), 11, 2)
    results = line.call(
        partial(forward_back_kernel, ats, *spots, len(more)),
        (core, upstream, middle, vector, hidden, *pairs[0], *pairs[1], *pairs[2], *more),
        [SMEM, VMEM, VMEM, VMEM] + [ANY] * (7 + len(more)),
        (shape_of(TOKENS, D), shape_of(12, D), *shapes),
        (VMEM, VMEM) + (ANY,) * len(shapes),
        [
            pltpu.VMEM((16, 48, FF), low),
            pltpu.VMEM((16, 192, D), low),
            pltpu.VMEM((D, TOKENS), low),
            pltpu.VMEM((TOKENS, D), low),
            pltpu.VMEM((2, TOKENS, D), full),
            pltpu.VMEM((2, 2, 4, 192, UNIT), low),
            pltpu.VMEM((2, 2, 16, 48, UNIT), low),
            pltpu.VMEM((TOKENS, D), full),
            DMA((16,)),
            DMA((2,)),
            DMA((2, 4)),
        ],
        aliases=aliases,
        cost=1,
    )
    grads.take(names, spots[1], results[2:])
    return results[:2]


def attention_back(line, grads, layer, core, grad_middle, stream, vector, triple, lse, mixed, pairs, ats):
    names, more, shapes, aliases, spots = grads.results((f"Q{layer}", f"O{layer}"), 11, 2)
    results = line.call(
        partial(attention_back_kernel, ats, *spots, len(more)),
        (core, grad_middle, stream, vector, triple, lse, mixed, *pairs[0], *pairs[1], *more),
        [SMEM] + [VMEM] * 6 + [ANY] * (4 + len(more)),
        (shape_of(TOKENS, D), shape_of(12, D), *shapes),
        (VMEM, VMEM) + (ANY,) * len(shapes),
        [
            pltpu.VMEM((16, 48, 3 * D), low),
            pltpu.VMEM((16, 48, D), low),
            pltpu.VMEM((TOKENS, D), low),
            pltpu.VMEM((3, TOKENS, D), low),
            pltpu.VMEM((4, 2, 16, 48, UNIT), low),
            DMA((8,)),
            DMA((8,)),
        ],
        aliases=aliases,
        cost=1,
    )
    grads.take(names, spots[1], results[2:])
    return results[:2]


def embed_back(line, grads, core, upstream, ids, chosen, grad_logits, small):
    names, more, shapes, aliases, spots = grads.results(("T",), 6, 0)
    results = line.call(
        partial(embed_back_kernel, spots[0][0][1], spots[1][0], len(more)),
        (core, upstream, ids, chosen, grad_logits, small, *more),
        [SMEM] + [VMEM] * 4 + [ANY] * (1 + len(more)),
        tuple(shapes),
        (ANY,) * len(shapes),
        [pltpu.VMEM((3, 2, 16, 48, UNIT), low), DMA((8,))],
        aliases=aliases,
        cost=1,
    )
    grads.take(names, spots[1], results)


def pass_on(line, array):
    def kernel(unused, out):
        pass

    shape = (shape_of(*array.shape, kind=array.dtype),)
    return line.call(kernel, (array,), [ANY], shape, (ANY,), [], aliases={0: 0})[0]


def join(line, bits, axis, own, other):
    dims = list(own.shape)
    dims[axis] = 2
    cut = next((i for i in range(4) if own.shape[i] == 2), None)
    steps = 1 if cut is None else 2

    def kernel(bits_ref, own_ref, other_ref, out, stage, in_sems, out_sems):
        loads, stores = [], []
        for step in range(steps):
            for which, source in enumerate((own_ref, other_ref)):
                slot = 2 * step + which
                part = [slice(None)] * 4
                if cut is not None:
                    part[cut] = pl.ds(step, 1)
                loads.append(pltpu.make_async_copy(source.at[tuple(part)], stage.at[slot], in_sems.at[slot]))
                place = bits_ref[axis] if which == 0 else 1 - bits_ref[axis]
                part[axis] = pl.ds(place, 1)
                stores.append(pltpu.make_async_copy(stage.at[slot], out.at[tuple(part)], out_sems.at[slot]))
        for copy in loads:
            copy.start()
        for load, store in zip(loads, stores):
            load.wait()
            store.start()
        for copy in stores:
            copy.wait()

    block = [1 if i == cut else size for i, size in enumerate(own.shape)]
    scratch = [pltpu.VMEM((2 * steps, *block), low), DMA((2 * steps,)), DMA((2 * steps,))]
    operands = (bits, own, other)
    return line.call(kernel, operands, [SMEM, ANY, ANY], (shape_of(*dims, kind=low),), (ANY,), scratch, cost=JOIN_COST)[0]


def merge(line, bits, parts, gone, axis, cost=2):
    rows = parts[-1].shape[-2]
    open_axes = [i for i in range(4) if i not in gone and i != axis]
    dims = [2 if i in open_axes else 1 for i in range(4)]
    kind = full if axis is None else low
    cut = open_axes[0] if open_axes else None
    block = [1 if i == cut else size for i, size in enumerate(dims)]

    def spec(shape):
        def index(step, bits_ref):
            place = []
            for i in range(4):
                if i == cut:
                    place.append(step)
                elif shape[i] == 1 or i in open_axes:
                    place.append(0)
                else:
                    place.append(1 - bits_ref[i] if i == axis else bits_ref[i])
            return (*place, 0, 0)

        return pl.BlockSpec((*block, rows, UNIT), index)

    def kernel(bits_ref, *refs):
        total = refs[0][...].astype(full)
        for ref in refs[1:-1]:
            total += ref[...].astype(full)
        refs[-1][...] = total.astype(kind)

    return line.call(
        kernel,
        (bits, *parts),
        [spec(part.shape) for part in parts],
        (shape_of(*dims, rows, UNIT, kind=kind),),
        (spec((*dims, rows, UNIT)),),
        [],
        grid=(1 if cut is None else 2,),
        prefetch=1,
        cost=cost,
    )[0]


def update(weight, moment, average, grad, factor):
    clipped = grad * factor
    moment_next = inertia * moment + clipped
    weight_next = weight - step_rate * (clipped + inertia * moment_next)
    return (weight_next, moment_next, average_decay * average + (1.0 - average_decay) * weight_next)


def pack_small(vecs, final_norm, counts):
    own = jnp.concatenate(
        [vecs[0], vecs[1], final_norm[0], final_norm[1], counts.astype(full)]
    ).astype(low)
    own = jnp.pad(own, (0, 2 * UNIT - own.shape[0])).reshape(2, UNIT)
    return jnp.pad(own, ((0, 14), (0, 0)))


def body(hops, *arguments):
    codes, mask_pos, mask_count, table, w_qkv, w_out, w_up, w_down = arguments[:8]
    layer_vecs, final_norm, head_bias = arguments[8:11]
    moments, averages = arguments[11:19], arguments[19:27]
    images, seq_len = codes.shape
    core = side("core") if hops else jnp.zeros((), jnp.int32)
    own = core.astype(jnp.int32).reshape(1)
    line = Line(own)
    places = placed(GATHER)
    table_t = jnp.pad(table.T, ((0, 0), (0, VPAD - V)))
    shards = {"T": table_t}
    for l in range(L):
        shards[f"Q{l}"], shards[f"O{l}"], shards[f"D{l}"] = w_qkv[l], w_out[l], w_down[l]
        shards[f"U{l}"] = w_up[l]

    def split_up(make):
        out = {}
        for name, shard in shards.items():
            if name[0] == "U":
                block = make(shard, 4, PIECES["E0"][1][0][1])
                half = block.shape[-2] // 2
                out["E" + name[1]], out["F" + name[1]] = block[..., :half, :], block[..., half:, :]
            else:
                out[name] = make(shard, *PIECES[name][1][0])
        return out

    if hops:
        bits = jnp.stack([side(hop) for hop in ("zhi", "zlo", "y", "x", "core")]).astype(jnp.int32)
        local = split_up(lambda shard, units, rows: column_units(shard).reshape(2, -1, UNIT).astype(low))
        pieces = [piece for name in GATHER for piece in GATHER[name]]
        halves = jnp.concatenate([local[piece] for piece in pieces], 1)
        mine_half = pick(halves, core, 0)[0]
        other_half = swap(pick(halves, 1 - core, 0)[0], "core")
        whole, start = {}, 0
        for piece in pieces:
            units, rows = PIECES[piece][1][0]
            mine = mine_half[start : start + units * rows].reshape(units, 1, rows, UNIT)
            yours = other_half[start : start + units * rows].reshape(units, 1, rows, UNIT)
            whole[piece] = in_order(core, mine, yours, 1).reshape(-1, UNIT)
            start += units * rows
        whole["T"] = jnp.concatenate([whole["T"], pack_small(layer_vecs, final_norm, mask_count)])
        flying, done, pairs = {}, {}, {}
        for name in GATHER:
            chunk = jnp.concatenate([whole[piece] for piece in GATHER[name]])
            if name not in GATHER_WAY:
                whole[name] = chunk
                continue
            chunk = chunk[None, None, None, None]
            flying[name], done[name] = (chunk, swap(chunk, GATHER_WAY[name][0])), 0

        def next_hop(name):
            way = GATHER_WAY[name]
            chunk = join(line, bits, HOPS[way[done[name]]][3], *flying[name])
            done[name] += 1
            if done[name] < len(way):
                flying[name] = chunk, swap(chunk, way[done[name]])
            else:
                pairs[name] = [part.reshape(16, -1, UNIT) for part in (chunk, swap(chunk, "core"))]
    else:

        def everywhere(shard):
            return lax.all_gather(shard.astype(low), BOTH, axis=0, tiled=True)

        blocks = split_up(lambda shard, units, rows: weight_blocks(everywhere(shard), units, 2 * rows))
        pairs = {}
        for name in GATHER:
            chunk = jnp.concatenate([blocks[piece] for piece in GATHER[name]], 2)
            pairs[name] = [chunk[0], chunk[1]]
        vectors = [everywhere(layer_vecs[l]).astype(full).reshape(12, D) for l in range(L)]
        final_float = everywhere(final_norm.T).T.astype(full)
        mask_total = lax.psum(jnp.sum(mask_count.astype(full)), BOTH)

    slots = jnp.arange(M, dtype=jnp.int32)
    valid = (slots[None, :] < mask_count[:, None]).astype(full)
    spots = mask_pos + seq_len * jnp.arange(images, dtype=jnp.int32)[:, None]
    codes_row, codes_column = codes.reshape(1, TOKENS), codes.reshape(TOKENS, 1)
    pos_row, pos_column = spots.reshape(1, SLOTS), spots.reshape(SLOTS, 1)
    valid_row, valid_column = valid.reshape(1, SLOTS), valid.reshape(SLOTS, 1)
    bias = jnp.pad(head_bias, (0, VPAD - V), constant_values=-1e30).reshape(1, VPAD)

    def sources(*names):
        return [pairs[places[name][0]] for name in names], tuple(places[name][1] for name in names)

    kept = [None] * L
    for step in FORWARD_ORDER:
        if step in GATHER:
            if hops and step in GATHER_WAY:
                next_hop(step)
            elif hops:
                chunk = lax.all_gather(pass_on(line, whole[step]), BOTH, axis=0)
                pairs[step] = [chunk.reshape(16, 2, *chunk.shape[1:])] * 2
        elif step == "embed":
            (pair,), (at,) = sources("T")
            ids, stream = embed(line, own, codes_column, pos_row, valid_row, pair, at)
            if hops:
                small = [part[:, at + 144 : at + 146].reshape(16, 1, 2 * UNIT) for part in pair]
                small = in_order(core, small[0], small[1], 1).reshape(32, 2 * UNIT).astype(full)
                vectors = [small[:, 288 * l : 288 * l + 288].reshape(12, D) for l in range(L)]
                final_float = small[:, 576:624].reshape(32, 2, 24).transpose(1, 0, 2).reshape(2, D)
                mask_total = jnp.sum(small[:, 624 : 624 + images])
        elif step == "head":
            scale = valid_column * (1.0 / mask_total)
            (pair,), (at,) = sources("T")
            upstream, chosen, grad_logits, bias_grad, final_grad, loss = head(
                line, own, stream, final_float, codes_row, pos_column, pos_row, scale, valid_column, bias, pair, at
            )
        elif step[:-1] == "attention":
            l = int(step[-1])
            two, ats = sources(f"Q{l}", f"O{l}")
            triple, lse, mixed, middle = attention(line, own, stream, vectors[l], two, ats)
            kept[l] = stream, triple, lse, mixed, middle
        else:
            l = int(step[-1])
            three, ats = sources(f"D{l}", f"E{l}", f"F{l}")
            hidden, stream = feed_forward(line, own, kept[l][4], vectors[l], three, ats)
            kept[l] = kept[l] + (hidden,)

    grads = Grads()
    vector_grads = [0.0] * L
    parts, gone, totals, settled = {}, {}, {}, None

    def small_blocks():
        small = [vector_grads[0].reshape(-1), vector_grads[1].reshape(-1), final_grad[0], final_grad[1]]
        if not hops:
            return small, jnp.zeros((16, 2, 16, UNIT), low)
        small.append(bias_grad[0, :2048])
        small = jnp.concatenate([grad.reshape(32, -1) for grad in small], 1)
        small = jnp.pad(small, ((0, 0), (0, 2 * UNIT - 688))).astype(low)
        small = small.reshape(16, 2, 2, UNIT)
        return small, jnp.pad(small, ((0, 0), (0, 0), (0, 14), (0, 0)))

    def ready(names):
        for name in names:
            grad = grads.arrays[name]
            if name in SCATTER_WAY:
                shape = (2, 2, 2, 2) + grad[0].shape[1:]
                parts[name], gone[name] = [grad[0].reshape(shape), swap(grad[1], "core").reshape(shape)], []
            else:
                grad = grad[0].reshape(32, -1, UNIT)
                total = lax.psum_scatter(grad, BOTH, scatter_dimension=0, tiled=False)
                parts[name], totals[name] = None, total.astype(full)
                return total

    complete = {name: [p for p in SCATTER[name]] for name in SCATTER}

    def finished(pieces):
        for piece in pieces:
            complete[grads.places[piece][0]].remove(piece)
        names = [name for name in SCATTER if name in grads.arrays and not complete[name] and name not in parts]
        return ready(names) if hops else None

    for at, step in enumerate(BACKWARD_ORDER):
        if step in SCATTER_WAY:
            if not hops:
                continue
            way = SCATTER_WAY[step]
            if len(gone[step]) == len(way):
                totals[step] = merge(line, bits, parts[step], gone[step], None)[0, 0, 0, 0]
                continue
            hop = way[len(gone[step])]
            axis = HOPS[hop][3]
            cost = LONG.get(at, 2)
            if at == SETTLED:
                line.wait(settled)
            parts[step].append(swap(merge(line, bits, parts[step], gone[step], axis, cost), hop))
            gone[step].append(axis)
        elif step == "embed":
            small_grads, block = small_blocks()
            embed_back(line, grads, own, upstream, ids, chosen, grad_logits, block)
            finished(("T",))
        elif step[:-1] == "attention":
            l = int(step[-1])
            stream, triple, lse, mixed = kept[l][:4]
            two, ats = sources(f"Q{l}", f"O{l}")
            upstream, early = attention_back(
                line, grads, l, own, grad_middle, stream, vectors[l], triple, lse, mixed, two, ats
            )
            vector_grads[l] += early
            finished((f"Q{l}", f"O{l}"))
        else:
            l = int(step[-1])
            three, ats = sources(f"D{l}", f"E{l}", f"F{l}")
            grad_middle, late = feed_forward_back(
                line, grads, l, own, upstream, kept[l][4], vectors[l], kept[l][5], three, ats
            )
            vector_grads[l] += late
            total = finished((f"D{l}", f"E{l}", f"F{l}"))
            settled = settled if total is None else total

    shares = {}
    if hops:
        for names in LAST:
            mine, leaving, where = [], [], []
            for name in names:
                start = 0
                for piece in SCATTER[name]:
                    units, rows = PIECES[piece][1][0]
                    block = totals[name][start : start + 2 * units * rows].reshape(units, 2, rows, UNIT)
                    mine.append(pick(block, core, 1).reshape(-1, UNIT))
                    leaving.append(pick(block, 1 - core, 1).reshape(-1, UNIT))
                    where.append((piece, units, rows))
                    start += PIECES[piece][0]
            mine, arrived = jnp.concatenate(mine), swap(jnp.concatenate(leaving), "core")
            both = in_order(core, mine[None], arrived[None], 0)
            start = 0
            for piece, units, rows in where:
                block = both[:, start : start + units * rows].reshape(2, units, rows, UNIT)
                shares[piece] = block
                start += units * rows
        for l in range(L):
            shares[f"U{l}"] = jnp.concatenate([shares[f"E{l}"], shares[f"F{l}"]], 1)
        for piece in list(shares):
            block = shares[piece]
            shares[piece] = block.transpose(2, 0, 1, 3).reshape(block.shape[2], -1)
        small_sum = totals[grads.places["T"][0]][144:146].reshape(-1)
    else:
        head_grad, loss_sum = lax.psum((bias_grad[0, :V], loss[0, 0]), BOTH)
        small_sum = [lax.psum_scatter(g, BOTH, scatter_dimension=0, tiled=True) for g in small_grads]
        small_sum = jnp.concatenate(small_sum)
        for piece, (name, start) in grads.places.items():
            size = 144 if piece == "T" else PIECES[piece][0]
            grad = grads.arrays[name]
            grad = jnp.stack(grad) if name in SCATTER_WAY else grad[0].transpose(1, 0, 2, 3)
            shares[piece] = grad[:, :, start : start + size]
        for l in range(L):
            shares[f"U{l}"] = jnp.concatenate([shares[f"E{l}"], shares[f"F{l}"]], 2)
        for piece, block in shares.items():
            units, rows = (4, 24) if piece[0] == "U" else PIECES[piece][1][0]
            weight = natural_weight(block, units, 2 * rows).astype(full)
            shares[piece] = lax.psum_scatter(weight, BOTH, scatter_dimension=0, tiled=True)
    width, narrow = layer_vecs.shape[1], final_norm.shape[1]
    grads_own = [shares["T"][:, :V].T]
    grads_own += [jnp.stack([shares[f"{kind}{l}"] for l in range(L)]) for kind in "QOUD"]
    grads_own += [
        small_sum[: 2 * width].reshape(L, width),
        small_sum[2 * width : 2 * width + 2 * narrow].reshape(2, narrow),
    ]
    if hops:
        squares = reduce(jnp.add, [jnp.sum(totals[name] * totals[name]) for name in SCATTER])
        bias_share = small_sum[624:688]
        tail = jnp.concatenate([bias_share, squares[None], loss[0, :1], jnp.zeros(62)])
        tail = tail.reshape(1, 1, 1, 1, 1, 128)
        for group in (("core",), ("x", "y"), ("zhi", "zlo")):
            if len(group) == 1:
                tail = jnp.concatenate([tail, swap(tail, group[0])], 4)
                continue
            axis, flips = [HOPS[hop][3] for hop in group], [swap(tail, hop) for hop in group]
            across = swap_both(tail, group)
            tail = jnp.concatenate(
                [jnp.concatenate([tail, flips[1]], axis[1]), jnp.concatenate([flips[0], across], axis[1])], axis[0]
            )
        for hop, axis in (("core", 4), ("x", 3), ("y", 2), ("zlo", 1), ("zhi", 0)):
            tail = jnp.where(side(hop) == 0, tail, jnp.flip(tail, axis))
        tail = tail.reshape(32, 128)
        head_grad = tail[:, :64].reshape(-1)[:V]
        squares, loss_sum = jnp.sum(tail[:, 64]), jnp.sum(tail[:, 65])
    else:
        squares = reduce(jnp.add, [jnp.sum(share * share) for share in grads_own])
        squares = lax.psum(squares, BOTH) + jnp.sum(head_grad * head_grad)
    grad_norm = jnp.sqrt(squares)
    factor = jnp.minimum(1.0, clip_bound / (grad_norm + epsilon))
    results = [
        update(weight, moment, average, grad, factor)
        for weight, moment, average, grad in zip(arguments[3:11], moments, averages, grads_own + [head_grad])
    ]
    return (
        (loss_sum, mask_total, grad_norm)
        + tuple(result[0] for result in results)
        + tuple(result[1] for result in results)
        + tuple(result[2] for result in results)
    )


def solution(mesh):
    return jax.shard_map(
        partial(body, mesh.shape["dp"] == 8 and mesh.shape["fsdp"] == 4),
        mesh=mesh,
        in_specs=(
            P(("dp", "fsdp"), None),
            P(("dp", "fsdp"), None),
            P(("dp", "fsdp")),
            P(None, ("dp", "fsdp")),
            P(None, ("dp", "fsdp"), None),
            P(None, ("dp", "fsdp"), None),
            P(None, ("dp", "fsdp"), None),
            P(None, ("dp", "fsdp"), None),
            P(None, ("dp", "fsdp")),
            P(None, ("dp", "fsdp")),
            P(),
            P(None, ("dp", "fsdp")),
            P(None, ("dp", "fsdp"), None),
            P(None, ("dp", "fsdp"), None),
            P(None, ("dp", "fsdp"), None),
            P(None, ("dp", "fsdp"), None),
            P(None, ("dp", "fsdp")),
            P(None, ("dp", "fsdp")),
            P(),
            P(None, ("dp", "fsdp")),
            P(None, ("dp", "fsdp"), None),
            P(None, ("dp", "fsdp"), None),
            P(None, ("dp", "fsdp"), None),
            P(None, ("dp", "fsdp"), None),
            P(None, ("dp", "fsdp")),
            P(None, ("dp", "fsdp")),
            P(),
        ),
        out_specs=(
            P(),
            P(),
            P(),
            P(None, ("dp", "fsdp")),
            P(None, ("dp", "fsdp"), None),
            P(None, ("dp", "fsdp"), None),
            P(None, ("dp", "fsdp"), None),
            P(None, ("dp", "fsdp"), None),
            P(None, ("dp", "fsdp")),
            P(None, ("dp", "fsdp")),
            P(),
            P(None, ("dp", "fsdp")),
            P(None, ("dp", "fsdp"), None),
            P(None, ("dp", "fsdp"), None),
            P(None, ("dp", "fsdp"), None),
            P(None, ("dp", "fsdp"), None),
            P(None, ("dp", "fsdp")),
            P(None, ("dp", "fsdp")),
            P(),
            P(None, ("dp", "fsdp")),
            P(None, ("dp", "fsdp"), None),
            P(None, ("dp", "fsdp"), None),
            P(None, ("dp", "fsdp"), None),
            P(None, ("dp", "fsdp"), None),
            P(None, ("dp", "fsdp")),
            P(None, ("dp", "fsdp")),
            P(),
        ),
        check_vma=False,
    )
```
